32 devices in a mesh: dp: 16 (over z, y, x), mp: 2 (over core).
Axes of the slice: x: 2, y: 2, z: 4, core: 2. Of those that a mesh axis runs over, the one named last changes fastest.
Arguments:
- normed_in: bfloat16 [65536, 512], P(('dp', 'mp')), may hold values from -6 to 6
- dual_in: bfloat16 [65536, 512], P(('dp', 'mp')), may hold values from -6 to 6
- query_weight: bfloat16 [512, 512], P(None, 'mp'), may hold values from -0.25 to 0.25
- key_weight: bfloat16 [512, 512], P(None, 'mp'), may hold values from -0.25 to 0.25
- value_weight: bfloat16 [512, 512], P(None, 'mp'), may hold values from -0.25 to 0.25
- output_weight: bfloat16 [512, 512], P('mp'), may hold values from -3 to 3
- first_gain: float32 [512], replicated, may hold values from 0.25 to 1.75
- first_bias: float32 [512], replicated, may hold values from -3 to 3
- up_weight: bfloat16 [512, 2048], P(None, 'mp'), may hold values from -0.25 to 0.25
- down_weight: bfloat16 [2048, 512], P('mp'), may hold values from -0.125 to 0.125
- second_gain: float32 [512], replicated, may hold values from 0.25 to 1.75
- second_bias: float32 [512], replicated, may hold values from -3 to 3
- segments: int32 [65536], P('dp'), may hold values from 0 to 4, as said below
- grad_normed_out: bfloat16 [65536, 512], P(('dp', 'mp')), may hold values from -12 to 12
- grad_dual_out: bfloat16 [65536, 512], P(('dp', 'mp')), may hold values from -12 to 12
Outputs:
- normed_out: bfloat16 [65536, 512], P(('dp', 'mp'))
- dual_out: bfloat16 [65536, 512], P(('dp', 'mp'))
- grad_normed_in: float32 [65536, 512], P(('dp', 'mp'))
- grad_query: float32 [512, 512], P(None, 'mp')
- grad_key: float32 [512, 512], P(None, 'mp')
- grad_value: float32 [512, 512], P(None, 'mp')
- grad_output: float32 [512, 512], P('mp')
- grad_first_gain: float32 [512], replicated
- grad_first_bias: float32 [512], replicated
- grad_up: float32 [512, 2048], P(None, 'mp')
- grad_down: float32 [2048, 512], P('mp')
- grad_second_gain: float32 [512], replicated
- grad_second_bias: float32 [512], replicated
The draws below stay inside these ranges and needn't reach their ends.
Inputs may be any that keep to these rules, and one draw needn't show every extreme that they name: `segments`: within each sequence of 1024 tokens the numbers never fall until the padding, which fills the last 1 to 128 positions of every sequence; documents are numbered from 1.
All inputs are finite; a program needn't handle non-finite values.
Results may differ from the reference program's by a relative error of at most 0.013.
The reference program's roundings to bfloat16 on the way count: a program that leaves them out, or rounds other values in their place, can miss the bound.
Values may be sent and summed in bfloat16 or wider, within the bound.
No kernel may reach another device: no remote copies, remote signals or barrier semaphores. Data moves between devices by JAX's collectives and lax.ppermute only.
A program may use at most 192 MiB of HBM per device.

```python
import jax
import jax.numpy as jnp
from jax import lax

D = 512
HEADS = 8
HD = 64
FF = 2048
LEN = 1024
TOKENS = 65536


def rising_scale(top):
    where = jnp.arange(TOKENS, dtype=jnp.float32) / TOKENS
    return 1.0 + (top - 1.0) * where


def draw_segments(key, part):
    key = jax.random.fold_in(key, 11)
    count = TOKENS // LEN
    cut_key, pad_key = jax.random.split(key)
    cuts = jax.random.randint(cut_key, (count, 3), 1, 3 * LEN // 4)
    pads = jax.random.randint(pad_key, (count, 1), 1, LEN // 8 + 1)
    where = jnp.arange(LEN, dtype=jnp.int32)
    labels = 1 + jnp.sum((cuts[:, None, :] <= where[None, :, None]).astype(jnp.int32), axis=-1)
    labels = jnp.where(where[None, :] >= LEN - pads, 0, labels)
    return labels.reshape(TOKENS).astype(jnp.int32)


def draw_grad_normed_out(key, part):
    key = jax.random.fold_in(key, 21)
    noise = jnp.clip(jax.random.normal(key, (TOKENS, D), jnp.float32), -4.0, 4.0)
    top = 3.0
    return (noise * rising_scale(top)[:, None]).astype(jnp.bfloat16)


def draw_grad_dual_out(key, part):
    key = jax.random.fold_in(key, 37)
    noise = jnp.clip(jax.random.normal(key, (TOKENS, D), jnp.float32), -4.0, 4.0)
    top = 3.0
    return (noise * rising_scale(top)[:, None]).astype(jnp.bfloat16)


def block_scale(own_key, dims, pieces, low, largest):
    def one(position, shards_of):
        draws = jax.random.uniform(jax.random.fold_in(jax.random.fold_in(own_key, 6), position), (shards_of,), jnp.float32, low / len(pieces), largest / len(pieces))
        return jnp.repeat(jnp.exp(draws), dims[position] // shards_of).reshape((-1,) + (1,) * (len(dims) - position - 1))

    loudness = one(*pieces[0])
    for cut in pieces[1:]:
        loudness = loudness * one(*cut)
    return loudness


def normal_values(own_key, shape, deviation, bound, cuts=(), kind=jnp.bfloat16):
    entries = deviation * jax.random.normal(own_key, shape, jnp.float32)
    if cuts:
        entries = entries * block_scale(own_key, shape, cuts, -0.22, 0.18)
    return jnp.clip(entries, -bound, bound).astype(kind)


def setup_inputs(seed: int = 0) -> dict:
    splits = jax.random.split(jax.random.key(seed), 16)
    return {
        "normed_in": normal_values(splits[0], (TOKENS, D), 1.0, 6.0, ((0, 32),)),
        "dual_in": normal_values(splits[1], (TOKENS, D), 1.0, 6.0, ((0, 32),)),
        "query_weight": normal_values(splits[2], (D, D), D ** -0.5, 0.25, ((1, 2),)),
        "key_weight": normal_values(splits[3], (D, D), D ** -0.5, 0.25, ((1, 2),)),
        "value_weight": normal_values(splits[4], (D, D), D ** -0.5, 0.25, ((1, 2),)),
        "output_weight": normal_values(splits[5], (D, D), (max(D // 128, 1)) ** -0.5, 3.0, ((0, 2),)),
        "first_gain": jnp.clip(1.0 + 0.15 * jax.random.normal(splits[6], (D,), jnp.float32), 0.25, 1.75),
        "first_bias": normal_values(splits[7], (D,), 0.5, 3.0, (), jnp.float32),
        "up_weight": normal_values(splits[8], (D, FF), D ** -0.5, 0.25, ((1, 2),)),
        "down_weight": normal_values(splits[9], (FF, D), FF ** -0.5, 0.125, ((0, 2),)),
        "second_gain": jnp.clip(1.0 + 0.15 * jax.random.normal(splits[10], (D,), jnp.float32), 0.25, 1.75),
        "second_bias": normal_values(splits[11], (D,), 0.5, 3.0, (), jnp.float32),
        "segments": draw_segments(jax.random.fold_in(splits[15], 71), 0),
        "grad_normed_out": draw_grad_normed_out(jax.random.fold_in(splits[15], 71), 0),
        "grad_dual_out": draw_grad_dual_out(jax.random.fold_in(splits[15], 71), 0),
    }


norm_eps = 1e-05
masked_score = -1e+30

@jax.custom_vjp
def low(v):
    return lax.optimization_barrier(v.astype(jnp.bfloat16)).astype(jnp.float32)

@jax.custom_vjp
def low_back(v):
    return v

def low_keep(v):
    return (low(v), None)

def low_pass(kept, grad):
    return (grad,)

def back_keep(v):
    return (v, None)

def back_low(kept, grad):
    return (low(grad),)
low.defvjp(low_keep, low_pass)
low_back.defvjp(back_keep, back_low)

def matmul_exact(left, right):
    return jnp.dot(left, right, precision=lax.Precision.HIGHEST)

def layer_norm(z, gain, bias):
    mean = lax.optimization_barrier(jnp.mean(z, axis=-1, keepdims=True))
    centred = z - mean
    spread = lax.optimization_barrier(jnp.mean(centred * centred, axis=-1, keepdims=True))
    return centred * lax.rsqrt(spread + norm_eps) * gain + bias

def split_heads(block):
    return block.reshape(LEN, HEADS, HD).transpose(1, 0, 2)

def attend(inputs):
    query, keys, values, labels = inputs
    raw = jnp.einsum('hqd,hkd->hqk', split_heads(query), split_heads(keys), precision=lax.Precision.HIGHEST) * HD ** (-0.5)
    scores = low_back(raw)
    same = labels[:, None] == labels[None, :]
    scores = jnp.where(same[None], scores, masked_score)
    probs = low(jax.nn.softmax(scores, axis=-1))
    mixed = jnp.einsum('hqk,hkd->hqd', probs, split_heads(values), precision=lax.Precision.HIGHEST)
    live = (labels != 0).astype(jnp.float32)
    return mixed.transpose(1, 0, 2).reshape(LEN, D) * live[:, None]

def layer(stream, dual, params, labels):
    query_weight, key_weight, value_weight, output_weight, first_gain, first_bias, up_weight, down_weight, second_gain, second_bias = params
    count = stream.shape[0] // LEN
    query = low(low_back(matmul_exact(stream, query_weight)))
    keys = low(low_back(matmul_exact(stream, key_weight)))
    values = low(low_back(matmul_exact(stream, value_weight)))
    heads_out = lax.map(jax.checkpoint(attend), (query.reshape(count, LEN, D), keys.reshape(count, LEN, D), values.reshape(count, LEN, D), labels.reshape(count, LEN)))
    heads_out = low(low_back(heads_out.reshape(count * LEN, D)))
    attn = low_back(matmul_exact(heads_out, output_weight))
    normed = layer_norm(stream + attn, first_gain, first_bias)
    dual_mid = dual + attn
    pre = low_back(matmul_exact(low(normed), up_weight))
    hidden = low(jax.nn.gelu(pre, approximate=True))
    ffn_out = low_back(matmul_exact(hidden, down_weight))
    return (layer_norm(normed + ffn_out, second_gain, second_bias), dual_mid + ffn_out)

def add_pair(left, right):
    return left + right

def reference(normed_in, dual_in, query_weight, key_weight, value_weight, output_weight, first_gain, first_bias, up_weight, down_weight, second_gain, second_bias, segments, grad_normed_out, grad_dual_out):
    params = tuple((weight.astype(jnp.float32) for weight in (query_weight, key_weight, value_weight, output_weight, first_gain, first_bias, up_weight, down_weight, second_gain, second_bias)))
    count_all = TOKENS // LEN
    per_step = 4 if count_all % 4 == 0 else 1
    steps_all = count_all // per_step
    span = per_step * LEN

    def one_step(carry, inputs):
        stream, dual, labels, upstream_x, upstream_y = inputs

        def run(stream_value, dual_value, param_value):
            return layer(stream_value, dual_value, param_value, labels)
        pair, pull = jax.vjp(run, stream.astype(jnp.float32), dual.astype(jnp.float32), params)
        grad_stream, grad_dual, grad_params = pull((upstream_x.astype(jnp.float32), upstream_y.astype(jnp.float32)))
        carry = jax.tree.map(add_pair, carry, grad_params)
        return (carry, (pair[0].astype(jnp.bfloat16), pair[1].astype(jnp.bfloat16), grad_stream))
    zeros = jax.tree.map(jnp.zeros_like, params)
    inputs = (normed_in.reshape(steps_all, span, D), dual_in.reshape(steps_all, span, D), segments.reshape(steps_all, span), grad_normed_out.reshape(steps_all, span, D), grad_dual_out.reshape(steps_all, span, D))
    totals, outputs = lax.scan(one_step, zeros, inputs)
    normed_out = outputs[0].reshape(TOKENS, D)
    dual_out = outputs[1].reshape(TOKENS, D)
    grad_normed_in = outputs[2].reshape(TOKENS, D)
    return (normed_out, dual_out, grad_normed_in, totals[0], totals[1], totals[2], totals[3], totals[4], totals[5], totals[6], totals[7], totals[8], totals[9])
```

```python
from functools import partial

import jax
import jax.numpy as jnp
from jax import lax
from jax.sharding import PartitionSpec as P

HD = 64
LEN = 1024


norm_eps = 1e-05
masked_score = -1e30


def layer_norm(z, gain, bias):
    mean = jnp.mean(z, axis=-1, keepdims=True)
    centred = z - mean
    spread = jnp.mean(centred * centred, axis=-1, keepdims=True)
    return centred * lax.rsqrt(spread + norm_eps) * gain + bias


def smooth_gate(value):
    return jax.nn.gelu(value, approximate=True)


def split_heads(block, head_size):
    return block.reshape(block.shape[0], block.shape[1] // head_size, head_size).transpose(1, 0, 2)


def join_heads(block):
    return block.transpose(1, 0, 2).reshape(block.shape[1], block.shape[0] * block.shape[2])


def masked_scores(query, keys, labels, head_size):
    raw = jnp.einsum(
        "hqd,hkd->hqk",
        split_heads(query, head_size),
        split_heads(keys, head_size),
        preferred_element_type=jnp.float32,
    ) * head_size ** (-0.5)
    same = labels[:, None] == labels[None, :]
    return jnp.where(same[None], raw, masked_score)


def attend_forward(inputs, head_size):
    query, keys, values, labels = inputs
    scores = masked_scores(query, keys, labels, head_size)
    top = jnp.max(scores, axis=-1, keepdims=True)
    shifted = jnp.exp(scores - top)
    total = jnp.sum(shifted, axis=-1, keepdims=True)
    probs = (shifted / total).astype(jnp.bfloat16)
    mixed = jnp.einsum(
        "hqk,hkd->hqd", probs, split_heads(values, head_size), preferred_element_type=jnp.float32
    )
    live = (labels != 0).astype(jnp.float32)
    return (
        (join_heads(mixed) * live[:, None]).astype(jnp.bfloat16),
        (top + jnp.log(total))[..., 0],
    )


def attend_backward(inputs, head_size):
    query, keys, values, labels, upstream, log_totals = inputs
    scale = head_size ** (-0.5)
    scores = masked_scores(query, keys, labels, head_size)
    probs = jnp.exp(scores - log_totals[..., None])
    live = (labels != 0).astype(jnp.bfloat16)
    grad_mixed = split_heads(upstream * live[:, None], head_size)
    grad_values = jnp.einsum(
        "hqk,hqd->hkd", probs.astype(jnp.bfloat16), grad_mixed, preferred_element_type=jnp.float32
    )
    grad_probs = jnp.einsum(
        "hqd,hkd->hqk",
        grad_mixed,
        split_heads(values, head_size),
        preferred_element_type=jnp.float32,
    )
    grad_scores = (
        probs * (grad_probs - jnp.sum(probs * grad_probs, axis=-1, keepdims=True))
    ).astype(jnp.bfloat16)
    grad_query = (
        jnp.einsum(
            "hqk,hkd->hqd",
            grad_scores,
            split_heads(keys, head_size),
            preferred_element_type=jnp.float32,
        )
        * scale
    )
    grad_keys = (
        jnp.einsum(
            "hqk,hqd->hkd",
            grad_scores,
            split_heads(query, head_size),
            preferred_element_type=jnp.float32,
        )
        * scale
    )
    joined = jnp.concatenate(
        [join_heads(grad_query), join_heads(grad_keys), join_heads(grad_values)], axis=1
    )
    return joined.astype(jnp.bfloat16)


def swap_cores(block):
    return lax.ppermute(block, "mp", [(0, 1), (1, 0)])


def partner(block, mask, count):
    return lax.ppermute(block, "dp", [(i, i ^ mask) for i in range(count)])


def add_rounded(left, right):
    return (left.astype(jnp.float32) + right.astype(jnp.float32)).astype(jnp.bfloat16)


def sum_over_chips(blocks, orders, count):
    me = lax.axis_index("dp")
    order_of = jnp.arange(count) ^ me
    pieces = [
        block.reshape(count, block.shape[0] // count, block.shape[1])[order_of] for block in blocks
    ]
    positions = [list(range(count)) for _ in blocks]
    for step in range(len(orders[0])):
        for which, order in enumerate(orders):
            mask = order[step]
            stay = [i for i, p in enumerate(positions[which]) if not p & mask]
            by_position = {p: i for i, p in enumerate(positions[which])}
            move = [by_position[positions[which][i] ^ mask] for i in stay]
            block = pieces[which]
            sent = jnp.concatenate([block[i : i + 1] for i in move])
            kept = jnp.concatenate([block[i : i + 1] for i in stay])
            pieces[which] = add_rounded(kept, partner(sent, mask, count))
            positions[which] = [positions[which][i] for i in stay]
    for step in reversed(range(len(orders[0]))):
        for which, order in enumerate(orders):
            mask = order[step]
            got = partner(pieces[which], mask, count)
            pieces[which] = jnp.concatenate([pieces[which], got])
            positions[which] = positions[which] + [p ^ mask for p in positions[which]]
    out = []
    for which, block in enumerate(blocks):
        back = jnp.asarray([positions[which].index(p) for p in range(count)])
        out.append(pieces[which][back[order_of]].reshape(block.shape))
    return out


def on_device(
    normed_in,
    dual_in,
    query_weight,
    key_weight,
    value_weight,
    output_weight,
    first_gain,
    first_bias,
    up_weight,
    down_weight,
    second_gain,
    second_bias,
    segments,
    grad_normed_out,
    grad_dual_out,
    chips,
):
    rows = normed_in.shape[0]
    count = rows // LEN
    core = lax.axis_index("mp")
    half = query_weight.shape[1]
    own_joint = jnp.concatenate([query_weight, key_weight, value_weight], axis=1)
    other_joint = swap_cores(own_joint)
    joint_weight = jnp.concatenate(
        [
            part[:, i * half : (i + 1) * half]
            for i in range(3)
            for part in (own_joint, other_joint)
        ],
        axis=1,
    )
    full_output = jnp.concatenate([output_weight, swap_cores(output_weight)], axis=0)
    full_up = jnp.concatenate([up_weight, swap_cores(up_weight)], axis=1)
    full_down = jnp.concatenate([down_weight, swap_cores(down_weight)], axis=0)
    width = 2 * half
    qkv = jnp.dot(normed_in, joint_weight, preferred_element_type=jnp.float32).astype(jnp.bfloat16)
    blocks = qkv.reshape(count, LEN, 3 * width)
    query = blocks[:, :, :width]
    keys = blocks[:, :, width : 2 * width]
    values = blocks[:, :, 2 * width :]
    labels = lax.dynamic_slice(segments, (core * rows,), (rows,)).reshape(count, LEN)
    heads_out, log_totals = lax.map(
        partial(attend_forward, head_size=HD), (query, keys, values, labels)
    )
    heads_out = heads_out.reshape(rows, width)
    attn = jnp.dot(heads_out, full_output, preferred_element_type=jnp.float32)
    normed, first_pull = jax.vjp(
        layer_norm, normed_in.astype(jnp.float32) + attn, first_gain, first_bias
    )
    dual_mid = dual_in.astype(jnp.float32) + attn
    normed_low = normed.astype(jnp.bfloat16)
    pre = jnp.dot(normed_low, full_up, preferred_element_type=jnp.float32)
    hidden_full, gate_pull = jax.vjp(smooth_gate, pre)
    hidden = hidden_full.astype(jnp.bfloat16)
    ffn_out = jnp.dot(hidden, full_down, preferred_element_type=jnp.float32)
    normed_final, second_pull = jax.vjp(layer_norm, normed + ffn_out, second_gain, second_bias)
    dual_final = dual_mid + ffn_out
    upstream_dual = grad_dual_out.astype(jnp.float32)
    grad_mid, second_gain_part, second_bias_part = second_pull(grad_normed_out.astype(jnp.float32))
    grad_ffn = (grad_mid + upstream_dual).astype(jnp.bfloat16)
    grad_hidden = jnp.einsum("td,fd->tf", grad_ffn, full_down, preferred_element_type=jnp.float32)
    grad_pre = gate_pull(grad_hidden)[0].astype(jnp.bfloat16)
    down_part = jnp.einsum("tf,td->fd", hidden, grad_ffn, preferred_element_type=jnp.float32)
    up_part = jnp.einsum("td,tf->df", normed_low, grad_pre, preferred_element_type=jnp.float32)
    down_part = down_part.astype(jnp.bfloat16)
    up_part = up_part.astype(jnp.bfloat16)
    mid = down_part.shape[0] // 2
    down_half = add_rounded(down_part[:mid], swap_cores(down_part[mid:]))
    up_half = add_rounded(up_part[:, :mid], swap_cores(up_part[:, mid:]))
    bits = [1 << i for i in range(chips.bit_length() - 1)]
    orders = (tuple(bits), tuple([bits[1], bits[0]] + bits[2:]))
    down_total, up_total = sum_over_chips((down_half, up_half), orders, chips)
    grad_normed = grad_mid + jnp.einsum(
        "tf,df->td", grad_pre, full_up, preferred_element_type=jnp.float32
    )
    grad_first, first_gain_part, first_bias_part = first_pull(grad_normed)
    grad_attn = (grad_first + upstream_dual).astype(jnp.bfloat16)
    output_part = jnp.einsum("th,td->hd", heads_out, grad_attn, preferred_element_type=jnp.float32)
    grad_heads = jnp.einsum(
        "td,hd->th", grad_attn, full_output, preferred_element_type=jnp.float32
    ).astype(jnp.bfloat16)
    grad_joint = lax.map(
        partial(attend_backward, head_size=HD),
        (query, keys, values, labels, grad_heads.reshape(count, LEN, width), log_totals),
    )
    grad_joint = grad_joint.reshape(rows, 3 * width)
    joint_part = jnp.einsum(
        "td,tc->dc", normed_in, grad_joint, preferred_element_type=jnp.float32
    ).astype(jnp.bfloat16)
    own = jnp.concatenate(
        [joint_part[:, 2 * i * half : (2 * i + 1) * half] for i in range(3)], axis=1
    )
    other = jnp.concatenate(
        [joint_part[:, (2 * i + 1) * half : (2 * i + 2) * half] for i in range(3)], axis=1
    )
    joint_half = add_rounded(own, swap_cores(other))
    output_part = output_part.astype(jnp.bfloat16)
    output_half = add_rounded(output_part[:half], swap_cores(output_part[half:]))
    small = jnp.stack([first_gain_part, first_bias_part, second_gain_part, second_bias_part])
    small = jnp.concatenate([small, jnp.zeros((12, small.shape[1]), jnp.float32)])
    small = small + swap_cores(small)
    for mask in bits:
        small = small + partner(small, mask, chips)
    joint_total, output_total = sum_over_chips((joint_half, output_half), orders, chips)
    grad_stream = grad_first + jnp.einsum(
        "tc,dc->td", grad_joint, joint_weight, preferred_element_type=jnp.float32
    )
    joint_total = joint_total.astype(jnp.float32)
    return (
        normed_final.astype(jnp.bfloat16),
        dual_final.astype(jnp.bfloat16),
        grad_stream,
        joint_total[:, :half],
        joint_total[:, half : 2 * half],
        joint_total[:, 2 * half :],
        output_total.astype(jnp.float32),
        small[0],
        small[1],
        up_total.astype(jnp.float32),
        down_total.astype(jnp.float32),
        small[2],
        small[3],
    )


def solution(mesh):
    rows = P(("dp", "mp"), None)
    columns = P(None, "mp")
    return jax.shard_map(
        partial(on_device, chips=mesh.shape["dp"]),
        mesh=mesh,
        in_specs=(
            rows, rows, columns, columns, columns, P("mp", None), P(), P(),
            columns, P("mp", None), P(), P(), P("dp"), rows, rows,
        ),
        out_specs=(
            rows, rows, rows, columns, columns, columns, P("mp", None), P(), P(),
            columns, P("mp", None), P(), P(),
        ),
        check_vma=False,
    )
```

```python
from functools import partial

import jax
import jax.numpy as jnp
from jax import lax
from jax.experimental import pallas as pl
from jax.experimental.pallas import tpu as pltpu
from jax.sharding import PartitionSpec as P

norm_eps = 1e-05
HD = 64
LEN = 1024
TILE = 128
TILES = LEN // TILE
PAIR = 2 * HD
FAR = -1e30
MARKS = 16
LSE_ROW = 8
MIB = 2**20


def dot(left, right):
    return jnp.dot(left, right, preferred_element_type=jnp.float32)


def three_parts(row):
    high = row.astype(jnp.bfloat16)
    rest = row - high.astype(jnp.float32)
    mid = rest.astype(jnp.bfloat16)
    low = (rest - mid.astype(jnp.float32)).astype(jnp.bfloat16)
    return high, mid, low


def label_marks(labels):
    lane = jnp.arange(TILE)
    key_marks = jnp.where(
        lane < LSE_ROW,
        jnp.where(labels[:, None] == lane, 0.0, FAR),
        jnp.where(lane < LSE_ROW + 3, 1.0, 0.0),
    ).astype(jnp.bfloat16)
    row = jnp.arange(MARKS)[:, None]
    query_marks = ((labels[None, :] == row) & (row < LSE_ROW)).astype(jnp.bfloat16)
    return key_marks, query_marks


def key_ranges(labels):
    seqs = labels.shape[0] // LEN
    table = labels.reshape(seqs, 1, LEN)
    ends = labels.reshape(seqs, TILES, TILE)
    where = jnp.arange(LEN, dtype=jnp.int32)
    first = jnp.min(jnp.where(table == ends[:, :, :1], where, LEN), axis=-1) // TILE
    last = jnp.max(jnp.where(table == ends[:, :, -1:], where, -1), axis=-1) // TILE
    return jnp.stack([first, last - first + 1], axis=-1).astype(jnp.int32).reshape(-1)


def halves_of(block):
    return jnp.concatenate([block[:HD, :TILE], block[HD:, TILE:]], axis=0)


def split_rows(tile_t):
    zero = jnp.zeros((HD, TILE), tile_t.dtype)
    return jnp.concatenate(
        [
            jnp.concatenate([tile_t[:HD], zero], axis=1),
            jnp.concatenate([zero, tile_t[HD:]], axis=1),
        ],
        axis=0,
    )


def split_lanes(tile):
    lane = lax.broadcasted_iota(jnp.int32, tile.shape, 1)
    zero = jnp.zeros_like(tile)
    return jnp.concatenate(
        [jnp.where(lane < HD, tile, zero), jnp.where(lane < HD, zero, tile)], axis=0
    )


def each_width(count, branch):
    for width in range(1, TILES + 1):
        pl.when(count == width)(partial(branch, width))


def attend_kernel(
    ranges, q_ref, k_ref, v_ref, key_marks, query_marks, out_ref, lse_ref, kcat, vt
):
    seq = pl.program_id(0)
    pairs = q_ref.shape[1] // PAIR
    for p in range(pairs):
        lanes = slice(p * PAIR, (p + 1) * PAIR)
        kcat[p, :, :PAIR] = k_ref[:, lanes]
        kcat[p, :, PAIR:] = key_marks[...]
        vt[lanes, :] = v_ref[:, lanes].T

    def step(i, carry):
        at = pl.multiple_of(i * TILE, TILE)
        first = ranges[(seq * TILES + i) * 2]
        count = ranges[(seq * TILES + i) * 2 + 1]
        start = pl.multiple_of(first * TILE, TILE)

        def branch(width):
            at_keys = pl.ds(start, width * TILE)
            marks = query_marks[:, pl.ds(at, TILE)]
            live = 1.0 - marks[:1].astype(jnp.float32)
            marks = jnp.concatenate([marks, marks], axis=1)
            rest = jnp.zeros((TILE - MARKS, 2 * TILE), jnp.bfloat16)

            def scores_of(p):
                query = q_ref[pl.ds(at, TILE), p * PAIR : (p + 1) * PAIR] * jnp.bfloat16(HD**-0.5)
                right = jnp.concatenate([split_rows(query.T), marks, rest], axis=0)
                return dot(kcat[p, at_keys, :], right)

            def finish(p, scores):
                top = jnp.max(scores, axis=0, keepdims=True)
                probs = jnp.exp(scores - top)
                total = jnp.sum(probs, axis=0, keepdims=True)
                mixed = dot(vt[p * PAIR : (p + 1) * PAIR, at_keys], probs.astype(jnp.bfloat16))
                mixed = halves_of(mixed / total) * live
                out_ref[pl.ds(at, TILE), p * PAIR : (p + 1) * PAIR] = mixed.T.astype(jnp.bfloat16)
                lse_ref[0, p, pl.ds(i, 1), :] = top + jnp.log(total)

            ahead = scores_of(0)
            for p in range(pairs):
                scores = ahead
                if p + 1 < pairs:
                    ahead = scores_of(p + 1)
                finish(p, scores)

        each_width(count, branch)
        return carry

    lax.fori_loop(0, TILES, step, 0)


def attend(ranges, qkv, key_marks, query_marks):
    rows, width = qkv.shape[0], qkv.shape[1] // 3
    seqs, pairs = rows // LEN, width // PAIR
    return pl.pallas_call(
        attend_kernel,
        grid_spec=pltpu.PrefetchScalarGridSpec(
            num_scalar_prefetch=1,
            grid=(seqs,),
            in_specs=[
                pl.BlockSpec((LEN, width), lambda s, _: (s, 0)),
                pl.BlockSpec((LEN, width), lambda s, _: (s, 1)),
                pl.BlockSpec((LEN, width), lambda s, _: (s, 2)),
                pl.BlockSpec((LEN, TILE), lambda s, _: (s, 0)),
                pl.BlockSpec((MARKS, LEN), lambda s, _: (0, s)),
            ],
            out_specs=[
                pl.BlockSpec((LEN, width), lambda s, _: (s, 0)),
                pl.BlockSpec((1, pairs, TILES, 2 * TILE), lambda s, _: (s, 0, 0, 0)),
            ],
            scratch_shapes=[
                pltpu.VMEM((pairs, LEN, PAIR + TILE), jnp.bfloat16),
                pltpu.VMEM((width, LEN), jnp.bfloat16),
            ],
        ),
        out_shape=[
            jax.ShapeDtypeStruct((rows, width), jnp.bfloat16),
            jax.ShapeDtypeStruct((seqs, pairs, TILES, 2 * TILE), jnp.float32),
        ],
        compiler_params=pltpu.CompilerParams(vmem_limit_bytes=48 * MIB),
        name="attend",
    )(ranges, qkv, qkv, qkv, key_marks, query_marks)


def attend_back_kernel(
    ranges, q_ref, k_ref, v_ref, g_ref, o_ref, key_marks, query_marks, lse_ref,
    dq_ref, dk_ref, dv_ref, kcat, vcat, kt, dk, dv,
):
    seq = pl.program_id(0)
    pairs = q_ref.shape[1] // PAIR
    for p in range(pairs):
        lanes = slice(p * PAIR, (p + 1) * PAIR)
        kcat[p, :, :PAIR] = k_ref[:, lanes]
        kcat[p, :, PAIR:] = key_marks[...]
        vcat[p, :, :PAIR] = v_ref[:, lanes]
        vcat[p, :, PAIR:] = key_marks[...]
        kt[lanes, :] = k_ref[:, lanes].T
    dk[...] = jnp.zeros_like(dk)
    dv[...] = jnp.zeros_like(dv)

    def negated(row):
        return [part.astype(jnp.float32) for part in three_parts(-row)]

    def step(i, carry):
        at = pl.multiple_of(i * TILE, TILE)
        first = ranges[(seq * TILES + i) * 2]
        count = ranges[(seq * TILES + i) * 2 + 1]
        start = pl.multiple_of(first * TILE, TILE)

        def branch(width):
            at_keys = pl.ds(start, width * TILE)
            marks = query_marks[:LSE_ROW, pl.ds(at, TILE)].astype(jnp.float32)
            marks = jnp.concatenate([marks, marks], axis=1)
            rest = jnp.zeros((TILE - MARKS, 2 * TILE), jnp.bfloat16)
            pad = jnp.zeros((MARKS - LSE_ROW - 3, 2 * TILE), jnp.float32)
            none = jnp.zeros((LSE_ROW, 2 * TILE), jnp.float32)

            def head(p):
                lanes = slice(p * PAIR, (p + 1) * PAIR)
                query = q_ref[pl.ds(at, TILE), lanes] * jnp.bfloat16(HD**-0.5)
                grad = g_ref[pl.ds(at, TILE), lanes]
                lse = lse_ref[0, p, pl.ds(i, 1), :]
                lse_rows = jnp.concatenate([marks, *negated(lse), pad], axis=0)
                agree = grad.astype(jnp.float32) * o_ref[pl.ds(at, TILE), lanes].astype(jnp.float32)
                agree = agree.T
                delta = jnp.concatenate(
                    [
                        jnp.sum(agree[:HD], axis=0, keepdims=True),
                        jnp.sum(agree[HD:], axis=0, keepdims=True),
                    ],
                    axis=1,
                )
                delta_rows = jnp.concatenate([none, *negated(delta), pad], axis=0)
                qt = jnp.concatenate(
                    [split_rows(query.T), lse_rows.astype(jnp.bfloat16), rest], axis=0
                )
                gt = jnp.concatenate(
                    [split_rows(grad.T), delta_rows.astype(jnp.bfloat16), rest], axis=0
                )
                scores = dot(kcat[p, at_keys, :], qt)
                grad_probs = dot(vcat[p, at_keys, :], gt)
                return query, grad, scores, grad_probs

            def finish(p, query, grad, scores, grad_probs):
                lanes = slice(p * PAIR, (p + 1) * PAIR)
                probs = jnp.exp(scores)
                grad_scores = (probs * grad_probs).astype(jnp.bfloat16)
                dv[p, at_keys, :] += dot(probs.astype(jnp.bfloat16), split_lanes(grad))
                dk[p, at_keys, :] += dot(grad_scores, split_lanes(query))
                dqt = halves_of(dot(kt[lanes, at_keys], grad_scores)) * HD**-0.5
                dq_ref[pl.ds(at, TILE), lanes] = dqt.T.astype(jnp.bfloat16)

            ahead = head(0)
            for p in range(pairs):
                now = ahead
                if p + 1 < pairs:
                    ahead = head(p + 1)
                finish(p, *now)

        each_width(count, branch)
        return carry

    lax.fori_loop(0, TILES, step, 0)
    for p in range(pairs):
        lanes = slice(p * PAIR, (p + 1) * PAIR)
        dk_ref[:, lanes] = dk[p].astype(jnp.bfloat16)
        dv_ref[:, lanes] = dv[p].astype(jnp.bfloat16)


def attend_back(ranges, qkv, grad_heads, heads_out, key_marks, query_marks, lse):
    rows, width = heads_out.shape
    seqs, pairs = rows // LEN, width // PAIR
    block = pl.BlockSpec((LEN, width), lambda s, _: (s, 0))
    grad = jax.ShapeDtypeStruct((rows, width), jnp.bfloat16)
    return pl.pallas_call(
        attend_back_kernel,
        grid_spec=pltpu.PrefetchScalarGridSpec(
            num_scalar_prefetch=1,
            grid=(seqs,),
            in_specs=[
                block,
                pl.BlockSpec((LEN, width), lambda s, _: (s, 1)),
                pl.BlockSpec((LEN, width), lambda s, _: (s, 2)),
                block,
                block,
                pl.BlockSpec((LEN, TILE), lambda s, _: (s, 0)),
                pl.BlockSpec((MARKS, LEN), lambda s, _: (0, s)),
                pl.BlockSpec((1, pairs, TILES, 2 * TILE), lambda s, _: (s, 0, 0, 0)),
            ],
            out_specs=[block, block, block],
            scratch_shapes=[
                pltpu.VMEM((pairs, LEN, PAIR + TILE), jnp.bfloat16),
                pltpu.VMEM((pairs, LEN, PAIR + TILE), jnp.bfloat16),
                pltpu.VMEM((width, LEN), jnp.bfloat16),
                pltpu.VMEM((pairs, LEN, PAIR), jnp.float32),
                pltpu.VMEM((pairs, LEN, PAIR), jnp.float32),
            ],
        ),
        out_shape=[grad, grad, grad],
        compiler_params=pltpu.CompilerParams(vmem_limit_bytes=48 * MIB),
        name="attend_back",
    )(ranges, qkv, qkv, qkv, grad_heads, heads_out, key_marks, query_marks, lse)


def layer_norm(z, gain, bias):
    mean = jnp.mean(z, axis=-1, keepdims=True)
    centred = z - mean
    spread = jnp.mean(centred * centred, axis=-1, keepdims=True)
    return centred * lax.rsqrt(spread + norm_eps) * gain + bias


def smooth_gate(value):
    return jax.nn.gelu(value, approximate=True)


def swap_cores(block):
    return lax.ppermute(block, "mp", [(0, 1), (1, 0)])


def partner(block, mask, count):
    return lax.ppermute(block, "dp", [(i, i ^ mask) for i in range(count)])


def add_rounded(left, right):
    return (left.astype(jnp.float32) + right.astype(jnp.float32)).astype(jnp.bfloat16)


def sum_over_chips(blocks, orders, count):
    me = lax.axis_index("dp")
    order_of = jnp.arange(count) ^ me
    pieces = [
        block.reshape(count, block.shape[0] // count, block.shape[1])[order_of] for block in blocks
    ]
    positions = [list(range(count)) for _ in blocks]
    for step in range(len(orders[0])):
        for which, order in enumerate(orders):
            mask = order[step]
            stay = [i for i, p in enumerate(positions[which]) if not p & mask]
            by_position = {p: i for i, p in enumerate(positions[which])}
            move = [by_position[positions[which][i] ^ mask] for i in stay]
            block = pieces[which]
            sent = jnp.concatenate([block[i : i + 1] for i in move])
            kept = jnp.concatenate([block[i : i + 1] for i in stay])
            pieces[which] = add_rounded(kept, partner(sent, mask, count))
            positions[which] = [positions[which][i] for i in stay]
    for step in reversed(range(len(orders[0]))):
        for which, order in enumerate(orders):
            mask = order[step]
            got = partner(pieces[which], mask, count)
            pieces[which] = jnp.concatenate([pieces[which], got])
            positions[which] = positions[which] + [p ^ mask for p in positions[which]]
    out = []
    for which, block in enumerate(blocks):
        back = jnp.asarray([positions[which].index(p) for p in range(count)])
        out.append(pieces[which][back[order_of]].reshape(block.shape))
    return out


def on_device(
    normed_in,
    dual_in,
    query_weight,
    key_weight,
    value_weight,
    output_weight,
    first_gain,
    first_bias,
    up_weight,
    down_weight,
    second_gain,
    second_bias,
    segments,
    grad_normed_out,
    grad_dual_out,
    chips,
):
    rows = normed_in.shape[0]
    core = lax.axis_index("mp")
    half = query_weight.shape[1]
    own_joint = jnp.concatenate([query_weight, key_weight, value_weight], axis=1)
    other_joint = swap_cores(own_joint)
    joint_weight = jnp.concatenate(
        [
            part[:, i * half : (i + 1) * half]
            for i in range(3)
            for part in (own_joint, other_joint)
        ],
        axis=1,
    )
    full_output = jnp.concatenate([output_weight, swap_cores(output_weight)], axis=0)
    full_up = jnp.concatenate([up_weight, swap_cores(up_weight)], axis=1)
    full_down = jnp.concatenate([down_weight, swap_cores(down_weight)], axis=0)
    width = 2 * half
    qkv = jnp.dot(normed_in, joint_weight, preferred_element_type=jnp.float32).astype(jnp.bfloat16)
    labels = lax.dynamic_slice(segments, (core * rows,), (rows,))
    key_marks, query_marks = label_marks(labels)
    ranges = key_ranges(labels)
    heads_out, log_totals = attend(ranges, qkv, key_marks, query_marks)
    attn = jnp.dot(heads_out, full_output, preferred_element_type=jnp.float32)
    normed, first_pull = jax.vjp(
        layer_norm, normed_in.astype(jnp.float32) + attn, first_gain, first_bias
    )
    dual_mid = dual_in.astype(jnp.float32) + attn
    normed_low = normed.astype(jnp.bfloat16)
    pre = jnp.dot(normed_low, full_up, preferred_element_type=jnp.float32)
    hidden_full, gate_pull = jax.vjp(smooth_gate, pre)
    hidden = hidden_full.astype(jnp.bfloat16)
    ffn_out = jnp.dot(hidden, full_down, preferred_element_type=jnp.float32)
    normed_final, second_pull = jax.vjp(layer_norm, normed + ffn_out, second_gain, second_bias)
    dual_final = dual_mid + ffn_out
    upstream_dual = grad_dual_out.astype(jnp.float32)
    grad_mid, second_gain_part, second_bias_part = second_pull(grad_normed_out.astype(jnp.float32))
    grad_ffn = (grad_mid + upstream_dual).astype(jnp.bfloat16)
    grad_hidden = jnp.einsum("td,fd->tf", grad_ffn, full_down, preferred_element_type=jnp.float32)
    grad_pre = gate_pull(grad_hidden)[0].astype(jnp.bfloat16)
    down_part = jnp.einsum("tf,td->fd", hidden, grad_ffn, preferred_element_type=jnp.float32)
    up_part = jnp.einsum("td,tf->df", normed_low, grad_pre, preferred_element_type=jnp.float32)
    down_part = down_part.astype(jnp.bfloat16)
    up_part = up_part.astype(jnp.bfloat16)
    mid = down_part.shape[0] // 2
    down_half = add_rounded(down_part[:mid], swap_cores(down_part[mid:]))
    up_half = add_rounded(up_part[:, :mid], swap_cores(up_part[:, mid:]))
    bits = [1 << i for i in range(chips.bit_length() - 1)]
    orders = (tuple(bits), tuple([bits[1], bits[0]] + bits[2:]))
    down_total, up_total = sum_over_chips((down_half, up_half), orders, chips)
    grad_normed = grad_mid + jnp.einsum(
        "tf,df->td", grad_pre, full_up, preferred_element_type=jnp.float32
    )
    grad_first, first_gain_part, first_bias_part = first_pull(grad_normed)
    grad_attn = (grad_first + upstream_dual).astype(jnp.bfloat16)
    output_part = jnp.einsum("th,td->hd", heads_out, grad_attn, preferred_element_type=jnp.float32)
    grad_heads = jnp.einsum(
        "td,hd->th", grad_attn, full_output, preferred_element_type=jnp.float32
    )
    grad_heads = (grad_heads * (labels != 0).astype(jnp.float32)[:, None]).astype(jnp.bfloat16)
    grad_joint = jnp.concatenate(
        attend_back(ranges, qkv, grad_heads, heads_out, key_marks, query_marks, log_totals), axis=1
    )
    joint_part = jnp.einsum(
        "td,tc->dc", normed_in, grad_joint, preferred_element_type=jnp.float32
    ).astype(jnp.bfloat16)
    own = jnp.concatenate(
        [joint_part[:, 2 * i * half : (2 * i + 1) * half] for i in range(3)], axis=1
    )
    other = jnp.concatenate(
        [joint_part[:, (2 * i + 1) * half : (2 * i + 2) * half] for i in range(3)], axis=1
    )
    joint_half = add_rounded(own, swap_cores(other))
    output_part = output_part.astype(jnp.bfloat16)
    output_half = add_rounded(output_part[:half], swap_cores(output_part[half:]))
    small = jnp.stack([first_gain_part, first_bias_part, second_gain_part, second_bias_part])
    small = jnp.concatenate([small, jnp.zeros((12, small.shape[1]), jnp.float32)])
    small = small + swap_cores(small)
    for mask in bits:
        small = small + partner(small, mask, chips)
    joint_total, output_total = sum_over_chips((joint_half, output_half), orders, chips)
    grad_stream = grad_first + jnp.einsum(
        "tc,dc->td", grad_joint, joint_weight, preferred_element_type=jnp.float32
    )
    joint_total = joint_total.astype(jnp.float32)
    return (
        normed_final.astype(jnp.bfloat16),
        dual_final.astype(jnp.bfloat16),
        grad_stream,
        joint_total[:, :half],
        joint_total[:, half : 2 * half],
        joint_total[:, 2 * half :],
        output_total.astype(jnp.float32),
        small[0],
        small[1],
        up_total.astype(jnp.float32),
        down_total.astype(jnp.float32),
        small[2],
        small[3],
    )


def solution(mesh):
    rows = P(("dp", "mp"), None)
    columns = P(None, "mp")
    return jax.shard_map(
        partial(on_device, chips=mesh.shape["dp"]),
        mesh=mesh,
        in_specs=(
            rows, rows, columns, columns, columns, P("mp", None), P(), P(),
            columns, P("mp", None), P(), P(), P("dp"), rows, rows,
        ),
        out_specs=(
            rows, rows, rows, columns, columns, columns, P("mp", None), P(), P(),
            columns, P("mp", None), P(), P(),
        ),
        check_vma=False,
    )
```

```python
from functools import partial

import jax
import jax.numpy as jnp
from jax import lax
from jax.experimental import pallas as pl
from jax.experimental.pallas import tpu as pltpu
from jax.sharding import PartitionSpec as P

norm_eps = 1e-05
BLOCK = 512
GATE = 0.7978845608028654
CUBE = 0.044715
HD = 64
LEN = 1024
TILE = 128
TILES = LEN // TILE
PAIR = 2 * HD
FAR = -1e30
MARKS = 16
LSE_ROW = 8
LIVE_LANE = 12
MIB = 2**20


def dot(left, right):
    return jnp.dot(left, right, preferred_element_type=jnp.float32)


def three_parts(row):
    high = row.astype(jnp.bfloat16)
    rest = row - high.astype(jnp.float32)
    mid = rest.astype(jnp.bfloat16)
    low = (rest - mid.astype(jnp.float32)).astype(jnp.bfloat16)
    return high, mid, low


def label_marks(labels):
    lane = jnp.arange(TILE)
    key_marks = jnp.where(
        lane < LSE_ROW,
        jnp.where(labels[:, None] == lane, 0.0, FAR),
        jnp.where(
            (lane < LSE_ROW + 3) | ((lane == LIVE_LANE) & (labels[:, None] != 0)), 1.0, 0.0
        ),
    ).astype(jnp.bfloat16)
    row = jnp.arange(MARKS)[:, None]
    query_marks = ((labels[None, :] == row) & (row < LSE_ROW)).astype(jnp.bfloat16)
    return key_marks, query_marks


def key_ranges(labels):
    seqs = labels.shape[0] // LEN
    table = labels.reshape(seqs, 1, LEN)
    ends = labels.reshape(seqs, TILES, TILE)
    where = jnp.arange(LEN, dtype=jnp.int32)
    first = jnp.min(jnp.where(table == ends[:, :, :1], where, LEN), axis=-1) // TILE
    last = jnp.max(jnp.where(table == ends[:, :, -1:], where, -1), axis=-1) // TILE
    return jnp.stack([first, last - first + 1], axis=-1).astype(jnp.int32).reshape(-1)


def halves_of(block):
    return jnp.concatenate([block[:HD, :TILE], block[HD:, TILE:]], axis=0)


def split_rows(tile_t):
    zero = jnp.zeros((HD, TILE), tile_t.dtype)
    return jnp.concatenate(
        [
            jnp.concatenate([tile_t[:HD], zero], axis=1),
            jnp.concatenate([zero, tile_t[HD:]], axis=1),
        ],
        axis=0,
    )


def split_lanes(tile):
    lane = lax.broadcasted_iota(jnp.int32, tile.shape, 1)
    zero = jnp.zeros_like(tile)
    return jnp.concatenate(
        [jnp.where(lane < HD, tile, zero), jnp.where(lane < HD, zero, tile)], axis=0
    )


def each_width(count, branch):
    for width in range(1, TILES + 1):
        pl.when(count == width)(partial(branch, width))


def attend_kernel(
    ranges, q_ref, k_ref, v_ref, key_marks, query_marks, out_ref, lse_ref, kcat, vt
):
    seq = pl.program_id(0)
    pairs = q_ref.shape[1] // PAIR
    for p in range(pairs):
        lanes = slice(p * PAIR, (p + 1) * PAIR)
        kcat[p, :, :PAIR] = k_ref[:, lanes]
        kcat[p, :, PAIR:] = key_marks[...]
        vt[lanes, :] = v_ref[:, lanes].T

    def step(i, carry):
        at = pl.multiple_of(i * TILE, TILE)
        first = ranges[(seq * TILES + i) * 2]
        count = ranges[(seq * TILES + i) * 2 + 1]
        start = pl.multiple_of(first * TILE, TILE)

        def branch(width):
            at_keys = pl.ds(start, width * TILE)
            marks = query_marks[:, pl.ds(at, TILE)]
            live = 1.0 - marks[:1].astype(jnp.float32)
            marks = jnp.concatenate([marks, marks], axis=1)
            rest = jnp.zeros((TILE - MARKS, 2 * TILE), jnp.bfloat16)

            def scores_of(p):
                query = q_ref[pl.ds(at, TILE), p * PAIR : (p + 1) * PAIR] * jnp.bfloat16(HD**-0.5)
                right = jnp.concatenate([split_rows(query.T), marks, rest], axis=0)
                return dot(kcat[p, at_keys, :], right)

            def finish(p, scores):
                top = jnp.max(scores, axis=0, keepdims=True)
                probs = jnp.exp(scores - top)
                total = jnp.sum(probs, axis=0, keepdims=True)
                mixed = dot(vt[p * PAIR : (p + 1) * PAIR, at_keys], probs.astype(jnp.bfloat16))
                mixed = halves_of(mixed / total) * live
                out_ref[pl.ds(at, TILE), p * PAIR : (p + 1) * PAIR] = mixed.T.astype(jnp.bfloat16)
                lse_ref[0, p, pl.ds(i, 1), :] = top + jnp.log(total)

            ahead = scores_of(0)
            for p in range(pairs):
                scores = ahead
                if p + 1 < pairs:
                    ahead = scores_of(p + 1)
                finish(p, scores)

        each_width(count, branch)
        return carry

    lax.fori_loop(0, TILES, step, 0)


def attend(ranges, qkv, key_marks, query_marks):
    rows, width = qkv.shape[0], qkv.shape[1] // 3
    seqs, pairs = rows // LEN, width // PAIR
    return pl.pallas_call(
        attend_kernel,
        grid_spec=pltpu.PrefetchScalarGridSpec(
            num_scalar_prefetch=1,
            grid=(seqs,),
            in_specs=[
                pl.BlockSpec((LEN, width), lambda s, _: (s, 0)),
                pl.BlockSpec((LEN, width), lambda s, _: (s, 1)),
                pl.BlockSpec((LEN, width), lambda s, _: (s, 2)),
                pl.BlockSpec((LEN, TILE), lambda s, _: (s, 0)),
                pl.BlockSpec((MARKS, LEN), lambda s, _: (0, s)),
            ],
            out_specs=[
                pl.BlockSpec((LEN, width), lambda s, _: (s, 0)),
                pl.BlockSpec((1, pairs, TILES, 2 * TILE), lambda s, _: (s, 0, 0, 0)),
            ],
            scratch_shapes=[
                pltpu.VMEM((pairs, LEN, PAIR + TILE), jnp.bfloat16),
                pltpu.VMEM((width, LEN), jnp.bfloat16),
            ],
        ),
        out_shape=[
            jax.ShapeDtypeStruct((rows, width), jnp.bfloat16),
            jax.ShapeDtypeStruct((seqs, pairs, TILES, 2 * TILE), jnp.float32),
        ],
        compiler_params=pltpu.CompilerParams(vmem_limit_bytes=48 * MIB),
        name="attend",
    )(ranges, qkv, qkv, qkv, key_marks, query_marks)


def dot_nt(left, right):
    return lax.dot_general(
        left, right, (((1,), (1,)), ((), ())), preferred_element_type=jnp.float32
    )


def dot_tn(left, right):
    return lax.dot_general(
        left, right, (((0,), (0,)), ((), ())), preferred_element_type=jnp.float32
    )


def full(ref):
    shape = ref.shape
    return pl.BlockSpec(shape, lambda *_: (0,) * len(shape), pipeline_mode=pl.Buffered(1))


def call(kernel, name, grid, ins, outs, scratch=(), scalars=(), flops=0):
    specs, arrays = [], []
    for item in ins:
        if isinstance(item, tuple):
            arrays.append(item[0])
            specs.append(pl.BlockSpec(item[1], item[2]))
        else:
            arrays.append(item)
            specs.append(full(item))
    size = sum(a.size * a.dtype.itemsize for a in arrays)
    size += sum(jnp.dtype(d).itemsize * s[0] * s[1] for s, d, _, _ in outs)
    return pl.pallas_call(
        kernel,
        grid_spec=pltpu.PrefetchScalarGridSpec(
            num_scalar_prefetch=len(scalars),
            grid=grid,
            in_specs=specs,
            out_specs=[pl.BlockSpec(b, m) for _, _, b, m in outs],
            scratch_shapes=scratch,
        ),
        out_shape=[jax.ShapeDtypeStruct(s, d) for s, d, _, _ in outs],
        compiler_params=pltpu.CompilerParams(vmem_limit_bytes=56 * MIB),
        cost_estimate=pl.CostEstimate(flops=flops, bytes_accessed=size, transcendentals=0),
        name=name,
    )(*scalars, *arrays)


def project_kernel(x_ref, qa, ka, va, qb, kb, vb, out_ref):
    x = x_ref[...]
    half = qa.shape[1]
    for i, w in enumerate((qa, qb, ka, kb, va, vb)):
        out_ref[:, i * half : (i + 1) * half] = dot(x, w[...]).astype(jnp.bfloat16)


def rows_of(i, *_):
    return (i, 0)


def project(x, own, other):
    rows, depth = x.shape
    width = 6 * own[0].shape[1]
    return call(
        project_kernel, "project", (rows // BLOCK,),
        [(x, (BLOCK, depth), rows_of), *own, *other],
        [((rows, width), jnp.bfloat16, (BLOCK, width), rows_of)],
        flops=2 * rows * depth * width,
    )[0]


def stats(z):
    mean = jnp.mean(z, axis=-1, keepdims=True)
    centred = z - mean
    spread = jnp.mean(centred * centred, axis=-1, keepdims=True)
    scale = lax.rsqrt(spread + norm_eps)
    return centred * scale, scale


def norm_back(upstream, unit, scale, gain):
    t = upstream * gain
    inner = jnp.mean(t * unit, axis=-1, keepdims=True)
    return (t - jnp.mean(t, axis=-1, keepdims=True) - unit * inner) * scale


def layer_kernel(
    heads, x, dual, gn, gd, marks, out_a, out_b, up_a, up_b, down_a, down_b, g1, b1, g2, b2,
    normed_out, dual_out, gfirst_ref, gheads, ffn_grad_a, ffn_grad_b, out_grad_a, out_grad_b, sums,
    hid, slope, acc_up, acc_down, acc_out,
):
    i = pl.program_id(0)
    half = out_a.shape[0]
    ff = up_a.shape[1]
    chunk = 512

    @pl.when(i == 0)
    def _():
        sums[...] = jnp.zeros_like(sums)
        acc_up[...] = jnp.zeros_like(acc_up)
        acc_down[...] = jnp.zeros_like(acc_down)
        acc_out[...] = jnp.zeros_like(acc_out)

    attn = dot(heads[:, :half], out_a[...]) + dot(heads[:, half:], out_b[...])
    z1 = x[...].astype(jnp.float32) + attn
    unit, scale = stats(z1)
    normed = unit * g1[...] + b1[...]
    low = normed.astype(jnp.bfloat16)
    ffn = None
    for n, (up, down) in enumerate(((up_a, down_a), (up_b, down_b))):
        for c in range(ff // chunk):
            cols = slice(c * chunk, (c + 1) * chunk)
            at = slice(n * ff + c * chunk, n * ff + (c + 1) * chunk)
            v = dot(low, up[:, cols])
            square = v * v
            t = jnp.tanh(v * (GATE + (GATE * CUBE) * square))
            open_part = 0.5 + 0.5 * t
            hidden = (v * open_part).astype(jnp.bfloat16)
            hid[:, at] = hidden
            slope[:, at] = open_part + (v * (0.5 - 0.5 * t * t)) * (
                GATE + (3 * GATE * CUBE) * square
            )
            part = dot(hidden, down[cols, :])
            ffn = part if ffn is None else ffn + part
    unit2, scale2 = stats(normed + ffn)
    normed_out[...] = (unit2 * g2[...] + b2[...]).astype(jnp.bfloat16)
    dual_out[...] = (dual[...].astype(jnp.float32) + attn + ffn).astype(jnp.bfloat16)
    upstream = gn[...].astype(jnp.float32)
    gmid = norm_back(upstream, unit2, scale2, g2[...])
    gdual = gd[...].astype(jnp.float32)
    gffn = (gmid + gdual).astype(jnp.bfloat16)
    gffn_t = gffn.T
    low_t = low.T
    gnormed = gmid
    for n, (up, down) in enumerate(((up_a, down_a), (up_b, down_b))):
        for c in range(ff // chunk):
            cols = slice(c * chunk, (c + 1) * chunk)
            at = slice(n * ff + c * chunk, n * ff + (c + 1) * chunk)
            gpre = (dot_nt(gffn, down[cols, :]) * slope[:, at]).astype(jnp.bfloat16)
            acc_down[:, at] += dot(gffn_t, hid[:, at])
            acc_up[:, at] += dot(low_t, gpre)
            gnormed = gnormed + dot_nt(gpre, up[:, cols])
    gfirst = norm_back(gnormed, unit, scale, g1[...])
    gfirst_ref[...] = gfirst
    gattn = (gfirst + gdual).astype(jnp.bfloat16)
    sums[0:1, :] += jnp.sum(gnormed * unit, axis=0, keepdims=True)
    sums[1:2, :] += jnp.sum(gnormed, axis=0, keepdims=True)
    sums[2:3, :] += jnp.sum(upstream * unit2, axis=0, keepdims=True)
    sums[3:4, :] += jnp.sum(upstream, axis=0, keepdims=True)
    acc_out[...] += dot_tn(heads[...], gattn)
    live = marks[:, LIVE_LANE : LIVE_LANE + 1].astype(jnp.float32)
    gheads[:, :half] = (dot_nt(gattn, out_a[...]) * live).astype(jnp.bfloat16)
    gheads[:, half:] = (dot_nt(gattn, out_b[...]) * live).astype(jnp.bfloat16)

    @pl.when(i == pl.num_programs(0) - 1)
    def _():
        depth = acc_up.shape[0]
        for n, (ffn_grad, out_grad) in enumerate(
            ((ffn_grad_a, out_grad_a), (ffn_grad_b, out_grad_b))
        ):
            ffn_grad[:ff, :] = acc_down[:, n * ff : (n + 1) * ff].T.astype(jnp.bfloat16)
            for c in range(ff // depth):
                at = n * ff + c * depth
                ffn_grad[ff + c * depth : ff + (c + 1) * depth, :] = acc_up[
                    :, at : at + depth
                ].astype(jnp.bfloat16)
            out_grad[...] = acc_out[n * half : (n + 1) * half, :].astype(jnp.bfloat16)


def layer(heads, x, dual, gn, gd, marks, outs, ups, downs, g1, b1, g2, b2, block=BLOCK):
    rows, depth = x.shape
    ff, half = ups[0].shape[1], outs[0].shape[0]
    tall = ((rows, depth), jnp.bfloat16, (block, depth), rows_of)
    tall32 = ((rows, depth), jnp.float32, (block, depth), rows_of)

    def once(*shape, dtype=jnp.bfloat16):
        return (shape, dtype, shape, lambda i: (0, 0))

    return call(
        layer_kernel, "layer", (rows // block,),
        [(a, (block, a.shape[1]), rows_of) for a in (heads, x, dual, gn, gd, marks)]
        + [*outs, *ups, *downs, g1, b1, g2, b2],
        [tall, tall, tall32, tall, once(2 * ff, depth), once(2 * ff, depth), once(half, depth), once(half, depth), once(8, depth, dtype=jnp.float32)],
        scratch=[
            pltpu.VMEM((block, 2 * ff), jnp.bfloat16),
            pltpu.VMEM((block, 2 * ff), jnp.float32),
            pltpu.VMEM((depth, 2 * ff), jnp.float32),
            pltpu.VMEM((depth, 2 * ff), jnp.float32),
            pltpu.VMEM((2 * half, depth), jnp.float32),
        ],
        flops=2 * rows * depth * (3 * depth + 12 * ff),
    )


def attend_back_kernel(
    pairs, ranges, *refs,
):
    q_refs, k_refs, v_refs, g_refs, o_refs = (refs[n * pairs : (n + 1) * pairs] for n in range(5))
    (x_ref, key_marks, query_marks, lse_ref, *extra,
     out_ref, own_ref, other_ref, kcat, vcat, kt, dk, dv, acc) = refs[5 * pairs :]
    seq = pl.program_id(0)
    for p in range(pairs):
        kcat[p, :, :PAIR] = k_refs[p][...]
        kcat[p, :, PAIR:] = key_marks[...]
        vcat[p, :, :PAIR] = v_refs[p][...]
        vcat[p, :, PAIR:] = key_marks[...]
        kt[p] = k_refs[p][...].T
    dk[...] = jnp.zeros_like(dk)
    dv[...] = jnp.zeros_like(dv)

    def negated(row):
        return [part.astype(jnp.float32) for part in three_parts(-row)]

    def step(i, carry):
        at = pl.multiple_of(i * TILE, TILE)
        first = ranges[(seq * TILES + i) * 2]
        count = ranges[(seq * TILES + i) * 2 + 1]
        start = pl.multiple_of(first * TILE, TILE)

        def branch(width):
            at_keys = pl.ds(start, width * TILE)
            marks = query_marks[:LSE_ROW, pl.ds(at, TILE)].astype(jnp.float32)
            marks = jnp.concatenate([marks, marks], axis=1)
            rest = jnp.zeros((TILE - MARKS, 2 * TILE), jnp.bfloat16)
            pad = jnp.zeros((MARKS - LSE_ROW - 3, 2 * TILE), jnp.float32)
            none = jnp.zeros((LSE_ROW, 2 * TILE), jnp.float32)

            def head(p):
                query = q_refs[p][pl.ds(at, TILE), :] * jnp.bfloat16(HD**-0.5)
                grad = g_refs[p][pl.ds(at, TILE), :]
                lse = lse_ref[0, p, pl.ds(i, 1), :]
                lse_rows = jnp.concatenate([marks, *negated(lse), pad], axis=0)
                agree = grad.astype(jnp.float32) * o_refs[p][pl.ds(at, TILE), :].astype(jnp.float32)
                agree = agree.T
                delta = jnp.concatenate(
                    [
                        jnp.sum(agree[:HD], axis=0, keepdims=True),
                        jnp.sum(agree[HD:], axis=0, keepdims=True),
                    ],
                    axis=1,
                )
                delta_rows = jnp.concatenate([none, *negated(delta), pad], axis=0)
                qt = jnp.concatenate(
                    [split_rows(query.T), lse_rows.astype(jnp.bfloat16), rest], axis=0
                )
                gt = jnp.concatenate(
                    [split_rows(grad.T), delta_rows.astype(jnp.bfloat16), rest], axis=0
                )
                scores = dot(kcat[p, at_keys, :], qt)
                grad_probs = dot(vcat[p, at_keys, :], gt)
                return query, grad, scores, grad_probs

            def finish(p, query, grad, scores, grad_probs):
                probs = jnp.exp(scores)
                grad_scores = (probs * grad_probs).astype(jnp.bfloat16)
                dv[p, at_keys, :] += dot(probs.astype(jnp.bfloat16), split_lanes(grad))
                dk[p, at_keys, :] += dot(grad_scores, split_lanes(query))
                dqt = halves_of(dot(kt[p, :, at_keys], grad_scores)) * HD**-0.5
                out_ref[pl.ds(at, TILE), 3 * p * PAIR : (3 * p + 1) * PAIR] = dqt.T.astype(
                    jnp.bfloat16
                )

            ahead = head(0)
            for p in range(pairs):
                now = ahead
                if p + 1 < pairs:
                    ahead = head(p + 1)
                finish(p, *now)

        each_width(count, branch)
        return carry

    lax.fori_loop(0, TILES, step, 0)
    for p in range(pairs):
        out_ref[:, (3 * p + 1) * PAIR : (3 * p + 2) * PAIR] = dk[p].astype(jnp.bfloat16)
        out_ref[:, (3 * p + 2) * PAIR : (3 * p + 3) * PAIR] = dv[p].astype(jnp.bfloat16)

    @pl.when(seq == 0)
    def _():
        acc[...] = jnp.zeros_like(acc)

    acc[...] += dot_tn(x_ref[...], out_ref[...])

    @pl.when(seq == pl.num_programs(0) - 1)
    def _():
        wide = pairs // 2 * 3
        depth = acc.shape[0]
        for n, buf in enumerate((own_ref, other_ref)):
            for m in range(wide):
                for r in range(depth // PAIR):
                    buf[m * PAIR : (m + 1) * PAIR, r * PAIR : (r + 1) * PAIR] = acc[
                        r * PAIR : (r + 1) * PAIR, (n * wide + m) * PAIR : (n * wide + m + 1) * PAIR
                    ].astype(jnp.bfloat16)
            used = wide * PAIR
            if extra:
                out_grad, sums = extra[n], extra[2]
                buf[used : used + out_grad.shape[0], :] = out_grad[...]
                used += out_grad.shape[0]
                both = jnp.concatenate([sums[...], jnp.zeros_like(sums)], axis=0)
                buf[used : used + MARKS, :] = both.astype(jnp.bfloat16)
                used += MARKS
            if used < buf.shape[0]:
                buf[used:, :] = jnp.zeros((buf.shape[0] - used, depth), jnp.bfloat16)


def attend_back(ranges, x, qkv, gheads, heads, key_marks, query_marks, lse, group, extra, height):
    rows, depth = x.shape
    width = heads.shape[1]
    seqs, total, pairs = rows // LEN, width // PAIR, len(group)
    by_seq = lambda s, _: (s, 0)
    ins = []
    for array, base in ((qkv, 0), (qkv, total), (qkv, 2 * total), (gheads, 0), (heads, 0)):
        for p in group:
            ins.append((array, (LEN, PAIR), lambda s, _, at=base + p: (s, at)))
    lse = lse[:, jnp.asarray(group)]
    ins += [
        (x, (LEN, depth), by_seq),
        (key_marks, (LEN, TILE), by_seq),
        (query_marks, (MARKS, LEN), lambda s, _: (0, s)),
        (lse, (1, pairs, TILES, 2 * TILE), lambda s, _: (s, 0, 0, 0)),
        *extra,
    ]
    wide = 3 * pairs * PAIR
    buf = ((height, depth), jnp.bfloat16, (height, depth), lambda s, _: (0, 0))
    return call(
        partial(attend_back_kernel, pairs), "attend_back", (seqs,), ins,
        [((rows, wide), jnp.bfloat16, (LEN, wide), by_seq), buf, buf],
        scratch=[
            pltpu.VMEM((pairs, LEN, PAIR + TILE), jnp.bfloat16),
            pltpu.VMEM((pairs, LEN, PAIR + TILE), jnp.bfloat16),
            pltpu.VMEM((pairs, PAIR, LEN), jnp.bfloat16),
            pltpu.VMEM((pairs, LEN, PAIR), jnp.float32),
            pltpu.VMEM((pairs, LEN, PAIR), jnp.float32),
            pltpu.VMEM((depth, wide), jnp.float32),
        ],
        scalars=(ranges,),
        flops=2 * rows * wide * (LEN * 2 + depth),
    )


def stream_kernel(gfirst, grad_a, grad_b, *refs):
    weights, out = refs[:-1], refs[-1]
    total = gfirst[...]
    for grad, half in ((grad_a, 0), (grad_b, 1)):
        for n in range(6):
            total = total + dot_nt(
                grad[:, n * PAIR : (n + 1) * PAIR],
                weights[n][:, half * PAIR : (half + 1) * PAIR],
            )
    out[...] = total


def stream(gfirst, grad_a, grad_b, own, other):
    rows, depth = gfirst.shape
    return call(
        stream_kernel, "stream", (rows // BLOCK,),
        [(a, (BLOCK, a.shape[1]), rows_of) for a in (gfirst, grad_a, grad_b)] + [*own, *other],
        [((rows, depth), jnp.float32, (BLOCK, depth), rows_of)],
        flops=2 * rows * depth * 3 * depth,
    )[0]


def swap_cores(block):
    return lax.ppermute(block, "mp", [(0, 1), (1, 0)])


def stages_of(chips):
    me, core = lax.axis_index("dp"), lax.axis_index("mp")
    low, high = me & 1, (me >> 1) & 1

    def pairs(masks):
        return [(2 * c + i, 2 * (c ^ masks[i]) + i) for c in range(chips) for i in range(2)]

    stages = [
        (jnp.where(core == 0, low, high), 2, [pairs((1, 2))]),
        (jnp.where(core == 0, high, low), 2, [pairs((2, 1))]),
    ]
    bit = 2
    while 1 << bit < chips:
        radix = 4 if 1 << (bit + 1) < chips else 2
        stages.append(
            (
                (me >> bit) & (radix - 1),
                radix,
                [pairs((j << bit, j << bit)) for j in range(1, radix)],
            )
        )
        bit += radix // 2
    return stages


def send(block, pairs):
    return lax.ppermute(block, ("dp", "mp"), pairs)


def part(block, which, rows):
    return lax.dynamic_slice_in_dim(block, which * rows, rows)


def added(blocks):
    total = blocks[0].astype(jnp.float32)
    for block in blocks[1:]:
        total = total + block.astype(jnp.float32)
    return total.astype(jnp.bfloat16)


def unpack_kernel(size, shapes, places, *refs):
    pieces, outs, table = refs[: -len(shapes) - 1], refs[-len(shapes) - 1 : -1], refs[-1]
    at = 0
    for piece in pieces:
        block = piece[...].astype(jnp.float32)
        for n in range(block.shape[0] // size):
            table[pl.ds(pl.multiple_of(places[at] * size, size), size), :] = block[
                n * size : (n + 1) * size
            ]
            at += 1
    row = 0
    for out, (kind, height, width) in zip(outs, shapes):
        depth = table.shape[1]
        if kind == "rows":
            out[...] = table[row : row + height, :]
            row += height
        elif kind == "wide":
            for n in range(width // depth):
                out[:, n * depth : (n + 1) * depth] = table[row : row + height, :]
                row += height
        else:
            for n in range(height // width):
                out[n * width : (n + 1) * width, :] = table[
                    row : row + width, n * width : (n + 1) * width
                ]
            row += width


def unpack(pieces, places, shapes, rows, chips):
    depth = pieces[0].shape[1]
    size = rows // chips
    return call(
        partial(unpack_kernel, size, shapes), "unpack", (1,), pieces,
        [((h, w), jnp.float32, (h, w), lambda i, _: (0, 0)) for _, h, w in shapes],
        scratch=[pltpu.VMEM((rows, depth), jnp.float32)],
        scalars=(places,),
    )


def sum_everywhere(own, other, shapes, chips):
    rows = own.shape[0]
    stages = stages_of(chips)
    addends = [own, swap_cores(other)]
    height = rows
    for digit, radix, ways in stages:
        height //= radix
        got = [
            send(added([part(a, digit ^ (j + 1), height) for a in addends]), pairs)
            for j, pairs in enumerate(ways)
        ]
        addends = [part(a, digit, height) for a in addends] + got
    pieces = [added(addends)]
    places = [jnp.int32(0)]
    for n, (digit, radix, ways) in enumerate(reversed(stages)):
        weight = chips
        for _, earlier, _ in stages[: len(stages) - n]:
            weight //= earlier
        held = pieces[0] if len(pieces) == 1 else jnp.concatenate(pieces)
        pieces = [held] + [send(held, pairs) for pairs in ways]
        places = [p + (digit ^ j) * weight for j in range(radix) for p in places]
    return unpack(pieces, jnp.stack(places).astype(jnp.int32), shapes, rows, chips)


def on_device(
    normed_in,
    dual_in,
    query_weight,
    key_weight,
    value_weight,
    output_weight,
    first_gain,
    first_bias,
    up_weight,
    down_weight,
    second_gain,
    second_bias,
    segments,
    grad_normed_out,
    grad_dual_out,
    chips,
):
    rows, depth = normed_in.shape
    core = lax.axis_index("mp")
    half, ff = query_weight.shape[1], up_weight.shape[1]
    own = (query_weight, key_weight, value_weight)
    other = tuple(swap_cores(w) for w in own)
    outs = (output_weight, swap_cores(output_weight))
    ups = (up_weight, swap_cores(up_weight))
    downs = (down_weight, swap_cores(down_weight))
    labels = lax.dynamic_slice(segments, (core * rows,), (rows,))
    key_marks, query_marks = label_marks(labels)
    ranges = key_ranges(labels)
    qkv = project(normed_in, own, other)
    heads_out, log_totals = attend(ranges, qkv, key_marks, query_marks)
    row = lambda v: v.reshape(1, depth)
    (normed_out, dual_out, grad_first, grad_heads, ffn_own, ffn_other, out_own, out_other, sums) = (
        layer(
            heads_out, normed_in, dual_in, grad_normed_out, grad_dual_out, key_marks, outs, ups,
            downs, row(first_gain), row(first_bias), row(second_gain), row(second_bias),
        )
    )
    down_total, up_total = sum_everywhere(
        ffn_own, ffn_other, [("rows", ff, depth), ("wide", depth, ff)], chips
    )
    back = partial(
        attend_back, ranges, normed_in, qkv, grad_heads, heads_out, key_marks, query_marks,
        log_totals,
    )
    grain = 8 * chips

    def padded(count):
        return -(-count // grain) * grain

    tall = 3 * PAIR
    grad_a, own_a, other_a = back(
        (0, 2), (out_own, out_other, sums), padded(tall + half + MARKS)
    )
    grad_b, own_b, other_b = back((1, 3), (), padded(tall))
    narrow = [("blocks", depth, PAIR)] * 3
    query_a, key_a, value_a, output_total, small = sum_everywhere(
        own_a, other_a, narrow + [("rows", half, depth), ("rows", 8, depth)], chips
    )
    query_b, key_b, value_b = sum_everywhere(own_b, other_b, narrow, chips)
    grad_stream = stream(grad_first, grad_a, grad_b, own, other)
    return (
        normed_out,
        dual_out,
        grad_stream,
        jnp.concatenate([query_a, query_b], axis=1),
        jnp.concatenate([key_a, key_b], axis=1),
        jnp.concatenate([value_a, value_b], axis=1),
        output_total,
        small[0],
        small[1],
        up_total,
        down_total,
        small[2],
        small[3],
    )


def solution(mesh):
    rows = P(("dp", "mp"), None)
    columns = P(None, "mp")
    return jax.shard_map(
        partial(on_device, chips=mesh.shape["dp"]),
        mesh=mesh,
        in_specs=(
            rows, rows, columns, columns, columns, P("mp", None), P(), P(),
            columns, P("mp", None), P(), P(), P("dp"), rows, rows,
        ),
        out_specs=(
            rows, rows, rows, columns, columns, columns, P("mp", None), P(), P(),
            columns, P("mp", None), P(), P(),
        ),
        check_vma=False,
    )
```

```python
from functools import partial

import jax
import jax.numpy as jnp
from jax import lax
from jax.experimental import pallas as pl
from jax.experimental.pallas import tpu as pltpu
from jax.sharding import PartitionSpec as P

norm_eps = 1e-05
BLOCK = 512
GATE = 0.7978845608028654
CUBE = 0.044715
HD = 64
LEN = 1024
TILE = 128
TILES = LEN // TILE
PAIR = 2 * HD
FAR = -1e30
MARKS = 16
LSE_ROW = 8
LIVE_LANE = 12
MIB = 2**20


def dot(left, right):
    return jnp.dot(left, right, preferred_element_type=jnp.float32)


def three_parts(row):
    high = row.astype(jnp.bfloat16)
    rest = row - high.astype(jnp.float32)
    mid = rest.astype(jnp.bfloat16)
    low = (rest - mid.astype(jnp.float32)).astype(jnp.bfloat16)
    return high, mid, low


def label_marks(labels):
    lane = jnp.arange(TILE)
    key_marks = jnp.where(
        lane < LSE_ROW,
        jnp.where(labels[:, None] == lane, 0.0, FAR),
        jnp.where(
            (lane < LSE_ROW + 3) | ((lane == LIVE_LANE) & (labels[:, None] != 0)), 1.0, 0.0
        ),
    ).astype(jnp.bfloat16)
    row = jnp.arange(MARKS)[:, None]
    query_marks = ((labels[None, :] == row) & (row < LSE_ROW)).astype(jnp.bfloat16)
    return key_marks, query_marks


def key_ranges(labels):
    seqs = labels.shape[0] // LEN
    table = labels.reshape(seqs, 1, LEN)
    ends = labels.reshape(seqs, TILES, TILE)
    where = jnp.arange(LEN, dtype=jnp.int32)
    first = jnp.min(jnp.where(table == ends[:, :, :1], where, LEN), axis=-1) // TILE
    last = jnp.max(jnp.where(table == ends[:, :, -1:], where, -1), axis=-1) // TILE
    return jnp.stack([first, last - first + 1], axis=-1).astype(jnp.int32).reshape(-1)


def halves_of(block):
    return jnp.concatenate([block[:HD, :TILE], block[HD:, TILE:]], axis=0)


def split_rows(tile_t):
    zero = jnp.zeros((HD, TILE), tile_t.dtype)
    return jnp.concatenate(
        [
            jnp.concatenate([tile_t[:HD], zero], axis=1),
            jnp.concatenate([zero, tile_t[HD:]], axis=1),
        ],
        axis=0,
    )


def split_lanes(tile):
    lane = lax.broadcasted_iota(jnp.int32, tile.shape, 1)
    zero = jnp.zeros_like(tile)
    return jnp.concatenate(
        [jnp.where(lane < HD, tile, zero), jnp.where(lane < HD, zero, tile)], axis=0
    )


def each_width(count, branch):
    for width in range(1, TILES + 1):
        pl.when(count == width)(partial(branch, width))


def attend_kernel(
    ranges, q_ref, k_ref, v_ref, key_marks, query_marks, out_ref, lse_ref, kcat, vt
):
    seq = pl.program_id(0)
    pairs = q_ref.shape[1] // PAIR
    for p in range(pairs):
        lanes = slice(p * PAIR, (p + 1) * PAIR)
        kcat[p, :, :PAIR] = k_ref[:, lanes]
        kcat[p, :, PAIR:] = key_marks[...]
        vt[lanes, :] = v_ref[:, lanes].T

    def step(i, carry):
        at = pl.multiple_of(i * TILE, TILE)
        first = ranges[(seq * TILES + i) * 2]
        count = ranges[(seq * TILES + i) * 2 + 1]
        start = pl.multiple_of(first * TILE, TILE)

        def branch(width):
            at_keys = pl.ds(start, width * TILE)
            marks = query_marks[:, pl.ds(at, TILE)]
            live = 1.0 - marks[:1].astype(jnp.float32)
            marks = jnp.concatenate([marks, marks], axis=1)
            rest = jnp.zeros((TILE - MARKS, 2 * TILE), jnp.bfloat16)

            def scores_of(p):
                query = q_ref[pl.ds(at, TILE), p * PAIR : (p + 1) * PAIR] * jnp.bfloat16(HD**-0.5)
                right = jnp.concatenate([split_rows(query.T), marks, rest], axis=0)
                return dot(kcat[p, at_keys, :], right)

            def finish(p, scores):
                top = jnp.max(scores, axis=0, keepdims=True)
                probs = jnp.exp(scores - top)
                total = jnp.sum(probs, axis=0, keepdims=True)
                mixed = dot(vt[p * PAIR : (p + 1) * PAIR, at_keys], probs.astype(jnp.bfloat16))
                mixed = halves_of(mixed / total) * live
                out_ref[pl.ds(at, TILE), p * PAIR : (p + 1) * PAIR] = mixed.T.astype(jnp.bfloat16)
                lse_ref[0, p, pl.ds(i, 1), :] = top + jnp.log(total)

            ahead = scores_of(0)
            for p in range(pairs):
                scores = ahead
                if p + 1 < pairs:
                    ahead = scores_of(p + 1)
                finish(p, scores)

        each_width(count, branch)
        return carry

    lax.fori_loop(0, TILES, step, 0)


def attend(ranges, qkv, key_marks, query_marks):
    rows, width = qkv.shape[0], qkv.shape[1] // 3
    seqs, pairs = rows // LEN, width // PAIR
    return pl.pallas_call(
        attend_kernel,
        grid_spec=pltpu.PrefetchScalarGridSpec(
            num_scalar_prefetch=1,
            grid=(seqs,),
            in_specs=[
                pl.BlockSpec((LEN, width), lambda s, _: (s, 0)),
                pl.BlockSpec((LEN, width), lambda s, _: (s, 1)),
                pl.BlockSpec((LEN, width), lambda s, _: (s, 2)),
                pl.BlockSpec((LEN, TILE), lambda s, _: (s, 0)),
                pl.BlockSpec((MARKS, LEN), lambda s, _: (0, s)),
            ],
            out_specs=[
                pl.BlockSpec((LEN, width), lambda s, _: (s, 0)),
                pl.BlockSpec((1, pairs, TILES, 2 * TILE), lambda s, _: (s, 0, 0, 0)),
            ],
            scratch_shapes=[
                pltpu.VMEM((pairs, LEN, PAIR + TILE), jnp.bfloat16),
                pltpu.VMEM((width, LEN), jnp.bfloat16),
            ],
        ),
        out_shape=[
            jax.ShapeDtypeStruct((rows, width), jnp.bfloat16),
            jax.ShapeDtypeStruct((seqs, pairs, TILES, 2 * TILE), jnp.float32),
        ],
        compiler_params=pltpu.CompilerParams(vmem_limit_bytes=48 * MIB),
        name="attend",
    )(ranges, qkv, qkv, qkv, key_marks, query_marks)


def dot_nt(left, right):
    return lax.dot_general(
        left, right, (((1,), (1,)), ((), ())), preferred_element_type=jnp.float32
    )


def dot_tn(left, right):
    return lax.dot_general(
        left, right, (((0,), (0,)), ((), ())), preferred_element_type=jnp.float32
    )


def full(ref):
    shape = ref.shape
    return pl.BlockSpec(shape, lambda *_: (0,) * len(shape), pipeline_mode=pl.Buffered(1))


def call(kernel, name, grid, ins, outs, scratch=(), scalars=(), flops=0, aliases=None):
    specs, arrays = [], []
    for item in ins:
        if isinstance(item, tuple):
            arrays.append(item[0])
            if item[1] is None:
                specs.append(pl.BlockSpec(memory_space=pl.ANY))
            else:
                specs.append(pl.BlockSpec(item[1], item[2]))
        else:
            arrays.append(item)
            specs.append(full(item))
    size = sum(a.size * a.dtype.itemsize for a in arrays)
    size += sum(jnp.dtype(d).itemsize * s[0] * s[1] for s, d, _, _ in outs)
    return pl.pallas_call(
        kernel,
        grid_spec=pltpu.PrefetchScalarGridSpec(
            num_scalar_prefetch=len(scalars),
            grid=grid,
            in_specs=specs,
            out_specs=[pl.BlockSpec(b, m) for _, _, b, m in outs],
            scratch_shapes=scratch,
        ),
        out_shape=[jax.ShapeDtypeStruct(s, d) for s, d, _, _ in outs],
        compiler_params=pltpu.CompilerParams(vmem_limit_bytes=56 * MIB),
        cost_estimate=pl.CostEstimate(flops=flops, bytes_accessed=size, transcendentals=0),
        input_output_aliases=aliases or {},
        name=name,
    )(*scalars, *arrays)


def project_kernel(x_ref, qa, ka, va, qb, kb, vb, out_ref):
    x = x_ref[...]
    half = qa.shape[1]
    for i, w in enumerate((qa, qb, ka, kb, va, vb)):
        out_ref[:, i * half : (i + 1) * half] = dot(x, w[...]).astype(jnp.bfloat16)


def rows_of(i, *_):
    return (i, 0)


def project(x, own, other):
    rows, depth = x.shape
    width = 6 * own[0].shape[1]
    return call(
        project_kernel, "project", (rows // BLOCK,),
        [(x, (BLOCK, depth), rows_of), *own, *other],
        [((rows, width), jnp.bfloat16, (BLOCK, width), rows_of)],
        flops=2 * rows * depth * width,
    )[0]


def stats(z):
    mean = jnp.mean(z, axis=-1, keepdims=True)
    centred = z - mean
    spread = jnp.mean(centred * centred, axis=-1, keepdims=True)
    scale = lax.rsqrt(spread + norm_eps)
    return centred * scale, scale


def norm_back(upstream, unit, scale, gain):
    t = upstream * gain
    inner = jnp.mean(t * unit, axis=-1, keepdims=True)
    return (t - jnp.mean(t, axis=-1, keepdims=True) - unit * inner) * scale


def layer_kernel(
    heads, x, dual, gn, gd, marks, out_a, out_b, up_a, up_b, down_a, down_b, g1, b1, g2, b2,
    normed_out, dual_out, gfirst_ref, gheads, ffn_grad_a, ffn_grad_b, out_grad_a, out_grad_b, sums,
    hid, slope, acc_up, acc_down, acc_out,
):
    i = pl.program_id(0)
    half = out_a.shape[0]
    ff = up_a.shape[1]
    chunk = 512

    @pl.when(i == 0)
    def _():
        sums[...] = jnp.zeros_like(sums)
        acc_up[...] = jnp.zeros_like(acc_up)
        acc_down[...] = jnp.zeros_like(acc_down)
        acc_out[...] = jnp.zeros_like(acc_out)

    attn = dot(heads[:, :half], out_a[...]) + dot(heads[:, half:], out_b[...])
    z1 = x[...].astype(jnp.float32) + attn
    unit, scale = stats(z1)
    normed = unit * g1[...] + b1[...]
    low = normed.astype(jnp.bfloat16)
    ffn = None
    for n, (up, down) in enumerate(((up_a, down_a), (up_b, down_b))):
        for c in range(ff // chunk):
            cols = slice(c * chunk, (c + 1) * chunk)
            at = slice(n * ff + c * chunk, n * ff + (c + 1) * chunk)
            v = dot(low, up[:, cols])
            square = v * v
            t = jnp.tanh(v * (GATE + (GATE * CUBE) * square))
            open_part = 0.5 + 0.5 * t
            hidden = (v * open_part).astype(jnp.bfloat16)
            hid[:, at] = hidden
            slope[:, at] = open_part + (v * (0.5 - 0.5 * t * t)) * (
                GATE + (3 * GATE * CUBE) * square
            )
            part = dot(hidden, down[cols, :])
            ffn = part if ffn is None else ffn + part
    unit2, scale2 = stats(normed + ffn)
    normed_out[...] = (unit2 * g2[...] + b2[...]).astype(jnp.bfloat16)
    dual_out[...] = (dual[...].astype(jnp.float32) + attn + ffn).astype(jnp.bfloat16)
    upstream = gn[...].astype(jnp.float32)
    gmid = norm_back(upstream, unit2, scale2, g2[...])
    gdual = gd[...].astype(jnp.float32)
    gffn = (gmid + gdual).astype(jnp.bfloat16)
    gffn_t = gffn.T
    low_t = low.T
    gnormed = gmid
    for n, (up, down) in enumerate(((up_a, down_a), (up_b, down_b))):
        for c in range(ff // chunk):
            cols = slice(c * chunk, (c + 1) * chunk)
            at = slice(n * ff + c * chunk, n * ff + (c + 1) * chunk)
            gpre = (dot_nt(gffn, down[cols, :]) * slope[:, at]).astype(jnp.bfloat16)
            acc_down[:, at] += dot(gffn_t, hid[:, at])
            acc_up[:, at] += dot(low_t, gpre)
            gnormed = gnormed + dot_nt(gpre, up[:, cols])
    gfirst = norm_back(gnormed, unit, scale, g1[...])
    gfirst_ref[...] = gfirst
    gattn = (gfirst + gdual).astype(jnp.bfloat16)
    sums[0:1, :] += jnp.sum(gnormed * unit, axis=0, keepdims=True)
    sums[1:2, :] += jnp.sum(gnormed, axis=0, keepdims=True)
    sums[2:3, :] += jnp.sum(upstream * unit2, axis=0, keepdims=True)
    sums[3:4, :] += jnp.sum(upstream, axis=0, keepdims=True)
    acc_out[...] += dot_tn(heads[...], gattn)
    live = marks[:, LIVE_LANE : LIVE_LANE + 1].astype(jnp.float32)
    gheads[:, :half] = (dot_nt(gattn, out_a[...]) * live).astype(jnp.bfloat16)
    gheads[:, half:] = (dot_nt(gattn, out_b[...]) * live).astype(jnp.bfloat16)

    @pl.when(i == pl.num_programs(0) - 1)
    def _():
        depth = acc_up.shape[0]
        for n, (ffn_grad, out_grad) in enumerate(
            ((ffn_grad_a, out_grad_a), (ffn_grad_b, out_grad_b))
        ):
            ffn_grad[:ff, :] = acc_down[:, n * ff : (n + 1) * ff].T.astype(jnp.bfloat16)
            for c in range(ff // depth):
                at = n * ff + c * depth
                ffn_grad[ff + c * depth : ff + (c + 1) * depth, :] = acc_up[
                    :, at : at + depth
                ].astype(jnp.bfloat16)
            out_grad[...] = acc_out[n * half : (n + 1) * half, :].astype(jnp.bfloat16)


def layer(heads, x, dual, gn, gd, marks, outs, ups, downs, g1, b1, g2, b2, block=BLOCK):
    rows, depth = x.shape
    ff, half = ups[0].shape[1], outs[0].shape[0]
    tall = ((rows, depth), jnp.bfloat16, (block, depth), rows_of)
    tall32 = ((rows, depth), jnp.float32, (block, depth), rows_of)

    def once(*shape, dtype=jnp.bfloat16):
        return (shape, dtype, shape, lambda i: (0, 0))

    return call(
        layer_kernel, "layer", (rows // block,),
        [(a, (block, a.shape[1]), rows_of) for a in (heads, x, dual, gn, gd, marks)]
        + [*outs, *ups, *downs, g1, b1, g2, b2],
        [tall, tall, tall32, tall, once(2 * ff, depth), once(2 * ff, depth), once(half, depth), once(half, depth), once(8, depth, dtype=jnp.float32)],
        scratch=[
            pltpu.VMEM((block, 2 * ff), jnp.bfloat16),
            pltpu.VMEM((block, 2 * ff), jnp.float32),
            pltpu.VMEM((depth, 2 * ff), jnp.float32),
            pltpu.VMEM((depth, 2 * ff), jnp.float32),
            pltpu.VMEM((2 * half, depth), jnp.float32),
        ],
        flops=2 * rows * depth * (3 * depth + 12 * ff),
    )


def attend_back_kernel(
    pairs, seq, ranges, *refs,
):
    q_refs, k_refs, v_refs, g_refs, o_refs = (refs[n * pairs : (n + 1) * pairs] for n in range(5))
    (x_ref, key_marks, query_marks, lse_ref, *extra) = refs[5 * pairs : -9 if seq else -7]
    if seq:
        before, _, *extra = extra
        out_ref, own_ref, other_ref, kcat, vcat, kt, dk, dv, acc = refs[-9:]
    else:
        extra = []
        out_ref, acc, kcat, vcat, kt, dk, dv = refs[-7:]
    for p in range(pairs):
        kcat[p, :, :PAIR] = k_refs[p][...]
        kcat[p, :, PAIR:] = key_marks[...]
        vcat[p, :, :PAIR] = v_refs[p][...]
        vcat[p, :, PAIR:] = key_marks[...]
        kt[p] = k_refs[p][...].T
    dk[...] = jnp.zeros_like(dk)
    dv[...] = jnp.zeros_like(dv)

    def negated(row):
        return [part.astype(jnp.float32) for part in three_parts(-row)]

    def step(i, carry):
        at = pl.multiple_of(i * TILE, TILE)
        first = ranges[(seq * TILES + i) * 2]
        count = ranges[(seq * TILES + i) * 2 + 1]
        start = pl.multiple_of(first * TILE, TILE)

        def branch(width):
            at_keys = pl.ds(start, width * TILE)
            marks = query_marks[:LSE_ROW, pl.ds(at, TILE)].astype(jnp.float32)
            marks = jnp.concatenate([marks, marks], axis=1)
            rest = jnp.zeros((TILE - MARKS, 2 * TILE), jnp.bfloat16)
            pad = jnp.zeros((MARKS - LSE_ROW - 3, 2 * TILE), jnp.float32)
            none = jnp.zeros((LSE_ROW, 2 * TILE), jnp.float32)

            def head(p):
                query = q_refs[p][pl.ds(at, TILE), :] * jnp.bfloat16(HD**-0.5)
                grad = g_refs[p][pl.ds(at, TILE), :]
                lse = lse_ref[0, p, pl.ds(i, 1), :]
                lse_rows = jnp.concatenate([marks, *negated(lse), pad], axis=0)
                agree = grad.astype(jnp.float32) * o_refs[p][pl.ds(at, TILE), :].astype(jnp.float32)
                agree = agree.T
                delta = jnp.concatenate(
                    [
                        jnp.sum(agree[:HD], axis=0, keepdims=True),
                        jnp.sum(agree[HD:], axis=0, keepdims=True),
                    ],
                    axis=1,
                )
                delta_rows = jnp.concatenate([none, *negated(delta), pad], axis=0)
                qt = jnp.concatenate(
                    [split_rows(query.T), lse_rows.astype(jnp.bfloat16), rest], axis=0
                )
                gt = jnp.concatenate(
                    [split_rows(grad.T), delta_rows.astype(jnp.bfloat16), rest], axis=0
                )
                scores = dot(kcat[p, at_keys, :], qt)
                grad_probs = dot(vcat[p, at_keys, :], gt)
                return query, grad, scores, grad_probs

            def finish(p, query, grad, scores, grad_probs):
                probs = jnp.exp(scores)
                grad_scores = (probs * grad_probs).astype(jnp.bfloat16)
                dv[p, at_keys, :] += dot(probs.astype(jnp.bfloat16), split_lanes(grad))
                dk[p, at_keys, :] += dot(grad_scores, split_lanes(query))
                dqt = halves_of(dot(kt[p, :, at_keys], grad_scores)) * HD**-0.5
                out_ref[pl.ds(at, TILE), 3 * p * PAIR : (3 * p + 1) * PAIR] = dqt.T.astype(
                    jnp.bfloat16
                )

            ahead = head(0)
            for p in range(pairs):
                now = ahead
                if p + 1 < pairs:
                    ahead = head(p + 1)
                finish(p, *now)

        each_width(count, branch)
        return carry

    lax.fori_loop(0, TILES, step, 0)
    for p in range(pairs):
        out_ref[:, (3 * p + 1) * PAIR : (3 * p + 2) * PAIR] = dk[p].astype(jnp.bfloat16)
        out_ref[:, (3 * p + 2) * PAIR : (3 * p + 3) * PAIR] = dv[p].astype(jnp.bfloat16)

    part = dot_tn(x_ref[...], out_ref[...])
    if not seq:
        acc[...] = part
        return
    acc[...] = before[...] + part
    wide = pairs // 2 * 3
    depth = acc.shape[0]
    for n, buf in enumerate((own_ref, other_ref)):
        for m in range(wide):
            for r in range(depth // PAIR):
                buf[m * PAIR : (m + 1) * PAIR, r * PAIR : (r + 1) * PAIR] = acc[
                    r * PAIR : (r + 1) * PAIR, (n * wide + m) * PAIR : (n * wide + m + 1) * PAIR
                ].astype(jnp.bfloat16)
        used = wide * PAIR
        if extra:
            out_grad, sums = extra[n], extra[2]
            buf[used : used + out_grad.shape[0], :] = out_grad[...]
            used += out_grad.shape[0]
            both = jnp.concatenate([sums[...], jnp.zeros_like(sums)], axis=0)
            buf[used : used + MARKS, :] = both.astype(jnp.bfloat16)
            used += MARKS
        if used < buf.shape[0]:
            buf[used:, :] = jnp.zeros((buf.shape[0] - used, depth), jnp.bfloat16)


def attend_back(
    x, qkv, gheads, heads, key_marks, query_marks, lse, group, seq, before, extra, height, ranges
):
    rows, depth = x.shape
    width = heads.shape[1]
    total, pairs = width // PAIR, len(group)
    by_seq = lambda i, _: (seq, 0)
    ins = []
    for array, base in ((qkv, 0), (qkv, total), (qkv, 2 * total), (gheads, 0), (heads, 0)):
        for p in group:
            ins.append((array, (LEN, PAIR), lambda i, _, at=base + p: (seq, at)))
    ins += [
        (x, (LEN, depth), by_seq),
        (key_marks, (LEN, TILE), by_seq),
        (query_marks, (MARKS, LEN), lambda i, _: (0, seq)),
        (lse[:, jnp.asarray(group)], (1, pairs, TILES, 2 * TILE), lambda i, _: (seq, 0, 0, 0)),
    ]
    wide = 3 * pairs * PAIR
    out = ((rows, wide), jnp.bfloat16, (LEN, wide), by_seq)
    fixed = lambda i, _: (0, 0)
    buf = ((height, depth), jnp.bfloat16, (height, depth), fixed)
    sums = ((depth, wide), jnp.float32, (depth, wide), fixed)
    aliases = {}
    if seq:
        aliases = {len(ins) + 2: 0}
        ins += [before[1], (before[0], None, None), *extra]
    scratch = [
        pltpu.VMEM((pairs, LEN, PAIR + TILE), jnp.bfloat16),
        pltpu.VMEM((pairs, LEN, PAIR + TILE), jnp.bfloat16),
        pltpu.VMEM((pairs, PAIR, LEN), jnp.bfloat16),
        pltpu.VMEM((pairs, LEN, PAIR), jnp.float32),
        pltpu.VMEM((pairs, LEN, PAIR), jnp.float32),
    ]
    if seq:
        scratch.append(pltpu.VMEM((depth, wide), jnp.float32))
    return call(
        partial(attend_back_kernel, pairs, seq), "attend_back", (1,), ins,
        [out, buf, buf] if seq else [out, sums],
        scratch=scratch,
        scalars=(ranges,),
        aliases=aliases,
        flops=2 * LEN * wide * (LEN * 2 + depth),
    )


def stream_kernel(gfirst, grad_a, grad_b, *refs):
    weights, out = refs[:-1], refs[-1]
    total = gfirst[...]
    for grad, half in ((grad_a, 0), (grad_b, 1)):
        for n in range(6):
            total = total + dot_nt(
                grad[:, n * PAIR : (n + 1) * PAIR],
                weights[n][:, half * PAIR : (half + 1) * PAIR],
            )
    out[...] = total


def stream(gfirst, grad_a, grad_b, own, other):
    rows, depth = gfirst.shape
    return call(
        stream_kernel, "stream", (rows // BLOCK,),
        [(a, (BLOCK, a.shape[1]), rows_of) for a in (gfirst, grad_a, grad_b)] + [*own, *other],
        [((rows, depth), jnp.float32, (BLOCK, depth), rows_of)],
        flops=2 * rows * depth * 3 * depth,
    )[0]


def swap_cores(block):
    return lax.ppermute(block, "mp", [(0, 1), (1, 0)])


def stages_of(chips, direct):
    me, core = lax.axis_index("dp"), lax.axis_index("mp")
    low, high = me & 1, (me >> 1) & 1

    def pairs(masks):
        return [(2 * c + i, 2 * (c ^ masks[i]) + i) for c in range(chips) for i in range(2)]

    if direct:
        stages = []
        bit = 0
    else:
        stages = [
            (jnp.where(core == 0, low, high), 2, [pairs((1, 2))]),
            (jnp.where(core == 0, high, low), 2, [pairs((2, 1))]),
        ]
        bit = 2
    while 1 << bit < chips:
        radix = 4 if 1 << (bit + 1) < chips else 2
        stages.append(
            (
                (me >> bit) & (radix - 1),
                radix,
                [pairs((j << bit, j << bit)) for j in range(1, radix)],
            )
        )
        bit += radix // 2
    return stages


def send(block, pairs):
    return lax.ppermute(block, ("dp", "mp"), pairs)


def part(block, which, rows):
    return lax.dynamic_slice_in_dim(block, which * rows, rows)


def added(blocks):
    total = blocks[0].astype(jnp.float32)
    for block in blocks[1:]:
        total = total + block.astype(jnp.float32)
    return total.astype(jnp.bfloat16)


def unpack_kernel(size, shapes, places, *refs):
    pieces, outs, table = refs[: -len(shapes) - 1], refs[-len(shapes) - 1 : -1], refs[-1]
    at = 0
    for piece in pieces:
        block = piece[...].astype(jnp.float32)
        for n in range(block.shape[0] // size):
            table[pl.ds(pl.multiple_of(places[at] * size, size), size), :] = block[
                n * size : (n + 1) * size
            ]
            at += 1
    row = 0
    for out, (kind, height, width) in zip(outs, shapes):
        depth = table.shape[1]
        if kind == "rows":
            out[...] = table[row : row + height, :]
            row += height
        elif kind == "wide":
            for n in range(width // depth):
                out[:, n * depth : (n + 1) * depth] = table[row : row + height, :]
                row += height
        else:
            for n in range(height // width):
                out[n * width : (n + 1) * width, :] = table[
                    row : row + width, n * width : (n + 1) * width
                ]
            row += width


def unpack(pieces, places, shapes, rows, chips):
    depth = pieces[0].shape[1]
    size = rows // chips
    return call(
        partial(unpack_kernel, size, shapes), "unpack", (1,), pieces,
        [((h, w), jnp.float32, (h, w), lambda i, _: (0, 0)) for _, h, w in shapes],
        scratch=[pltpu.VMEM((rows, depth), jnp.float32)],
        scalars=(places,),
    )


def sum_everywhere(own, other, shapes, chips, direct):
    rows = own.shape[0]
    stages = stages_of(chips, direct)
    cores = [(2 * c + i, 2 * c + 1 - i) for c in range(chips) for i in range(2)]
    addends = [own, *(yield [(other, cores)])]
    height = rows
    for digit, radix, ways in stages:
        height //= radix
        got = yield [
            (added([part(a, digit ^ (j + 1), height) for a in addends]), pairs)
            for j, pairs in enumerate(ways)
        ]
        addends = [part(a, digit, height) for a in addends] + got
    pieces = [added(addends)]
    places = [jnp.int32(0)]
    for n, (digit, radix, ways) in enumerate(reversed(stages)):
        weight = chips
        for _, earlier, _ in stages[: len(stages) - n]:
            weight //= earlier
        held = pieces[0] if len(pieces) == 1 else jnp.concatenate(pieces)
        pieces = [held] + (yield [(held, pairs) for pairs in ways])
        places = [p + (digit ^ j) * weight for j in range(radix) for p in places]
    return unpack(pieces, jnp.stack(places).astype(jnp.int32), shapes, rows, chips)


class Chain:
    def __init__(self, steps):
        self.steps, self.result = steps, None
        self.wishes = next(steps)

    def take(self, got):
        try:
            self.wishes = self.steps.send(got)
        except StopIteration as end:
            self.wishes, self.result = [], end.value


def advance(chains, work=None, token=None):
    blocks = [block for chain in chains for block, _ in chain.wishes]
    if work is not None:
        *blocks, token = lax.optimization_barrier((*blocks, token))
    ways = [pairs for chain in chains for _, pairs in chain.wishes]
    got = [send(block, pairs) for block, pairs in zip(blocks, ways)]
    out = None
    if work is not None:
        out = work(token)
        *got, last = lax.optimization_barrier((*got, out[-1]))
        out = (*out[:-1], last)
    for chain in chains:
        if chain.wishes:
            count = len(chain.wishes)
            chain.take(got[:count])
            got = got[count:]
    return out


def on_device(
    normed_in,
    dual_in,
    query_weight,
    key_weight,
    value_weight,
    output_weight,
    first_gain,
    first_bias,
    up_weight,
    down_weight,
    second_gain,
    second_bias,
    segments,
    grad_normed_out,
    grad_dual_out,
    chips,
):
    rows, depth = normed_in.shape
    core = lax.axis_index("mp")
    half, ff = query_weight.shape[1], up_weight.shape[1]
    own = (query_weight, key_weight, value_weight)
    other = tuple(swap_cores(w) for w in own)
    outs = (output_weight, swap_cores(output_weight))
    ups = (up_weight, swap_cores(up_weight))
    downs = (down_weight, swap_cores(down_weight))
    labels = lax.dynamic_slice(segments, (core * rows,), (rows,))
    key_marks, query_marks = label_marks(labels)
    ranges = key_ranges(labels)
    qkv = project(normed_in, own, other)
    heads_out, log_totals = attend(ranges, qkv, key_marks, query_marks)
    row = lambda v: v.reshape(1, depth)
    (normed_out, dual_out, grad_first, grad_heads, ffn_own, ffn_other, out_own, out_other, sums) = (
        layer(
            heads_out, normed_in, dual_in, grad_normed_out, grad_dual_out, key_marks, outs, ups,
            downs, row(first_gain), row(first_bias), row(second_gain), row(second_bias),
        )
    )
    grain = 8 * chips

    def padded(count):
        return -(-count // grain) * grain

    back = partial(
        attend_back, normed_in, qkv, grad_heads, heads_out, key_marks, query_marks, log_totals
    )
    tall = 3 * PAIR
    height_a, height_b = padded(tall + half + MARKS), padded(tall)
    narrow = [("blocks", depth, PAIR)] * 3
    fed = Chain(
        sum_everywhere(
            ffn_own, ffn_other, [("rows", ff, depth), ("wide", depth, ff)], chips, False
        )
    )
    token = ranges
    before = advance([fed], partial(back, (0, 2), 0, None, (), height_a), token)
    grad_a, own_a, other_a = advance(
        [fed], partial(back, (0, 2), 1, before, (out_own, out_other, sums), height_a), token
    )
    some = Chain(
        sum_everywhere(
            own_a, other_a, narrow + [("rows", half, depth), ("rows", 8, depth)], chips, True
        )
    )
    before = advance([fed, some], partial(back, (1, 3), 0, None, (), height_b), token)
    grad_b, own_b, other_b = advance(
        [fed, some], partial(back, (1, 3), 1, before, (), height_b), token
    )
    rest = Chain(sum_everywhere(own_b, other_b, narrow, chips, True))
    chains = [fed, some, rest]
    (grad_stream,) = advance(
        chains, lambda grad: (stream(grad, grad_a, grad_b, own, other),), grad_first
    )
    while any(chain.wishes for chain in chains):
        advance(chains)
    down_total, up_total = fed.result
    query_a, key_a, value_a, output_total, small = some.result
    query_b, key_b, value_b = rest.result
    return (
        normed_out,
        dual_out,
        grad_stream,
        jnp.concatenate([query_a, query_b], axis=1),
        jnp.concatenate([key_a, key_b], axis=1),
        jnp.concatenate([value_a, value_b], axis=1),
        output_total,
        small[0],
        small[1],
        up_total,
        down_total,
        small[2],
        small[3],
    )


def solution(mesh):
    rows = P(("dp", "mp"), None)
    columns = P(None, "mp")
    return jax.shard_map(
        partial(on_device, chips=mesh.shape["dp"]),
        mesh=mesh,
        in_specs=(
            rows, rows, columns, columns, columns, P("mp", None), P(), P(),
            columns, P("mp", None), P(), P(), P("dp"), rows, rows,
        ),
        out_specs=(
            rows, rows, rows, columns, columns, columns, P("mp", None), P(), P(),
            columns, P("mp", None), P(), P(),
        ),
        check_vma=False,
    )
```

```python
import math
from functools import partial

import jax
import jax.numpy as jnp
from jax import lax
from jax.experimental import pallas as pl
from jax.experimental.pallas import tpu as pltpu
from jax.sharding import PartitionSpec as P

norm_eps = 1e-05
BLOCK = 512
GATE = 0.7978845608028654
CUBE = 0.044715
HD = 64
LEN = 1024
TILE = 128
TILES = LEN // TILE
PAIR = 2 * HD
FAR = -1e30
MARKS = 16
LSE_ROW = 8
LIVE_LANE = 12
MIB = 2**20


def dot(left, right):
    return jnp.dot(left, right, preferred_element_type=jnp.float32)


def three_parts(row):
    high = row.astype(jnp.bfloat16)
    rest = row - high.astype(jnp.float32)
    mid = rest.astype(jnp.bfloat16)
    low = (rest - mid.astype(jnp.float32)).astype(jnp.bfloat16)
    return high, mid, low


def label_marks(labels):
    lane = jnp.arange(TILE)
    key_marks = jnp.where(
        lane < LSE_ROW,
        jnp.where(labels[:, None] == lane, 0.0, FAR),
        jnp.where(
            (lane < LSE_ROW + 3) | ((lane == LIVE_LANE) & (labels[:, None] != 0)), 1.0, 0.0
        ),
    ).astype(jnp.bfloat16)
    row = jnp.arange(MARKS)[:, None]
    query_marks = ((labels[None, :] == row) & (row < LSE_ROW)).astype(jnp.bfloat16)
    return key_marks, query_marks


def key_ranges(labels):
    seqs = labels.shape[0] // LEN
    table = labels.reshape(seqs, 1, LEN)
    ends = labels.reshape(seqs, TILES, TILE)
    where = jnp.arange(LEN, dtype=jnp.int32)
    first = jnp.min(jnp.where(table == ends[:, :, :1], where, LEN), axis=-1) // TILE
    last = jnp.max(jnp.where(table == ends[:, :, -1:], where, -1), axis=-1) // TILE
    return jnp.stack([first, last - first + 1], axis=-1).astype(jnp.int32).reshape(-1)


def halves_of(block):
    return jnp.concatenate([block[:HD, :TILE], block[HD:, TILE:]], axis=0)


def split_rows(tile_t):
    zero = jnp.zeros((HD, TILE), tile_t.dtype)
    return jnp.concatenate(
        [
            jnp.concatenate([tile_t[:HD], zero], axis=1),
            jnp.concatenate([zero, tile_t[HD:]], axis=1),
        ],
        axis=0,
    )


def split_lanes(tile):
    lane = lax.broadcasted_iota(jnp.int32, tile.shape, 1)
    zero = jnp.zeros_like(tile)
    return jnp.concatenate(
        [jnp.where(lane < HD, tile, zero), jnp.where(lane < HD, zero, tile)], axis=0
    )


def each_width(count, branch):
    for width in range(1, TILES + 1):
        pl.when(count == width)(partial(branch, width))


def dot_nt(left, right):
    return lax.dot_general(
        left, right, (((1,), (1,)), ((), ())), preferred_element_type=jnp.float32
    )


def dot_tn(left, right):
    return lax.dot_general(
        left, right, (((0,), (0,)), ((), ())), preferred_element_type=jnp.float32
    )


def full(ref):
    shape = ref.shape
    return pl.BlockSpec(shape, lambda *_: (0,) * len(shape), pipeline_mode=pl.Buffered(1))


def call(kernel, name, grid, ins, outs, scratch=(), scalars=(), flops=0, aliases=None):
    specs, arrays = [], []
    for item in ins:
        if isinstance(item, tuple):
            arrays.append(item[0])
            if item[1] is None:
                specs.append(pl.BlockSpec(memory_space=pl.ANY))
            else:
                specs.append(pl.BlockSpec(item[1], item[2]))
        else:
            arrays.append(item)
            specs.append(full(item))
    size = sum(a.size * a.dtype.itemsize for a in arrays)
    size += sum(jnp.dtype(d).itemsize * math.prod(s) for s, d, _, _ in outs)
    return pl.pallas_call(
        kernel,
        grid_spec=pltpu.PrefetchScalarGridSpec(
            num_scalar_prefetch=len(scalars),
            grid=grid,
            in_specs=specs,
            out_specs=[pl.BlockSpec(b, m) for _, _, b, m in outs],
            scratch_shapes=scratch,
        ),
        out_shape=[jax.ShapeDtypeStruct(s, d) for s, d, _, _ in outs],
        compiler_params=pltpu.CompilerParams(vmem_limit_bytes=56 * MIB),
        cost_estimate=pl.CostEstimate(flops=flops, bytes_accessed=size, transcendentals=0),
        input_output_aliases=aliases or {},
        name=name,
    )(*scalars, *arrays)


def rows_of(i, *_):
    return (i, 0)


def stats(z):
    mean = jnp.mean(z, axis=-1, keepdims=True)
    centred = z - mean
    spread = jnp.mean(centred * centred, axis=-1, keepdims=True)
    scale = lax.rsqrt(spread + norm_eps)
    return centred * scale, scale


def norm_back(upstream, unit, scale, gain):
    t = upstream * gain
    inner = jnp.mean(t * unit, axis=-1, keepdims=True)
    return (t - jnp.mean(t, axis=-1, keepdims=True) - unit * inner) * scale


def layer_kernel(
    heads, x, dual, gn, gd, marks, out_a, out_b, up_a, up_b, down_a, down_b, g1, b1, g2, b2,
    normed_out, dual_out, gfirst_ref, gheads, ffn_grad_a, ffn_grad_b, out_grad_a, out_grad_b, sums,
    hid, slope, acc_up, acc_down, acc_out,
):
    i = pl.program_id(0)
    half = out_a.shape[0]
    ff = up_a.shape[1]
    chunk = 512

    @pl.when(i == 0)
    def _():
        sums[...] = jnp.zeros_like(sums)
        acc_up[...] = jnp.zeros_like(acc_up)
        acc_down[...] = jnp.zeros_like(acc_down)
        acc_out[...] = jnp.zeros_like(acc_out)

    attn = dot(heads[:, :half], out_a[...]) + dot(heads[:, half:], out_b[...])
    z1 = x[...].astype(jnp.float32) + attn
    unit, scale = stats(z1)
    normed = unit * g1[...] + b1[...]
    low = normed.astype(jnp.bfloat16)
    ffn = None
    for n, (up, down) in enumerate(((up_a, down_a), (up_b, down_b))):
        for c in range(ff // chunk):
            cols = slice(c * chunk, (c + 1) * chunk)
            at = slice(n * ff + c * chunk, n * ff + (c + 1) * chunk)
            v = dot(low, up[:, cols])
            square = v * v
            t = jnp.tanh(v * (GATE + (GATE * CUBE) * square))
            open_part = 0.5 + 0.5 * t
            hidden = (v * open_part).astype(jnp.bfloat16)
            hid[:, at] = hidden
            slope[:, at] = open_part + (v * (0.5 - 0.5 * t * t)) * (
                GATE + (3 * GATE * CUBE) * square
            )
            part = dot(hidden, down[cols, :])
            ffn = part if ffn is None else ffn + part
    unit2, scale2 = stats(normed + ffn)
    normed_out[...] = (unit2 * g2[...] + b2[...]).astype(jnp.bfloat16)
    dual_out[...] = (dual[...].astype(jnp.float32) + attn + ffn).astype(jnp.bfloat16)
    upstream = gn[...].astype(jnp.float32)
    gmid = norm_back(upstream, unit2, scale2, g2[...])
    gdual = gd[...].astype(jnp.float32)
    gffn = (gmid + gdual).astype(jnp.bfloat16)
    gffn_t = gffn.T
    low_t = low.T
    gnormed = gmid
    for n, (up, down) in enumerate(((up_a, down_a), (up_b, down_b))):
        for c in range(ff // chunk):
            cols = slice(c * chunk, (c + 1) * chunk)
            at = slice(n * ff + c * chunk, n * ff + (c + 1) * chunk)
            gpre = (dot_nt(gffn, down[cols, :]) * slope[:, at]).astype(jnp.bfloat16)
            acc_down[:, at] += dot(gffn_t, hid[:, at])
            acc_up[:, at] += dot(low_t, gpre)
            gnormed = gnormed + dot_nt(gpre, up[:, cols])
    gfirst = norm_back(gnormed, unit, scale, g1[...])
    gfirst_ref[...] = gfirst
    gattn = (gfirst + gdual).astype(jnp.bfloat16)
    sums[0:1, :] += jnp.sum(gnormed * unit, axis=0, keepdims=True)
    sums[1:2, :] += jnp.sum(gnormed, axis=0, keepdims=True)
    sums[2:3, :] += jnp.sum(upstream * unit2, axis=0, keepdims=True)
    sums[3:4, :] += jnp.sum(upstream, axis=0, keepdims=True)
    acc_out[...] += dot_tn(heads[...], gattn)
    live = marks[:, LIVE_LANE : LIVE_LANE + 1].astype(jnp.float32)
    gheads[:, :half] = (dot_nt(gattn, out_a[...]) * live).astype(jnp.bfloat16)
    gheads[:, half:] = (dot_nt(gattn, out_b[...]) * live).astype(jnp.bfloat16)

    @pl.when(i == pl.num_programs(0) - 1)
    def _():
        depth = acc_up.shape[0]
        for n, (ffn_grad, out_grad) in enumerate(
            ((ffn_grad_a, out_grad_a), (ffn_grad_b, out_grad_b))
        ):
            ffn_grad[:ff, :] = acc_down[:, n * ff : (n + 1) * ff].T.astype(jnp.bfloat16)
            for c in range(ff // depth):
                at = n * ff + c * depth
                ffn_grad[ff + c * depth : ff + (c + 1) * depth, :] = acc_up[
                    :, at : at + depth
                ].astype(jnp.bfloat16)
            out_grad[...] = acc_out[n * half : (n + 1) * half, :].astype(jnp.bfloat16)


def layer(heads, x, dual, gn, gd, marks, outs, ups, downs, g1, b1, g2, b2, block=BLOCK):
    rows, depth = x.shape
    ff, half = ups[0].shape[1], outs[0].shape[0]
    tall = ((rows, depth), jnp.bfloat16, (block, depth), rows_of)
    tall32 = ((rows, depth), jnp.float32, (block, depth), rows_of)

    def once(*shape, dtype=jnp.bfloat16):
        return (shape, dtype, shape, lambda i: (0, 0))

    return call(
        layer_kernel, "layer", (rows // block,),
        [(a, (block, a.shape[1]), rows_of) for a in (heads, x, dual, gn, gd, marks)]
        + [*outs, *ups, *downs, g1, b1, g2, b2],
        [tall, tall, tall32, tall, once(2 * ff, depth), once(2 * ff, depth), once(half, depth), once(half, depth), once(8, depth, dtype=jnp.float32)],
        scratch=[
            pltpu.VMEM((block, 2 * ff), jnp.bfloat16),
            pltpu.VMEM((block, 2 * ff), jnp.float32),
            pltpu.VMEM((depth, 2 * ff), jnp.float32),
            pltpu.VMEM((depth, 2 * ff), jnp.float32),
            pltpu.VMEM((2 * half, depth), jnp.float32),
        ],
        flops=2 * rows * depth * (3 * depth + 12 * ff),
    )


def fill_block(table, p, i, tile_t):
    table[p, i, :HD, :TILE] = tile_t[:HD]
    table[p, i, HD:PAIR, TILE:] = tile_t[HD:]


def attend_kernel(
    ranges, x_ref, qa, ka, va, qb, kb, vb, key_marks, query_marks,
    qkv_ref, out_ref, lse_ref, kcat, vt, qt, mixed_t,
):
    seq = pl.program_id(0)
    half = qa.shape[1]
    width = 2 * half
    pairs = width // PAIR
    x = x_ref[...]

    @pl.when(seq == 0)
    def _():
        qt[...] = jnp.zeros_like(qt)

    for n, w in enumerate((qa, qb, ka, kb, va, vb)):
        qkv_ref[:, n * half : (n + 1) * half] = dot(x, w[...]).astype(jnp.bfloat16)
    for p in range(pairs):
        lanes = slice(p * PAIR, (p + 1) * PAIR)
        kcat[p, :, :PAIR] = qkv_ref[:, width + p * PAIR : width + (p + 1) * PAIR]
        kcat[p, :, PAIR:] = key_marks[...]
        vt[lanes, :] = qkv_ref[:, 2 * width + p * PAIR : 2 * width + (p + 1) * PAIR].T
        for i in range(TILES):
            cols = slice(i * TILE, (i + 1) * TILE)
            fill_block(qt, p, i, (qkv_ref[cols, lanes] * jnp.bfloat16(HD**-0.5)).T)
            qt[p, i, PAIR : PAIR + MARKS, :TILE] = query_marks[:, cols]
            qt[p, i, PAIR : PAIR + MARKS, TILE:] = query_marks[:, cols]

    def step(i, carry):
        at = pl.multiple_of(i * TILE, TILE)
        first = ranges[(seq * TILES + i) * 2]
        count = ranges[(seq * TILES + i) * 2 + 1]
        start = pl.multiple_of(first * TILE, TILE)

        def branch(width):
            at_keys = pl.ds(start, width * TILE)

            def scores_of(p):
                return dot(kcat[p, at_keys, :], qt[p, i])

            def finish(p, scores):
                top = jnp.max(scores, axis=0, keepdims=True)
                probs = jnp.exp(scores - top)
                total = jnp.sum(probs, axis=0, keepdims=True)
                mixed = dot(vt[p * PAIR : (p + 1) * PAIR, at_keys], probs.astype(jnp.bfloat16))
                mixed_t[p * PAIR : (p + 1) * PAIR, pl.ds(at, TILE)] = halves_of(mixed / total)
                lse_ref[0, p, pl.ds(i, 1), :] = top + jnp.log(total)

            ahead = scores_of(0)
            for p in range(pairs):
                scores = ahead
                if p + 1 < pairs:
                    ahead = scores_of(p + 1)
                finish(p, scores)

        each_width(count, branch)
        return carry

    lax.fori_loop(0, TILES, step, 0)
    live = 1.0 - query_marks[:1, :].astype(jnp.float32)
    for p in range(pairs):
        lanes = slice(p * PAIR, (p + 1) * PAIR)
        out_ref[:, lanes] = (mixed_t[lanes, :] * live).astype(jnp.bfloat16).T


def attend(ranges, x, own, other, key_marks, query_marks):
    rows, depth = x.shape
    half = own[0].shape[1]
    width = 2 * half
    seqs, pairs = rows // LEN, width // PAIR
    return call(
        attend_kernel, "attend", (seqs,),
        [
            (x, (LEN, depth), lambda s, _: (s, 0)),
            *own,
            *other,
            (key_marks, (LEN, TILE), lambda s, _: (s, 0)),
            (query_marks, (MARKS, LEN), lambda s, _: (0, s)),
        ],
        [
            ((rows, 3 * width), jnp.bfloat16, (LEN, 3 * width), lambda s, _: (s, 0)),
            ((rows, width), jnp.bfloat16, (LEN, width), lambda s, _: (s, 0)),
            (
                (seqs, pairs, TILES, 2 * TILE), jnp.float32, (1, pairs, TILES, 2 * TILE),
                lambda s, _: (s, 0, 0, 0),
            ),
        ],
        scratch=[
            pltpu.VMEM((pairs, LEN, PAIR + TILE), jnp.bfloat16),
            pltpu.VMEM((width, LEN), jnp.bfloat16),
            pltpu.VMEM((pairs, TILES, PAIR + TILE, 2 * TILE), jnp.bfloat16),
            pltpu.VMEM((width, LEN), jnp.float32),
        ],
        scalars=(ranges,),
        flops=2 * rows * (3 * width * depth + 2 * width * LEN),
    )


def attend_back_kernel(seq, ranges, *refs):
    q_ref, k_ref, v_ref, g_ref, o_ref, key_marks, query_marks, lse_ref = refs[:8]
    out_ref, kcat, vcat, kt, qt, gt, dk, dv, dqt = refs[-9:]
    width = q_ref.shape[1]
    pairs = width // PAIR
    groups = pairs // 2

    def place(p, what):
        at = (((p % groups) * 2 + p // groups) * 3 + what) * PAIR
        return slice(at, at + PAIR)

    def negated(row):
        return [part.astype(jnp.float32) for part in three_parts(-row)]

    qt[...] = jnp.zeros_like(qt)
    gt[...] = jnp.zeros_like(gt)
    dk[...] = jnp.zeros_like(dk)
    dv[...] = jnp.zeros_like(dv)
    pad = jnp.zeros((MARKS - LSE_ROW - 3, 2 * TILE), jnp.float32)
    none = jnp.zeros((LSE_ROW, 2 * TILE), jnp.float32)
    for p in range(pairs):
        lanes = slice(p * PAIR, (p + 1) * PAIR)
        kcat[p, :, :PAIR] = k_ref[:, lanes]
        kcat[p, :, PAIR:] = key_marks[...]
        vcat[p, :, :PAIR] = v_ref[:, lanes]
        vcat[p, :, PAIR:] = key_marks[...]
        kt[lanes, :] = k_ref[:, lanes].T
        for i in range(TILES):
            cols = slice(i * TILE, (i + 1) * TILE)
            fill_block(qt, p, i, (q_ref[cols, lanes] * jnp.bfloat16(HD**-0.5)).T)
            grad_t = g_ref[cols, lanes].T
            fill_block(gt, p, i, grad_t)
            agree = grad_t.astype(jnp.float32) * o_ref[cols, lanes].T.astype(jnp.float32)
            delta = jnp.concatenate(
                [
                    jnp.sum(agree[:HD], axis=0, keepdims=True),
                    jnp.sum(agree[HD:], axis=0, keepdims=True),
                ],
                axis=1,
            )
            marks = query_marks[:LSE_ROW, cols].astype(jnp.float32)
            marks = jnp.concatenate([marks, marks], axis=1)
            lse = lse_ref[0, p, i : i + 1, :]
            qt[p, i, PAIR : PAIR + MARKS, :] = jnp.concatenate(
                [marks, *negated(lse), pad], axis=0
            ).astype(jnp.bfloat16)
            gt[p, i, PAIR : PAIR + MARKS, :] = jnp.concatenate(
                [none, *negated(delta), pad], axis=0
            ).astype(jnp.bfloat16)

    def step(i, carry):
        at = pl.multiple_of(i * TILE, TILE)
        first = ranges[(seq * TILES + i) * 2]
        count = ranges[(seq * TILES + i) * 2 + 1]
        start = pl.multiple_of(first * TILE, TILE)

        def branch(width):
            at_keys = pl.ds(start, width * TILE)

            def head(p):
                scores = dot(kcat[p, at_keys, :], qt[p, i])
                grad_probs = dot(vcat[p, at_keys, :], gt[p, i])
                return scores, grad_probs

            def finish(p, scores, grad_probs):
                lanes = slice(p * PAIR, (p + 1) * PAIR)
                query = q_ref[pl.ds(at, TILE), lanes] * jnp.bfloat16(HD**-0.5)
                grad = g_ref[pl.ds(at, TILE), lanes]
                probs = jnp.exp(scores)
                grad_scores = (probs * grad_probs).astype(jnp.bfloat16)
                dv[p, at_keys, :] += dot(probs.astype(jnp.bfloat16), split_lanes(grad))
                dk[p, at_keys, :] += dot(grad_scores, split_lanes(query))
                dqt[lanes, pl.ds(at, TILE)] = halves_of(dot(kt[lanes, at_keys], grad_scores))

            ahead = head(0)
            for p in range(pairs):
                now = ahead
                if p + 1 < pairs:
                    ahead = head(p + 1)
                finish(p, *now)

        each_width(count, branch)
        return carry

    lax.fori_loop(0, TILES, step, 0)
    for p in range(pairs):
        lanes = slice(p * PAIR, (p + 1) * PAIR)
        out_ref[:, place(p, 0)] = (dqt[lanes, :] * HD**-0.5).astype(jnp.bfloat16).T
        out_ref[:, place(p, 1)] = dk[p].astype(jnp.bfloat16)
        out_ref[:, place(p, 2)] = dv[p].astype(jnp.bfloat16)


def attend_back(qkv, gheads, heads, key_marks, query_marks, lse, seq, before, ranges):
    rows, width = heads.shape
    seqs, pairs = rows // LEN, width // PAIR
    by_seq = lambda i, _: (seq, 0)
    ins = [
        (qkv, (LEN, width), by_seq),
        (qkv, (LEN, width), lambda i, _: (seq, 1)),
        (qkv, (LEN, width), lambda i, _: (seq, 2)),
        (gheads, (LEN, width), by_seq),
        (heads, (LEN, width), by_seq),
        (key_marks, (LEN, TILE), by_seq),
        (query_marks, (MARKS, LEN), lambda i, _: (0, seq)),
        (lse, (1, pairs, TILES, 2 * TILE), lambda i, _: (seq, 0, 0, 0)),
    ]
    aliases = {}
    if before is not None:
        aliases[len(ins) + 1] = 0
        ins.append((before, None, None))
    return call(
        partial(attend_back_kernel, seq), "attend_back", (1,), ins,
        [((rows, 3 * width), jnp.bfloat16, (LEN, 3 * width), by_seq)],
        scratch=[
            pltpu.VMEM((pairs, LEN, PAIR + TILE), jnp.bfloat16),
            pltpu.VMEM((pairs, LEN, PAIR + TILE), jnp.bfloat16),
            pltpu.VMEM((width, LEN), jnp.bfloat16),
            pltpu.VMEM((pairs, TILES, PAIR + TILE, 2 * TILE), jnp.bfloat16),
            pltpu.VMEM((pairs, TILES, PAIR + TILE, 2 * TILE), jnp.bfloat16),
            pltpu.VMEM((pairs, LEN, PAIR), jnp.float32),
            pltpu.VMEM((pairs, LEN, PAIR), jnp.float32),
            pltpu.VMEM((width, LEN), jnp.float32),
        ],
        scalars=(ranges,),
        aliases=aliases,
        flops=10 * LEN * width * LEN,
    )


def project_back_kernel(x_ref, grad, out_a, out_b, sums, own_ref, other_ref, acc):
    part = dot_tn(x_ref[...], grad[...])

    @pl.when(pl.program_id(0) == 0)
    def _():
        acc[...] = part

    @pl.when(pl.program_id(0) != 0)
    def _():
        acc[...] += part

    @pl.when(pl.program_id(0) == pl.num_programs(0) - 1)
    def _():
        depth = acc.shape[0]
        wide = acc.shape[1] // 2
        for n, (buf, out_grad) in enumerate(((own_ref, out_a), (other_ref, out_b))):
            for m in range(wide // PAIR):
                at = ((m // 3 * 2 + n) * 3 + m % 3) * PAIR
                for r in range(depth // PAIR):
                    buf[m * PAIR : (m + 1) * PAIR, r * PAIR : (r + 1) * PAIR] = acc[
                        r * PAIR : (r + 1) * PAIR, at : at + PAIR
                    ].astype(jnp.bfloat16)
            end = wide + out_grad.shape[0]
            buf[wide:end, :] = out_grad[...]
            both = jnp.concatenate([sums[...], jnp.zeros_like(sums)], axis=0)
            buf[end : end + MARKS, :] = both.astype(jnp.bfloat16)
            if end + MARKS < buf.shape[0]:
                buf[end + MARKS :, :] = jnp.zeros(
                    (buf.shape[0] - end - MARKS, depth), jnp.bfloat16
                )


def project_back(x, grad, out_a, out_b, sums, height):
    rows, depth = x.shape
    wide = grad.shape[1]
    buf = ((height, depth), jnp.bfloat16, (height, depth), lambda i: (0, 0))
    return call(
        project_back_kernel, "project_back", (rows // BLOCK,),
        [(x, (BLOCK, depth), rows_of), (grad, (BLOCK, wide), rows_of), out_a, out_b, sums],
        [buf, buf],
        scratch=[pltpu.VMEM((depth, wide), jnp.float32)],
        flops=2 * rows * depth * wide,
    )


def stream_kernel(gfirst, grad, *refs):
    weights, out, table = refs[:-2], refs[-2], refs[-1]

    @pl.when(pl.program_id(0) == 0)
    def _():
        count = len(weights)
        for n, weight in enumerate(weights):
            for g in range(weight.shape[1] // PAIR):
                at = (g * count + n) * PAIR
                table[:, at : at + PAIR] = weight[:, g * PAIR : (g + 1) * PAIR]

    out[...] = gfirst[...] + dot_nt(grad[...], table[...])


def stream(gfirst, grad, own, other):
    rows, depth = gfirst.shape
    wide = grad.shape[1]
    return call(
        stream_kernel, "stream", (rows // BLOCK,),
        [(a, (BLOCK, a.shape[1]), rows_of) for a in (gfirst, grad)] + [*own, *other],
        [((rows, depth), jnp.float32, (BLOCK, depth), rows_of)],
        scratch=[pltpu.VMEM((depth, wide), jnp.bfloat16)],
        flops=2 * rows * depth * wide,
    )[0]


def swap_cores(block):
    return lax.ppermute(block, "mp", [(0, 1), (1, 0)])


def stages_of(chips, radices):
    me, core = lax.axis_index("dp"), lax.axis_index("mp")

    def pairs(masks):
        return [(2 * c + i, 2 * (c ^ masks[i]) + i) for c in range(chips) for i in range(2)]

    stages = []
    bit = 0
    if radices[:2] == (2, 2):
        low, high = me & 1, (me >> 1) & 1
        stages = [
            (jnp.where(core == 0, low, high), 2, [pairs((1, 2))]),
            (jnp.where(core == 0, high, low), 2, [pairs((2, 1))]),
        ]
        bit = 2
        radices = radices[2:]
    while 1 << bit < chips:
        radix = min(radices[0], chips >> bit)
        radices = radices[1:] or radices
        ways = [pairs((j << bit, j << bit)) for j in range(1, radix)]
        stages.append(((me >> bit) & (radix - 1), radix, ways))
        bit += radix // 2
    return stages


def send(block, pairs):
    return lax.ppermute(block, ("dp", "mp"), pairs)


def part(block, which, rows):
    return lax.dynamic_slice_in_dim(block, which * rows, rows)


def added(blocks):
    total = blocks[0].astype(jnp.float32)
    for block in blocks[1:]:
        total = total + block.astype(jnp.float32)
    return total.astype(jnp.bfloat16)


def unpack_kernel(size, shapes, places, *refs):
    pieces, outs, table = refs[: -len(shapes) - 1], refs[-len(shapes) - 1 : -1], refs[-1]
    at = 0
    for piece in pieces:
        block = piece[...].astype(jnp.float32)
        for n in range(block.shape[0] // size):
            table[pl.ds(pl.multiple_of(places[at] * size, size), size), :] = block[
                n * size : (n + 1) * size
            ]
            at += 1
    row = 0
    depth = table.shape[1]
    for out, (kind, height, width) in zip(outs, shapes):
        if kind == "rows":
            out[...] = table[row : row + height, :]
            row += height
        elif kind == "wide":
            for n in range(width // depth):
                out[:, n * depth : (n + 1) * depth] = table[row : row + height, :]
                row += height
        else:
            base, count = kind
            for g in range(width // PAIR):
                at = (g * count + base) * PAIR
                for n in range(height // PAIR):
                    out[n * PAIR : (n + 1) * PAIR, g * PAIR : (g + 1) * PAIR] = table[
                        at : at + PAIR, n * PAIR : (n + 1) * PAIR
                    ]
                row += PAIR


def unpack(pieces, places, shapes, rows, chips):
    depth = pieces[0].shape[1]
    size = rows // chips
    return call(
        partial(unpack_kernel, size, shapes), "unpack", (1,), pieces,
        [((h, w), jnp.float32, (h, w), lambda i, _: (0, 0)) for _, h, w in shapes],
        scratch=[pltpu.VMEM((rows, depth), jnp.float32)],
        scalars=(places,),
    )


def sum_everywhere(own, other, shapes, chips, radices):
    rows = own.shape[0]
    stages = stages_of(chips, radices)
    cores = [(2 * c + i, 2 * c + 1 - i) for c in range(chips) for i in range(2)]
    addends = [own, *(yield [(other, cores)])]
    height = rows
    for digit, radix, ways in stages:
        height //= radix
        got = yield [
            (added([part(a, digit ^ (j + 1), height) for a in addends]), pairs)
            for j, pairs in enumerate(ways)
        ]
        addends = [part(a, digit, height) for a in addends] + got
    pieces = [added(addends)]
    places = [jnp.int32(0)]
    for n, (digit, radix, ways) in enumerate(reversed(stages)):
        weight = chips
        for _, earlier, _ in stages[: len(stages) - n]:
            weight //= earlier
        held = pieces[0] if len(pieces) == 1 else jnp.concatenate(pieces)
        pieces = [held] + (yield [(held, pairs) for pairs in ways])
        places = [p + (digit ^ j) * weight for j in range(radix) for p in places]
    return unpack(pieces, jnp.stack(places).astype(jnp.int32), shapes, rows, chips)


class Chain:
    def __init__(self, steps):
        self.steps, self.result = steps, None
        self.wishes = next(steps)

    def take(self, got):
        try:
            self.wishes = self.steps.send(got)
        except StopIteration as end:
            self.wishes, self.result = [], end.value


def advance(chains, work=None, token=None, beside=()):
    blocks = [block for chain in chains for block, _ in chain.wishes]
    if work is not None:
        *blocks, token = lax.optimization_barrier((*blocks, token))
    else:
        blocks = lax.optimization_barrier(blocks)
    ways = [pairs for chain in chains for _, pairs in chain.wishes]
    got = [send(block, pairs) for block, pairs in zip(blocks, ways)]
    out = None
    if work is not None:
        out = work(token)
        *got, last = lax.optimization_barrier((*got, out[-1]))
        out = (*out[:-1], last)
    elif beside:
        *got, _ = lax.optimization_barrier((*got, *beside))[: len(got) + 1]
    for chain in chains:
        if chain.wishes:
            count = len(chain.wishes)
            chain.take(got[:count])
            got = got[count:]
    return out


def on_device(
    normed_in,
    dual_in,
    query_weight,
    key_weight,
    value_weight,
    output_weight,
    first_gain,
    first_bias,
    up_weight,
    down_weight,
    second_gain,
    second_bias,
    segments,
    grad_normed_out,
    grad_dual_out,
    chips,
):
    rows, depth = normed_in.shape
    core = lax.axis_index("mp")
    half, ff = query_weight.shape[1], up_weight.shape[1]
    own = (query_weight, key_weight, value_weight)
    other = tuple(swap_cores(w) for w in own)
    outs = (output_weight, swap_cores(output_weight))
    ups = (up_weight, swap_cores(up_weight))
    downs = (down_weight, swap_cores(down_weight))
    labels = lax.dynamic_slice(segments, (core * rows,), (rows,))
    key_marks, query_marks = label_marks(labels)
    ranges = key_ranges(labels)
    qkv, heads_out, log_totals = attend(ranges, normed_in, own, other, key_marks, query_marks)
    row = lambda v: v.reshape(1, depth)
    (normed_out, dual_out, grad_first, grad_heads, ffn_own, ffn_other, out_own, out_other, sums) = (
        layer(
            heads_out, normed_in, dual_in, grad_normed_out, grad_dual_out, key_marks, outs, ups,
            downs, row(first_gain), row(first_bias), row(second_gain), row(second_bias),
        )
    )
    grain = 8 * chips

    def padded(count):
        return -(-count // grain) * grain

    height = padded(3 * half + half + MARKS)
    back = partial(
        attend_back, qkv, grad_heads, heads_out, key_marks, query_marks, log_totals
    )
    fed = Chain(
        sum_everywhere(
            ffn_own, ffn_other, [("rows", ff, depth), ("wide", depth, ff)], chips, (2, 2, 4)
        )
    )
    grad_qkv = None
    for seq in range(rows // LEN):
        (grad_qkv,) = advance([fed], partial(back, seq, grad_qkv), ranges)
    own_grads, other_grads = advance(
        [fed],
        lambda total: project_back(normed_in, grad_qkv, out_own, out_other, total, height),
        sums,
    )
    rest = Chain(
        sum_everywhere(
            own_grads, other_grads,
            [((n, 3), depth, half) for n in range(3)] + [("rows", half, depth), ("rows", 8, depth)],
            chips, (4,),
        )
    )
    chains = [fed, rest]
    (grad_stream,) = advance(
        chains, lambda grad: (stream(grad, grad_qkv, own, other),), grad_first
    )
    while any(chain.wishes for chain in chains):
        advance(chains, beside=() if fed.result is None else fed.result)
    down_total, up_total = fed.result
    query_total, key_total, value_total, output_total, small = rest.result
    return (
        normed_out,
        dual_out,
        grad_stream,
        query_total,
        key_total,
        value_total,
        output_total,
        small[0],
        small[1],
        up_total,
        down_total,
        small[2],
        small[3],
    )


def solution(mesh):
    rows = P(("dp", "mp"), None)
    columns = P(None, "mp")
    return jax.shard_map(
        partial(on_device, chips=mesh.shape["dp"]),
        mesh=mesh,
        in_specs=(
            rows, rows, columns, columns, columns, P("mp", None), P(), P(),
            columns, P("mp", None), P(), P(), P("dp"), rows, rows,
        ),
        out_specs=(
            rows, rows, rows, columns, columns, columns, P("mp", None), P(), P(),
            columns, P("mp", None), P(), P(),
        ),
        check_vma=False,
    )
```

```python
import math
from functools import partial

import jax
import jax.numpy as jnp
from jax import lax
from jax.experimental import pallas as pl
from jax.experimental.pallas import tpu as pltpu
from jax.sharding import PartitionSpec as P

norm_eps = 1e-05
BLOCK = 512
GATE = 0.7978845608028654
CUBE = 0.044715
SAFE = 3600.0
VM_ATT, VM_LAYER, VM_BACK, VM_PROJ, VM_STREAM, VM_UNPACK = 56, 56, 56, 56, 56, 56
HD = 64
LEN = 1024
TILE = 128
TILES = LEN // TILE
PAIR = 2 * HD
FAR = -1e30
MARKS = 16
LSE_ROW = 8
LIVE_LANE = 12
MIB = 2**20


def dot(left, right):
    return jnp.dot(left, right, preferred_element_type=jnp.float32)


def three_parts(row):
    high = row.astype(jnp.bfloat16)
    rest = row - high.astype(jnp.float32)
    mid = rest.astype(jnp.bfloat16)
    low = (rest - mid.astype(jnp.float32)).astype(jnp.bfloat16)
    return high, mid, low


def label_marks(labels):
    row = lax.broadcasted_iota(jnp.int32, (TILE, labels.shape[1]), 0)
    same = labels == row
    ones = (row < LSE_ROW + 3) | ((row == LIVE_LANE) & (labels != 0))
    keys = jnp.where(row < LSE_ROW, jnp.where(same, 0.0, FAR), jnp.where(ones, 1.0, 0.0))
    queries = jnp.where(same & (row < LSE_ROW), 1.0, 0.0)[:MARKS]
    return keys.astype(jnp.bfloat16).T, queries.astype(jnp.bfloat16)


def tile_edges(segments):
    return segments.reshape(-1, TILE)[:, :: TILE - 1].reshape(-1)


def key_range(edges, base, i):
    low, high = edges[(base + i) * 2], edges[(base + i) * 2 + 1]
    first, last = i, i
    for j in reversed(range(TILES)):
        first = jnp.where((j < i) & (edges[(base + j) * 2 + 1] == low), j, first)
    for j in range(TILES):
        last = jnp.where((j > i) & (edges[(base + j) * 2] == high), j, last)
    return first, last - first + 1


def halves_of(block):
    return jnp.concatenate([block[:HD, :TILE], block[HD:, TILE:]], axis=0)


def split_rows(tile_t):
    zero = jnp.zeros((HD, TILE), tile_t.dtype)
    return jnp.concatenate(
        [
            jnp.concatenate([tile_t[:HD], zero], axis=1),
            jnp.concatenate([zero, tile_t[HD:]], axis=1),
        ],
        axis=0,
    )


def split_lanes(tile):
    lane = lax.broadcasted_iota(jnp.int32, tile.shape, 1)
    zero = jnp.zeros_like(tile)
    return jnp.concatenate(
        [jnp.where(lane < HD, tile, zero), jnp.where(lane < HD, zero, tile)], axis=0
    )


def each_width(count, branch):
    for width in range(1, TILES + 1):
        pl.when(count == width)(partial(branch, width))


def dot_nt(left, right):
    return lax.dot_general(
        left, right, (((1,), (1,)), ((), ())), preferred_element_type=jnp.float32
    )


def dot_tn(left, right):
    return lax.dot_general(
        left, right, (((0,), (0,)), ((), ())), preferred_element_type=jnp.float32
    )


def full(ref):
    shape = ref.shape
    return pl.BlockSpec(shape, lambda *_: (0,) * len(shape), pipeline_mode=pl.Buffered(1))


def call(kernel, name, grid, ins, outs, scratch=(), scalars=(), flops=0, aliases=None, vmem=56):
    specs, arrays = [], []
    for item in ins:
        if isinstance(item, tuple):
            arrays.append(item[0])
            if item[1] is None:
                specs.append(pl.BlockSpec(memory_space=pl.ANY))
            else:
                specs.append(pl.BlockSpec(item[1], item[2]))
        else:
            arrays.append(item)
            specs.append(full(item))
    size = sum(a.size * a.dtype.itemsize for a in arrays)
    size += sum(jnp.dtype(d).itemsize * math.prod(s) for s, d, _, _ in outs)
    return pl.pallas_call(
        kernel,
        grid_spec=pltpu.PrefetchScalarGridSpec(
            num_scalar_prefetch=len(scalars),
            grid=grid,
            in_specs=specs,
            out_specs=[pl.BlockSpec(b, m) for _, _, b, m in outs],
            scratch_shapes=scratch,
        ),
        out_shape=[jax.ShapeDtypeStruct(s, d) for s, d, _, _ in outs],
        compiler_params=pltpu.CompilerParams(vmem_limit_bytes=vmem * MIB),
        cost_estimate=pl.CostEstimate(flops=flops, bytes_accessed=size, transcendentals=0),
        input_output_aliases=aliases or {},
        name=name,
    )(*scalars, *arrays)


def rows_of(i, *_):
    return (i, 0)


def stats(z):
    mean = jnp.mean(z, axis=-1, keepdims=True)
    centred = z - mean
    spread = jnp.mean(centred * centred, axis=-1, keepdims=True)
    scale = lax.rsqrt(spread + norm_eps)
    return centred * scale, scale


def norm_back(upstream, unit, scale, gain):
    t = upstream * gain
    inner = jnp.mean(t * unit, axis=-1, keepdims=True)
    return (t - jnp.mean(t, axis=-1, keepdims=True) - unit * inner) * scale


def layer_kernel(
    heads, x, dual, gn, gd, marks, out_a, out_b, up_a, up_b, down_a, down_b, g1, b1, g2, b2,
    normed_out, dual_out, gfirst_ref, gheads, ffn_grad_a, ffn_grad_b,
    out_grad_a, out_grad_b, sums,
    hid, slope, acc_up, acc_down, acc_out,
):
    i = pl.program_id(0)
    half = out_a.shape[0]
    ff = up_a.shape[1]
    chunk = 512

    @pl.when(i == 0)
    def _():
        sums[...] = jnp.zeros_like(sums)
        acc_up[...] = jnp.zeros_like(acc_up)
        acc_down[...] = jnp.zeros_like(acc_down)
        acc_out[...] = jnp.zeros_like(acc_out)

    attn = dot(heads[:, :half], out_a[...]) + dot(heads[:, half:], out_b[...])
    z1 = x[...].astype(jnp.float32) + attn
    unit, scale = stats(z1)
    normed = unit * g1[...] + b1[...]
    low = normed.astype(jnp.bfloat16)
    ffn = None
    for n, (up, down) in enumerate(((up_a, down_a), (up_b, down_b))):
        for c in range(ff // chunk):
            cols = slice(c * chunk, (c + 1) * chunk)
            at = slice(n * ff + c * chunk, n * ff + (c + 1) * chunk)
            v = dot(low, up[:, cols])
            square = v * v
            t = jnp.tanh(v * (GATE + (GATE * CUBE) * square))
            open_part = 0.5 + 0.5 * t
            hidden = (v * open_part).astype(jnp.bfloat16)
            hid[:, at] = hidden
            slope[:, at] = open_part + (v * (0.5 - 0.5 * t * t)) * (
                GATE + (3 * GATE * CUBE) * square
            )
            part = dot(hidden, down[cols, :])
            ffn = part if ffn is None else ffn + part
    unit2, scale2 = stats(normed + ffn)
    normed_out[...] = (unit2 * g2[...] + b2[...]).astype(jnp.bfloat16)
    dual_out[...] = (dual[...].astype(jnp.float32) + attn + ffn).astype(jnp.bfloat16)
    upstream = gn[...].astype(jnp.float32)
    gmid = norm_back(upstream, unit2, scale2, g2[...])
    gdual = gd[...].astype(jnp.float32)
    gffn = (gmid + gdual).astype(jnp.bfloat16)
    gffn_t = gffn.T
    low_t = low.T
    gnormed = gmid
    for n, (up, down) in enumerate(((up_a, down_a), (up_b, down_b))):
        for c in range(ff // chunk):
            cols = slice(c * chunk, (c + 1) * chunk)
            at = slice(n * ff + c * chunk, n * ff + (c + 1) * chunk)
            gpre = (dot_nt(gffn, down[cols, :]) * slope[:, at]).astype(jnp.bfloat16)
            acc_down[:, at] += dot(gffn_t, hid[:, at])
            acc_up[:, at] += dot(low_t, gpre)
            gnormed = gnormed + dot_nt(gpre, up[:, cols])
    gfirst = norm_back(gnormed, unit, scale, g1[...])
    gfirst_ref[...] = gfirst
    gattn = (gfirst + gdual).astype(jnp.bfloat16)
    sums[0:1, :] += jnp.sum(gnormed * unit, axis=0, keepdims=True)
    sums[1:2, :] += jnp.sum(gnormed, axis=0, keepdims=True)
    sums[2:3, :] += jnp.sum(upstream * unit2, axis=0, keepdims=True)
    sums[3:4, :] += jnp.sum(upstream, axis=0, keepdims=True)
    acc_out[...] += dot_tn(heads[...], gattn)
    live = marks[:, LIVE_LANE : LIVE_LANE + 1].astype(jnp.float32)
    gheads[:, :half] = (dot_nt(gattn, out_a[...]) * live).astype(jnp.bfloat16)
    gheads[:, half:] = (dot_nt(gattn, out_b[...]) * live).astype(jnp.bfloat16)

    @pl.when(i == pl.num_programs(0) - 1)
    def _():
        depth = acc_up.shape[0]
        for n, (ffn_grad, out_grad) in enumerate(
            ((ffn_grad_a, out_grad_a), (ffn_grad_b, out_grad_b))
        ):
            ffn_grad[:ff, :] = acc_down[:, n * ff : (n + 1) * ff].T.astype(jnp.bfloat16)
            for c in range(ff // depth):
                at = n * ff + c * depth
                ffn_grad[ff + c * depth : ff + (c + 1) * depth, :] = acc_up[
                    :, at : at + depth
                ].astype(jnp.bfloat16)
            out_grad[...] = acc_out[n * half : (n + 1) * half, :].astype(jnp.bfloat16)


def layer(heads, x, dual, gn, gd, marks, outs, ups, downs, g1, b1, g2, b2, block=BLOCK):
    rows, depth = x.shape
    ff, half = ups[0].shape[1], outs[0].shape[0]
    tall = ((rows, depth), jnp.bfloat16, (block, depth), rows_of)
    tall32 = ((rows, depth), jnp.float32, (block, depth), rows_of)

    def once(*shape, dtype=jnp.bfloat16):
        return (shape, dtype, shape, lambda i: (0, 0))

    return call(
        layer_kernel, "layer", (rows // block,),
        [(a, (block, a.shape[1]), rows_of) for a in (heads, x, dual, gn, gd, marks)]
        + [*outs, *ups, *downs, g1, b1, g2, b2],
        [tall, tall, tall32, tall, once(2 * ff, depth), once(2 * ff, depth),
         once(half, depth), once(half, depth), once(8, depth, dtype=jnp.float32)],
        scratch=[
            pltpu.VMEM((block, 2 * ff), jnp.bfloat16),
            pltpu.VMEM((block, 2 * ff), jnp.float32),
            pltpu.VMEM((depth, 2 * ff), jnp.float32),
            pltpu.VMEM((depth, 2 * ff), jnp.float32),
            pltpu.VMEM((2 * half, depth), jnp.float32),
        ],
        flops=2 * rows * depth * (3 * depth + 12 * ff),
        vmem=VM_LAYER,
    )


def fill_block(table, p, i, tile_t):
    table[p, i, :HD, :TILE] = tile_t[:HD]
    table[p, i, HD:PAIR, TILE:] = tile_t[HD:]


def score_bound(qkv, width):
    row = lax.broadcasted_iota(jnp.int32, (width, TILE), 0)
    head = lax.broadcasted_iota(jnp.int32, (width, TILE), 1)
    heads = (row // HD == head).astype(jnp.bfloat16)
    largest = []
    for at in (0, width):
        block = qkv[:, at : at + width].astype(jnp.float32)
        norms = dot((block * block).astype(jnp.bfloat16), heads)
        largest.append(jnp.max(norms, axis=0, keepdims=True))
    return jnp.max(largest[0] * largest[1]) * (1.02 / HD)


def attend_kernel(
    edges, core, x_ref, qa, ka, va, qb, kb, vb, labels,
    qkv_ref, out_ref, lse_ref, key_marks, query_marks, kcat, vt, qt, mixed_t,
):
    seq = pl.program_id(0)
    base = (core[0] * pl.num_programs(0) + seq) * TILES
    key_marks[...], query_marks[...] = label_marks(labels[...])
    half = qa.shape[1]
    width = 2 * half
    pairs = width // PAIR
    x = x_ref[...]

    @pl.when(seq == 0)
    def _():
        qt[...] = jnp.zeros_like(qt)

    for n, w in enumerate((qa, qb, ka, kb, va, vb)):
        qkv_ref[:, n * half : (n + 1) * half] = dot(x, w[...]).astype(jnp.bfloat16)
    small_scores = score_bound(qkv_ref, width) < SAFE
    for p in range(pairs):
        lanes = slice(p * PAIR, (p + 1) * PAIR)
        kcat[p, :, :PAIR] = qkv_ref[:, width + p * PAIR : width + (p + 1) * PAIR]
        kcat[p, :, PAIR:] = key_marks[...]
        vt[lanes, :] = qkv_ref[:, 2 * width + p * PAIR : 2 * width + (p + 1) * PAIR].T
        for i in range(TILES):
            cols = slice(i * TILE, (i + 1) * TILE)
            fill_block(qt, p, i, (qkv_ref[cols, lanes] * jnp.bfloat16(HD**-0.5)).T)
            qt[p, i, PAIR : PAIR + MARKS, :TILE] = query_marks[:, cols]
            qt[p, i, PAIR : PAIR + MARKS, TILE:] = query_marks[:, cols]

    def step(i, carry):
        at = pl.multiple_of(i * TILE, TILE)
        first, count = key_range(edges, base, i)
        first = jnp.where(small_scores, first, 0)
        start = pl.multiple_of(first * TILE, TILE)

        def branch(width, small=True):
            at_keys = pl.ds(start, width * TILE)

            def scores_of(p):
                return dot(kcat[p, at_keys, :], qt[p, i])

            def finish(p, scores):
                top = None
                if not small:
                    top = jnp.max(scores, axis=0, keepdims=True)
                    scores = scores - top
                probs = jnp.exp(scores)
                total = jnp.sum(probs, axis=0, keepdims=True)
                mixed = dot(vt[p * PAIR : (p + 1) * PAIR, at_keys], probs.astype(jnp.bfloat16))
                mixed_t[p * PAIR : (p + 1) * PAIR, pl.ds(at, TILE)] = halves_of(mixed / total)
                log_total = jnp.log(total)
                lse_ref[0, p, pl.ds(i, 1), :] = log_total if small else top + log_total

            ahead = scores_of(0)
            for p in range(pairs):
                scores = ahead
                if p + 1 < pairs:
                    ahead = scores_of(p + 1)
                finish(p, scores)

        each_width(jnp.where(small_scores, count, 0), branch)
        pl.when(jnp.logical_not(small_scores))(partial(branch, TILES, False))
        return carry

    lax.fori_loop(0, TILES, step, 0)
    live = 1.0 - query_marks[:1, :].astype(jnp.float32)
    for p in range(pairs):
        lanes = slice(p * PAIR, (p + 1) * PAIR)
        out_ref[:, lanes] = (mixed_t[lanes, :] * live).astype(jnp.bfloat16).T


def attend(edges, core, x, own, other, segments):
    rows, depth = x.shape
    half = own[0].shape[1]
    width = 2 * half
    seqs, pairs = rows // LEN, width // PAIR
    return call(
        attend_kernel, "attend", (seqs,),
        [
            (x, (LEN, depth), lambda s, *_: (s, 0)),
            *own,
            *other,
            (segments.reshape(1, -1), (1, LEN), lambda s, _, core: (0, core[0] * seqs + s)),
        ],
        [
            ((rows, 3 * width), jnp.bfloat16, (LEN, 3 * width), lambda s, *_: (s, 0)),
            ((rows, width), jnp.bfloat16, (LEN, width), lambda s, *_: (s, 0)),
            (
                (seqs, pairs, TILES, 2 * TILE), jnp.float32, (1, pairs, TILES, 2 * TILE),
                lambda s, *_: (s, 0, 0, 0),
            ),
            ((rows, TILE), jnp.bfloat16, (LEN, TILE), lambda s, *_: (s, 0)),
            ((MARKS, rows), jnp.bfloat16, (MARKS, LEN), lambda s, *_: (0, s)),
        ],
        scratch=[
            pltpu.VMEM((pairs, LEN, PAIR + TILE), jnp.bfloat16),
            pltpu.VMEM((width, LEN), jnp.bfloat16),
            pltpu.VMEM((pairs, TILES, PAIR + TILE, 2 * TILE), jnp.bfloat16),
            pltpu.VMEM((width, LEN), jnp.float32),
        ],
        scalars=(edges, core),
        flops=2 * rows * (3 * width * depth + 2 * width * LEN),
        vmem=VM_ATT,
    )


def attend_back_kernel(edges, where, *refs):
    base = where[1] * TILES
    q_ref, k_ref, v_ref, g_ref, o_ref, key_marks, query_marks, lse_ref = refs[:8]
    out_ref, kcat, vcat, kt, qt, gt, dk, dv, dqt = refs[-9:]
    width = q_ref.shape[1]
    pairs = width // PAIR
    groups = pairs // 2

    def place(p, what):
        at = (((p % groups) * 2 + p // groups) * 3 + what) * PAIR
        return slice(at, at + PAIR)

    def negated(row):
        return [part.astype(jnp.float32) for part in three_parts(-row)]

    qt[...] = jnp.zeros_like(qt)
    gt[...] = jnp.zeros_like(gt)
    dk[...] = jnp.zeros_like(dk)
    dv[...] = jnp.zeros_like(dv)
    pad = jnp.zeros((MARKS - LSE_ROW - 3, 2 * TILE), jnp.float32)
    none = jnp.zeros((LSE_ROW, 2 * TILE), jnp.float32)
    for p in range(pairs):
        lanes = slice(p * PAIR, (p + 1) * PAIR)
        kcat[p, :, :PAIR] = k_ref[:, lanes]
        kcat[p, :, PAIR:] = key_marks[...]
        vcat[p, :, :PAIR] = v_ref[:, lanes]
        vcat[p, :, PAIR:] = key_marks[...]
        kt[lanes, :] = k_ref[:, lanes].T
        for i in range(TILES):
            cols = slice(i * TILE, (i + 1) * TILE)
            fill_block(qt, p, i, (q_ref[cols, lanes] * jnp.bfloat16(HD**-0.5)).T)
            grad_t = g_ref[cols, lanes].T
            fill_block(gt, p, i, grad_t)
            agree = grad_t.astype(jnp.float32) * o_ref[cols, lanes].T.astype(jnp.float32)
            delta = jnp.concatenate(
                [
                    jnp.sum(agree[:HD], axis=0, keepdims=True),
                    jnp.sum(agree[HD:], axis=0, keepdims=True),
                ],
                axis=1,
            )
            marks = query_marks[:LSE_ROW, cols].astype(jnp.float32)
            marks = jnp.concatenate([marks, marks], axis=1)
            lse = lse_ref[0, p, i : i + 1, :]
            qt[p, i, PAIR : PAIR + MARKS, :] = jnp.concatenate(
                [marks, *negated(lse), pad], axis=0
            ).astype(jnp.bfloat16)
            gt[p, i, PAIR : PAIR + MARKS, :] = jnp.concatenate(
                [none, *negated(delta), pad], axis=0
            ).astype(jnp.bfloat16)

    def step(i, carry):
        at = pl.multiple_of(i * TILE, TILE)
        first, count = key_range(edges, base, i)
        start = pl.multiple_of(first * TILE, TILE)

        def branch(width):
            at_keys = pl.ds(start, width * TILE)

            def head(p):
                scores = dot(kcat[p, at_keys, :], qt[p, i])
                grad_probs = dot(vcat[p, at_keys, :], gt[p, i])
                return scores, grad_probs

            def finish(p, scores, grad_probs):
                lanes = slice(p * PAIR, (p + 1) * PAIR)
                query = q_ref[pl.ds(at, TILE), lanes] * jnp.bfloat16(HD**-0.5)
                grad = g_ref[pl.ds(at, TILE), lanes]
                probs = jnp.exp(scores)
                grad_scores = (probs * grad_probs).astype(jnp.bfloat16)
                dv[p, at_keys, :] += dot(probs.astype(jnp.bfloat16), split_lanes(grad))
                dk[p, at_keys, :] += dot(grad_scores, split_lanes(query))
                dqt[lanes, pl.ds(at, TILE)] = halves_of(dot(kt[lanes, at_keys], grad_scores))

            ahead = head(0)
            for p in range(pairs):
                now = ahead
                if p + 1 < pairs:
                    ahead = head(p + 1)
                finish(p, *now)

        each_width(count, branch)
        return carry

    lax.fori_loop(0, TILES, step, 0)
    for p in range(pairs):
        lanes = slice(p * PAIR, (p + 1) * PAIR)
        out_ref[:, place(p, 0)] = (dqt[lanes, :] * HD**-0.5).astype(jnp.bfloat16).T
        out_ref[:, place(p, 1)] = dk[p].astype(jnp.bfloat16)
        out_ref[:, place(p, 2)] = dv[p].astype(jnp.bfloat16)


def attend_back(qkv, gheads, heads, key_marks, query_marks, lse, core, seq, edges):
    rows, width = heads.shape
    seqs, pairs = rows // LEN, width // PAIR
    where = jnp.concatenate([jnp.full((1,), seq, jnp.int32), core * seqs + seq])
    by_seq = lambda i, _, where: (where[0], 0)
    return call(
        attend_back_kernel, "attend_back", (1,),
        [
            (qkv, (LEN, width), by_seq),
            (qkv, (LEN, width), lambda i, _, where: (where[0], 1)),
            (qkv, (LEN, width), lambda i, _, where: (where[0], 2)),
            (gheads, (LEN, width), by_seq),
            (heads, (LEN, width), by_seq),
            (key_marks, (LEN, TILE), by_seq),
            (query_marks, (MARKS, LEN), lambda i, _, where: (0, where[0])),
            (lse, (1, pairs, TILES, 2 * TILE), lambda i, _, where: (where[0], 0, 0, 0)),
        ],
        [((LEN, 3 * width), jnp.bfloat16, (LEN, 3 * width), lambda i, *_: (0, 0))],
        scratch=[
            pltpu.VMEM((pairs, LEN, PAIR + TILE), jnp.bfloat16),
            pltpu.VMEM((pairs, LEN, PAIR + TILE), jnp.bfloat16),
            pltpu.VMEM((width, LEN), jnp.bfloat16),
            pltpu.VMEM((pairs, TILES, PAIR + TILE, 2 * TILE), jnp.bfloat16),
            pltpu.VMEM((pairs, TILES, PAIR + TILE, 2 * TILE), jnp.bfloat16),
            pltpu.VMEM((pairs, LEN, PAIR), jnp.float32),
            pltpu.VMEM((pairs, LEN, PAIR), jnp.float32),
            pltpu.VMEM((width, LEN), jnp.float32),
        ],
        scalars=(edges, where),
        flops=10 * LEN * width * LEN,
        vmem=VM_BACK,
    )[0]


def project_back_kernel(seqs, x_ref, *refs):
    grads = refs[:seqs]
    out_a, out_b, sums, own_ref, other_ref, x_t = refs[seqs:]
    step = pl.program_id(0)

    @pl.when(step == 0)
    def _():
        x_t[...] = x_ref[...].T

        start = grads[0].shape[1] * pl.num_programs(0) // 2
        both = jnp.concatenate([sums[...], jnp.zeros_like(sums)], axis=0)
        end = start + out_a.shape[0]
        for buf, out_grad in ((own_ref, out_a), (other_ref, out_b)):
            buf[start:end, :] = out_grad[...]
            buf[end : end + MARKS, :] = both.astype(jnp.bfloat16)
            if end + MARKS < buf.shape[0]:
                rest = (buf.shape[0] - end - MARKS, buf.shape[1])
                buf[end + MARKS :, :] = jnp.zeros(rest, jnp.bfloat16)

    part = dot(x_t[:, :LEN], grads[0][...])
    for s in range(1, seqs):
        part = part + dot(x_t[:, s * LEN : (s + 1) * LEN], grads[s][...])
    depth = part.shape[0]
    for n, buf in enumerate((own_ref, other_ref)):

        @pl.when(step % 2 == n)
        def _():
            for m in range(3):
                rows = pl.ds(pl.multiple_of((step // 2 * 3 + m) * PAIR, PAIR), PAIR)
                for r in range(depth // PAIR):
                    buf[rows, r * PAIR : (r + 1) * PAIR] = part[
                        r * PAIR : (r + 1) * PAIR, m * PAIR : (m + 1) * PAIR
                    ].astype(jnp.bfloat16)


def project_back(x, grads, extra, height):
    rows, depth = x.shape
    wide = grads[0].shape[1]
    size = 3 * PAIR
    buf = ((height, depth), jnp.bfloat16, (height, depth), lambda i: (0, 0))
    return call(
        partial(project_back_kernel, len(grads)), "project_back", (wide // size,),
        [x, *((grad, (LEN, size), lambda i: (0, i)) for grad in grads), *extra],
        [buf, buf],
        scratch=[pltpu.VMEM((depth, rows), jnp.bfloat16)],
        flops=2 * rows * depth * wide,
        vmem=VM_PROJ,
    )


def stream_kernel(seqs, gfirst, *refs):
    grads, weights, out, table = refs[:seqs], refs[seqs:-2], refs[-2], refs[-1]
    i = pl.program_id(0)

    @pl.when(i == 0)
    def _():
        count = len(weights)
        for n, weight in enumerate(weights):
            for g in range(weight.shape[1] // PAIR):
                at = (g * count + n) * PAIR
                table[:, at : at + PAIR] = weight[:, g * PAIR : (g + 1) * PAIR]

    for s, grad in enumerate(grads):

        @pl.when(i // (LEN // BLOCK) == s)
        def _():
            out[...] = gfirst[...] + dot_nt(grad[...], table[...])


def stream(gfirst, grads, own, other):
    rows, depth = gfirst.shape
    wide = grads[0].shape[1]
    per = LEN // BLOCK

    def part(s):
        return lambda i: (jnp.clip(i - s * per, 0, per - 1), 0)

    return call(
        partial(stream_kernel, len(grads)), "stream", (rows // BLOCK,),
        [(gfirst, (BLOCK, depth), rows_of)]
        + [(grad, (BLOCK, wide), part(s)) for s, grad in enumerate(grads)]
        + [*own, *other],
        [((rows, depth), jnp.float32, (BLOCK, depth), rows_of)],
        scratch=[pltpu.VMEM((depth, wide), jnp.bfloat16)],
        flops=2 * rows * depth * wide,
        vmem=VM_STREAM,
    )[0]


def swap_cores(block):
    return lax.ppermute(block, "mp", [(0, 1), (1, 0)])


def stages_of(chips, radices):
    me, core = lax.axis_index("dp"), lax.axis_index("mp")

    def pairs(masks):
        return [(2 * c + i, 2 * (c ^ masks[i]) + i) for c in range(chips) for i in range(2)]

    stages = []
    bit = 0
    if radices[:2] == (2, 2):
        low, high = me & 1, (me >> 1) & 1
        stages = [
            (jnp.where(core == 0, low, high), 2, [pairs((1, 2))]),
            (jnp.where(core == 0, high, low), 2, [pairs((2, 1))]),
        ]
        bit = 2
        radices = radices[2:]
    while 1 << bit < chips:
        radix = min(radices[0], chips >> bit)
        radices = radices[1:] or radices
        ways = [pairs((j << bit, j << bit)) for j in range(1, radix)]
        stages.append(((me >> bit) & (radix - 1), radix, ways))
        bit += radix // 2
    return stages


def send(block, pairs):
    return lax.ppermute(block, ("dp", "mp"), pairs)


def part(block, which, rows):
    return lax.dynamic_slice_in_dim(block, which * rows, rows)


def added(blocks):
    total = blocks[0].astype(jnp.float32)
    for block in blocks[1:]:
        total = total + block.astype(jnp.float32)
    return total.astype(jnp.bfloat16)


def unpack_kernel(size, shapes, places, *refs):
    pieces, outs, table = refs[: -len(shapes) - 1], refs[-len(shapes) - 1 : -1], refs[-1]
    at = 0
    for piece in pieces:
        block = piece[...].astype(jnp.float32)
        for n in range(block.shape[0] // size):
            table[pl.ds(pl.multiple_of(places[at] * size, size), size), :] = block[
                n * size : (n + 1) * size
            ]
            at += 1
    row = 0
    depth = table.shape[1]
    for out, (kind, height, width) in zip(outs, shapes):
        if kind == "rows":
            out[...] = table[row : row + height, :]
            row += height
        elif kind == "wide":
            for n in range(width // depth):
                out[:, n * depth : (n + 1) * depth] = table[row : row + height, :]
                row += height
        else:
            base, count = kind
            for g in range(width // PAIR):
                at = (g * count + base) * PAIR
                for n in range(height // PAIR):
                    out[n * PAIR : (n + 1) * PAIR, g * PAIR : (g + 1) * PAIR] = table[
                        at : at + PAIR, n * PAIR : (n + 1) * PAIR
                    ]
                row += PAIR


def unpack(pieces, places, shapes, rows, chips):
    depth = pieces[0].shape[1]
    size = rows // chips
    return call(
        partial(unpack_kernel, size, shapes), "unpack", (1,), pieces,
        [((h, w), jnp.float32, (h, w), lambda i, _: (0, 0)) for _, h, w in shapes],
        scratch=[pltpu.VMEM((rows, depth), jnp.float32)],
        scalars=(places,),
        vmem=VM_UNPACK,
    )


def sum_everywhere(own, other, shapes, chips, radices):
    rows = own.shape[0]
    stages = stages_of(chips, radices)
    cores = [(2 * c + i, 2 * c + 1 - i) for c in range(chips) for i in range(2)]
    addends = [own, *(yield [(other, cores)])]
    height = rows
    for digit, radix, ways in stages:
        height //= radix
        got = yield [
            (added([part(a, digit ^ (j + 1), height) for a in addends]), pairs)
            for j, pairs in enumerate(ways)
        ]
        addends = [part(a, digit, height) for a in addends] + got
    pieces = [added(addends)]
    places = [jnp.int32(0)]
    for n, (digit, radix, ways) in enumerate(reversed(stages)):
        weight = chips
        for _, earlier, _ in stages[: len(stages) - n]:
            weight //= earlier
        held = pieces[0] if len(pieces) == 1 else jnp.concatenate(pieces)
        pieces = [held] + (yield [(held, pairs) for pairs in ways])
        places = [p + (digit ^ j) * weight for j in range(radix) for p in places]
    return unpack(pieces, jnp.stack(places).astype(jnp.int32), shapes, rows, chips)


class Chain:
    def __init__(self, steps):
        self.steps, self.result = steps, None
        self.wishes = next(steps)

    def take(self, got):
        try:
            self.wishes = self.steps.send(got)
        except StopIteration as end:
            self.wishes, self.result = [], end.value


def advance(chains, work=None, token=None, beside=()):
    blocks = [block for chain in chains for block, _ in chain.wishes]
    if work is not None:
        *blocks, token = lax.optimization_barrier((*blocks, token))
    else:
        blocks = lax.optimization_barrier(blocks)
    ways = [pairs for chain in chains for _, pairs in chain.wishes]
    got = [send(block, pairs) for block, pairs in zip(blocks, ways)]
    out = None
    if work is not None:
        out = work(token)
        *got, last = lax.optimization_barrier((*got, out[-1]))
        out = (*out[:-1], last)
    elif beside:
        *got, _ = lax.optimization_barrier((*got, *beside))[: len(got) + 1]
    for chain in chains:
        if chain.wishes:
            count = len(chain.wishes)
            chain.take(got[:count])
            got = got[count:]
    return out


def on_device(
    normed_in,
    dual_in,
    query_weight,
    key_weight,
    value_weight,
    output_weight,
    first_gain,
    first_bias,
    up_weight,
    down_weight,
    second_gain,
    second_bias,
    segments,
    grad_normed_out,
    grad_dual_out,
    chips,
):
    rows, depth = normed_in.shape
    core = lax.axis_index("mp")
    half, ff = query_weight.shape[1], up_weight.shape[1]
    own = (query_weight, key_weight, value_weight)
    other = tuple(swap_cores(w) for w in own)
    outs = (output_weight, swap_cores(output_weight))
    ups = (up_weight, swap_cores(up_weight))
    downs = (down_weight, swap_cores(down_weight))
    edges = tile_edges(segments)
    core = core.astype(jnp.int32).reshape(1)
    qkv, heads_out, log_totals, key_marks, query_marks = attend(
        edges, core, normed_in, own, other, segments
    )
    grain = 8 * chips

    def padded(count):
        return -(-count // grain) * grain

    row = lambda v: v.reshape(1, depth)
    normed_out, dual_out, grad_first, grad_heads, ffn_own, ffn_other, *extra = layer(
        heads_out, normed_in, dual_in, grad_normed_out, grad_dual_out, key_marks, outs, ups, downs,
        row(first_gain), row(first_bias), row(second_gain), row(second_bias),
    )
    back = partial(
        attend_back, qkv, grad_heads, heads_out, key_marks, query_marks, log_totals, core
    )
    fed = Chain(
        sum_everywhere(
            ffn_own, ffn_other,
            [("rows", ff, depth), ("wide", depth, ff)], chips, (2, 2, 4)
        )
    )
    grad_qkv = []
    for seq in range(rows // LEN):
        grad_qkv += advance([fed], lambda token: (back(seq, token),), edges)
    height = padded(3 * half + half + MARKS)
    own_grads, other_grads = advance(
        [fed], lambda x: project_back(x, grad_qkv, extra, height), normed_in
    )
    rest = Chain(
        sum_everywhere(
            own_grads, other_grads,
            [((n, 3), depth, half) for n in range(3)]
            + [("rows", half, depth)] + [("rows", 1, depth)] * 4,
            chips, (4,),
        )
    )
    chains = [fed, rest]
    (grad_stream,) = advance(
        chains, lambda grad: (stream(grad, grad_qkv, own, other),), grad_first
    )
    while any(chain.wishes for chain in chains):
        advance(chains, beside=() if fed.result is None else fed.result[:1])
    down_total, up_total = fed.result
    query_total, key_total, value_total, output_total, *small = rest.result
    small = [total.reshape(depth) for total in small]
    return (
        normed_out,
        dual_out,
        grad_stream,
        query_total,
        key_total,
        value_total,
        output_total,
        small[0],
        small[1],
        up_total,
        down_total,
        small[2],
        small[3],
    )


def solution(mesh):
    rows = P(("dp", "mp"), None)
    columns = P(None, "mp")
    return jax.shard_map(
        partial(on_device, chips=mesh.shape["dp"]),
        mesh=mesh,
        in_specs=(
            rows, rows, columns, columns, columns, P("mp", None), P(), P(),
            columns, P("mp", None), P(), P(), P("dp"), rows, rows,
        ),
        out_specs=(
            rows, rows, rows, columns, columns, columns, P("mp", None), P(), P(),
            columns, P("mp", None), P(), P(),
        ),
        check_vma=False,
    )
```

```python
import math
from functools import partial

import jax
import jax.numpy as jnp
from jax import lax
from jax.experimental import pallas as pl
from jax.experimental.pallas import tpu as pltpu
from jax.sharding import PartitionSpec as P

norm_eps = 1e-05
BLOCK = 512
GATE = 0.7978845608028654
CUBE = 0.044715
SAFE = 3600.0
LAYER_BLOCK, SLOPE_TYPE = 256, jnp.float32
VM_ATT, VM_LAYER, VM_BACK, VM_PROJ, VM_STREAM, VM_UNPACK = 56, 56, 56, 56, 56, 56
HD = 64
LEN = 1024
TILE = 128
TILES = LEN // TILE
PAIR = 2 * HD
FAR = -1e30
MARKS = 16
LSE_ROW = 8
LIVE_LANE = 12
MIB = 2**20


def dot(left, right):
    return jnp.dot(left, right, preferred_element_type=jnp.float32)


def three_parts(row):
    high = row.astype(jnp.bfloat16)
    rest = row - high.astype(jnp.float32)
    mid = rest.astype(jnp.bfloat16)
    low = (rest - mid.astype(jnp.float32)).astype(jnp.bfloat16)
    return high, mid, low


def label_marks(labels):
    row = lax.broadcasted_iota(jnp.int32, (TILE, labels.shape[1]), 0)
    same = labels == row
    ones = (row < LSE_ROW + 3) | ((row == LIVE_LANE) & (labels != 0))
    keys = jnp.where(row < LSE_ROW, jnp.where(same, 0.0, FAR), jnp.where(ones, 1.0, 0.0))
    queries = jnp.where(same & (row < LSE_ROW), 1.0, 0.0)[:MARKS]
    return keys.astype(jnp.bfloat16).T, queries.astype(jnp.bfloat16)


def tile_edges(segments):
    return segments.reshape(-1, TILE)[:, :: TILE - 1].reshape(-1)


def key_range(edges, base, i):
    low, high = edges[(base + i) * 2], edges[(base + i) * 2 + 1]
    first, last = i, i
    for j in reversed(range(TILES)):
        first = jnp.where((j < i) & (edges[(base + j) * 2 + 1] == low), j, first)
    for j in range(TILES):
        last = jnp.where((j > i) & (edges[(base + j) * 2] == high), j, last)
    return first, last - first + 1


def halves_of(block):
    return jnp.concatenate([block[:HD, :TILE], block[HD:, TILE:]], axis=0)


def split_lanes(tile):
    lane = lax.broadcasted_iota(jnp.int32, tile.shape, 1)
    zero = jnp.zeros_like(tile)
    return jnp.concatenate(
        [jnp.where(lane < HD, tile, zero), jnp.where(lane < HD, zero, tile)], axis=0
    )


def each_width(count, branch):
    for width in range(1, TILES + 1):
        pl.when(count == width)(partial(branch, width))


def dot_nt(left, right):
    return lax.dot_general(
        left, right, (((1,), (1,)), ((), ())), preferred_element_type=jnp.float32
    )


def dot_tn(left, right):
    return lax.dot_general(
        left, right, (((0,), (0,)), ((), ())), preferred_element_type=jnp.float32
    )


def full(ref):
    shape = ref.shape
    return pl.BlockSpec(shape, lambda *_: (0,) * len(shape), pipeline_mode=pl.Buffered(1))


def call(kernel, name, grid, ins, outs, scratch=(), scalars=(), flops=0, aliases=None, vmem=56):
    specs, arrays = [], []
    for item in ins:
        if isinstance(item, tuple):
            arrays.append(item[0])
            if item[1] is None:
                specs.append(pl.BlockSpec(memory_space=pl.ANY))
            else:
                specs.append(pl.BlockSpec(item[1], item[2]))
        else:
            arrays.append(item)
            specs.append(full(item))
    size = sum(a.size * a.dtype.itemsize for a in arrays)
    size += sum(jnp.dtype(d).itemsize * math.prod(s) for s, d, _, _ in outs)
    return pl.pallas_call(
        kernel,
        grid_spec=pltpu.PrefetchScalarGridSpec(
            num_scalar_prefetch=len(scalars),
            grid=grid,
            in_specs=specs,
            out_specs=[
                pl.BlockSpec(b, m) if b else pl.BlockSpec(memory_space=pl.ANY)
                for _, _, b, m in outs
            ],
            scratch_shapes=scratch,
        ),
        out_shape=[jax.ShapeDtypeStruct(s, d) for s, d, _, _ in outs],
        compiler_params=pltpu.CompilerParams(vmem_limit_bytes=vmem * MIB),
        cost_estimate=pl.CostEstimate(flops=flops, bytes_accessed=size, transcendentals=0),
        input_output_aliases=aliases or {},
        name=name,
    )(*scalars, *arrays)


def rows_of(i, *_):
    return (i, 0)


def stats(z):
    mean = jnp.mean(z, axis=-1, keepdims=True)
    centred = z - mean
    spread = jnp.mean(centred * centred, axis=-1, keepdims=True)
    scale = lax.rsqrt(spread + norm_eps)
    return centred * scale, scale


def norm_back(upstream, unit, scale, gain):
    t = upstream * gain
    inner = jnp.mean(t * unit, axis=-1, keepdims=True)
    return (t - jnp.mean(t, axis=-1, keepdims=True) - unit * inner) * scale


def layer_kernel(
    heads, x, dual, gn, gd, marks, out_a, out_b, up_a, up_b, down_a, down_b, g1, b1, g2, b2,
    normed_out, dual_out, gfirst_ref, gheads, ffn_grad_a, ffn_grad_b,
    out_grad_a, out_grad_b, sums,
    hid, slope, acc_up, acc_down, acc_out,
):
    i = pl.program_id(0)
    half = out_a.shape[0]
    ff = up_a.shape[1]
    chunk = 512

    @pl.when(i == 0)
    def _():
        sums[...] = jnp.zeros_like(sums)
        acc_up[...] = jnp.zeros_like(acc_up)
        acc_down[...] = jnp.zeros_like(acc_down)
        acc_out[...] = jnp.zeros_like(acc_out)

    attn = dot(heads[:, :half], out_a[...]) + dot(heads[:, half:], out_b[...])
    z1 = x[...].astype(jnp.float32) + attn
    unit, scale = stats(z1)
    normed = unit * g1[...] + b1[...]
    low = normed.astype(jnp.bfloat16)
    ffn = None
    for n, (up, down) in enumerate(((up_a, down_a), (up_b, down_b))):
        for c in range(ff // chunk):
            cols = slice(c * chunk, (c + 1) * chunk)
            at = slice(n * ff + c * chunk, n * ff + (c + 1) * chunk)
            v = dot(low, up[:, cols])
            square = v * v
            t = jnp.tanh(v * (GATE + (GATE * CUBE) * square))
            open_part = 0.5 + 0.5 * t
            hidden = (v * open_part).astype(jnp.bfloat16)
            hid[:, at] = hidden
            slope[:, at] = open_part + (v * (0.5 - 0.5 * t * t)) * (
                GATE + (3 * GATE * CUBE) * square
            )
            part = dot(hidden, down[cols, :])
            ffn = part if ffn is None else ffn + part
    unit2, scale2 = stats(normed + ffn)
    normed_out[...] = (unit2 * g2[...] + b2[...]).astype(jnp.bfloat16)
    dual_out[...] = (dual[...].astype(jnp.float32) + attn + ffn).astype(jnp.bfloat16)
    upstream = gn[...].astype(jnp.float32)
    gmid = norm_back(upstream, unit2, scale2, g2[...])
    gdual = gd[...].astype(jnp.float32)
    gffn = (gmid + gdual).astype(jnp.bfloat16)
    gffn_t = gffn.T
    low_t = low.T
    gnormed = gmid
    for n, (up, down) in enumerate(((up_a, down_a), (up_b, down_b))):
        for c in range(ff // chunk):
            cols = slice(c * chunk, (c + 1) * chunk)
            at = slice(n * ff + c * chunk, n * ff + (c + 1) * chunk)
            gpre = (dot_nt(gffn, down[cols, :]) * slope[:, at]).astype(jnp.bfloat16)
            acc_down[:, at] += dot(gffn_t, hid[:, at])
            acc_up[:, at] += dot(low_t, gpre)
            gnormed = gnormed + dot_nt(gpre, up[:, cols])
    gfirst = norm_back(gnormed, unit, scale, g1[...])
    gfirst_ref[...] = gfirst
    gattn = (gfirst + gdual).astype(jnp.bfloat16)
    sums[0:1, :] += jnp.sum(gnormed * unit, axis=0, keepdims=True)
    sums[1:2, :] += jnp.sum(gnormed, axis=0, keepdims=True)
    sums[2:3, :] += jnp.sum(upstream * unit2, axis=0, keepdims=True)
    sums[3:4, :] += jnp.sum(upstream, axis=0, keepdims=True)
    acc_out[...] += dot_tn(heads[...], gattn)
    live = marks[:, LIVE_LANE : LIVE_LANE + 1].astype(jnp.float32)
    gheads[:, :half] = (dot_nt(gattn, out_a[...]) * live).astype(jnp.bfloat16)
    gheads[:, half:] = (dot_nt(gattn, out_b[...]) * live).astype(jnp.bfloat16)

    @pl.when(i == pl.num_programs(0) - 1)
    def _():
        depth = acc_up.shape[0]
        for n, (ffn_grad, out_grad) in enumerate(
            ((ffn_grad_a, out_grad_a), (ffn_grad_b, out_grad_b))
        ):
            ffn_grad[:ff, :] = acc_down[:, n * ff : (n + 1) * ff].T.astype(jnp.bfloat16)
            for c in range(ff // depth):
                at = n * ff + c * depth
                ffn_grad[ff + c * depth : ff + (c + 1) * depth, :] = acc_up[
                    :, at : at + depth
                ].astype(jnp.bfloat16)
            out_grad[...] = acc_out[n * half : (n + 1) * half, :].astype(jnp.bfloat16)


def layer(heads, x, dual, gn, gd, marks, outs, ups, downs, g1, b1, g2, b2, block=BLOCK):
    rows, depth = x.shape
    ff, half = ups[0].shape[1], outs[0].shape[0]
    tall = ((rows, depth), jnp.bfloat16, (block, depth), rows_of)
    tall32 = ((rows, depth), jnp.float32, (block, depth), rows_of)

    def once(*shape, dtype=jnp.bfloat16):
        return (shape, dtype, shape, lambda i: (0, 0))

    return call(
        layer_kernel, "layer", (rows // block,),
        [(a, (block, a.shape[1]), rows_of) for a in (heads, x, dual, gn, gd, marks)]
        + [*outs, *ups, *downs, g1, b1, g2, b2],
        [tall, tall, tall32, tall, once(2 * ff, depth), once(2 * ff, depth),
         once(half, depth), once(half, depth), once(8, depth, dtype=jnp.float32)],
        scratch=[
            pltpu.VMEM((block, 2 * ff), jnp.bfloat16),
            pltpu.VMEM((block, 2 * ff), jnp.float32),
            pltpu.VMEM((depth, 2 * ff), jnp.float32),
            pltpu.VMEM((depth, 2 * ff), jnp.float32),
            pltpu.VMEM((2 * half, depth), jnp.float32),
        ],
        flops=2 * rows * depth * (3 * depth + 12 * ff),
        vmem=VM_LAYER,
    )


def fill_block(table, p, i, tile_t):
    table[p, i, :HD, :TILE] = tile_t[:HD]
    table[p, i, HD:PAIR, TILE:] = tile_t[HD:]


def score_bound(qkv, width):
    row = lax.broadcasted_iota(jnp.int32, (width, TILE), 0)
    head = lax.broadcasted_iota(jnp.int32, (width, TILE), 1)
    heads = (row // HD == head).astype(jnp.bfloat16)
    largest = []
    for at in (0, width):
        block = qkv[:, at : at + width].astype(jnp.float32)
        norms = dot((block * block).astype(jnp.bfloat16), heads)
        largest.append(jnp.max(norms, axis=0, keepdims=True))
    return jnp.max(largest[0] * largest[1]) * (1.02 / HD)


def attend_kernel(
    edges, core, x_ref, qa, ka, va, qb, kb, vb, labels,
    qkv_ref, out_ref, lse_ref, key_marks, query_marks, kcat, vt, qt, mixed_t,
):
    seq = pl.program_id(0)
    base = (core[0] * pl.num_programs(0) + seq) * TILES
    key_marks[...], query_marks[...] = label_marks(labels[...])
    half = qa.shape[1]
    width = 2 * half
    pairs = width // PAIR
    x = x_ref[...]

    @pl.when(seq == 0)
    def _():
        qt[...] = jnp.zeros_like(qt)

    for n, w in enumerate((qa, qb, ka, kb, va, vb)):
        qkv_ref[:, n * half : (n + 1) * half] = dot(x, w[...]).astype(jnp.bfloat16)
    small_scores = score_bound(qkv_ref, width) < SAFE
    for p in range(pairs):
        lanes = slice(p * PAIR, (p + 1) * PAIR)
        kcat[p, :, :PAIR] = qkv_ref[:, width + p * PAIR : width + (p + 1) * PAIR]
        kcat[p, :, PAIR:] = key_marks[...]
        vt[lanes, :] = qkv_ref[:, 2 * width + p * PAIR : 2 * width + (p + 1) * PAIR].T
        for i in range(TILES):
            cols = slice(i * TILE, (i + 1) * TILE)
            fill_block(qt, p, i, (qkv_ref[cols, lanes] * jnp.bfloat16(HD**-0.5)).T)
            qt[p, i, PAIR : PAIR + MARKS, :TILE] = query_marks[:, cols]
            qt[p, i, PAIR : PAIR + MARKS, TILE:] = query_marks[:, cols]

    def step(i, carry):
        at = pl.multiple_of(i * TILE, TILE)
        first, count = key_range(edges, base, i)
        first = jnp.where(small_scores, first, 0)
        start = pl.multiple_of(first * TILE, TILE)

        def branch(width, small=True):
            at_keys = pl.ds(start, width * TILE)

            def scores_of(p):
                return dot(kcat[p, at_keys, :], qt[p, i])

            def finish(p, scores):
                top = None
                if not small:
                    top = jnp.max(scores, axis=0, keepdims=True)
                    scores = scores - top
                probs = jnp.exp(scores)
                total = jnp.sum(probs, axis=0, keepdims=True)
                mixed = dot(vt[p * PAIR : (p + 1) * PAIR, at_keys], probs.astype(jnp.bfloat16))
                mixed_t[p * PAIR : (p + 1) * PAIR, pl.ds(at, TILE)] = halves_of(mixed / total)
                log_total = jnp.log(total)
                lse_ref[0, p, pl.ds(i, 1), :] = log_total if small else top + log_total

            ahead = scores_of(0)
            for p in range(pairs):
                scores = ahead
                if p + 1 < pairs:
                    ahead = scores_of(p + 1)
                finish(p, scores)

        each_width(jnp.where(small_scores, count, 0), branch)
        pl.when(jnp.logical_not(small_scores))(partial(branch, TILES, False))
        return carry

    lax.fori_loop(0, TILES, step, 0)
    live = 1.0 - query_marks[:1, :].astype(jnp.float32)
    for p in range(pairs):
        lanes = slice(p * PAIR, (p + 1) * PAIR)
        out_ref[:, lanes] = (mixed_t[lanes, :] * live).astype(jnp.bfloat16).T


def attend(edges, core, x, own, other, segments):
    rows, depth = x.shape
    half = own[0].shape[1]
    width = 2 * half
    seqs, pairs = rows // LEN, width // PAIR
    return call(
        attend_kernel, "attend", (seqs,),
        [
            (x, (LEN, depth), lambda s, *_: (s, 0)),
            *own,
            *other,
            (segments.reshape(1, -1), (1, LEN), lambda s, _, core: (0, core[0] * seqs + s)),
        ],
        [
            ((rows, 3 * width), jnp.bfloat16, (LEN, 3 * width), lambda s, *_: (s, 0)),
            ((rows, width), jnp.bfloat16, (LEN, width), lambda s, *_: (s, 0)),
            (
                (seqs, pairs, TILES, 2 * TILE), jnp.float32, (1, pairs, TILES, 2 * TILE),
                lambda s, *_: (s, 0, 0, 0),
            ),
            ((rows, TILE), jnp.bfloat16, (LEN, TILE), lambda s, *_: (s, 0)),
            ((MARKS, rows), jnp.bfloat16, (MARKS, LEN), lambda s, *_: (0, s)),
        ],
        scratch=[
            pltpu.VMEM((pairs, LEN, PAIR + TILE), jnp.bfloat16),
            pltpu.VMEM((width, LEN), jnp.bfloat16),
            pltpu.VMEM((pairs, TILES, PAIR + TILE, 2 * TILE), jnp.bfloat16),
            pltpu.VMEM((width, LEN), jnp.float32),
        ],
        scalars=(edges, core),
        flops=2 * rows * (3 * width * depth + 2 * width * LEN),
        vmem=VM_ATT,
    )


def attend_back_kernel(
    edges, where, qkv_hbm, g_hbm, o_hbm, key_marks, query_marks, lse_ref, out_hbm,
    q_ref, k_ref, v_ref, g_ref, o_ref, out_ref, kcat, vcat, kt, qt, gt, dk, dv, dqt, arrived, left,
):
    base = where[1] * TILES
    width = q_ref.shape[1]
    pairs = width // PAIR
    groups = pairs // 2
    rows = pl.ds(pl.multiple_of(where[0] * LEN, LEN), LEN)
    k_copy, v_copy, q_copy, g_copy, o_copy = (
        pltpu.make_async_copy(source, target, arrived.at[n])
        for n, (source, target) in enumerate(
            (
                (qkv_hbm.at[rows, pl.ds(width, width)], k_ref),
                (qkv_hbm.at[rows, pl.ds(2 * width, width)], v_ref),
                (qkv_hbm.at[rows, pl.ds(0, width)], q_ref),
                (g_hbm.at[rows, :], g_ref),
                (o_hbm.at[rows, :], o_ref),
            )
        )
    )
    for copy in (k_copy, v_copy, q_copy, g_copy, o_copy):
        copy.start()

    def place(p, what):
        at = (((p % groups) * 2 + p // groups) * 3 + what) * PAIR
        return slice(at, at + PAIR)

    def negated(row):
        return [part.astype(jnp.float32) for part in three_parts(-row)]

    qt[...] = jnp.zeros_like(qt)
    gt[...] = jnp.zeros_like(gt)
    dk[...] = jnp.zeros_like(dk)
    dv[...] = jnp.zeros_like(dv)
    for p in range(pairs):
        kcat[p, :, PAIR:] = key_marks[...]
        vcat[p, :, PAIR:] = key_marks[...]
    k_copy.wait()
    for p in range(pairs):
        lanes = slice(p * PAIR, (p + 1) * PAIR)
        kcat[p, :, :PAIR] = k_ref[:, lanes]
        kt[lanes, :] = k_ref[:, lanes].T
    v_copy.wait()
    for p in range(pairs):
        vcat[p, :, :PAIR] = v_ref[:, p * PAIR : (p + 1) * PAIR]
    q_copy.wait()
    g_copy.wait()
    o_copy.wait()
    pad = jnp.zeros((MARKS - LSE_ROW - 3, 2 * TILE), jnp.float32)
    none = jnp.zeros((LSE_ROW, 2 * TILE), jnp.float32)
    for p in range(pairs):
        lanes = slice(p * PAIR, (p + 1) * PAIR)
        for i in range(TILES):
            cols = slice(i * TILE, (i + 1) * TILE)
            fill_block(qt, p, i, (q_ref[cols, lanes] * jnp.bfloat16(HD**-0.5)).T)
            grad_t = g_ref[cols, lanes].T
            fill_block(gt, p, i, grad_t)
            agree = grad_t.astype(jnp.float32) * o_ref[cols, lanes].T.astype(jnp.float32)
            delta = jnp.concatenate(
                [
                    jnp.sum(agree[:HD], axis=0, keepdims=True),
                    jnp.sum(agree[HD:], axis=0, keepdims=True),
                ],
                axis=1,
            )
            marks = query_marks[:LSE_ROW, cols].astype(jnp.float32)
            marks = jnp.concatenate([marks, marks], axis=1)
            lse = lse_ref[0, p, i : i + 1, :]
            qt[p, i, PAIR : PAIR + MARKS, :] = jnp.concatenate(
                [marks, *negated(lse), pad], axis=0
            ).astype(jnp.bfloat16)
            gt[p, i, PAIR : PAIR + MARKS, :] = jnp.concatenate(
                [none, *negated(delta), pad], axis=0
            ).astype(jnp.bfloat16)

    def step(i, carry):
        at = pl.multiple_of(i * TILE, TILE)
        first, count = key_range(edges, base, i)
        start = pl.multiple_of(first * TILE, TILE)

        def branch(width):
            at_keys = pl.ds(start, width * TILE)

            def head(p):
                scores = dot(kcat[p, at_keys, :], qt[p, i])
                grad_probs = dot(vcat[p, at_keys, :], gt[p, i])
                return scores, grad_probs

            def finish(p, scores, grad_probs):
                lanes = slice(p * PAIR, (p + 1) * PAIR)
                query = q_ref[pl.ds(at, TILE), lanes] * jnp.bfloat16(HD**-0.5)
                grad = g_ref[pl.ds(at, TILE), lanes]
                probs = jnp.exp(scores)
                grad_scores = (probs * grad_probs).astype(jnp.bfloat16)
                dv[p, at_keys, :] += dot(probs.astype(jnp.bfloat16), split_lanes(grad))
                dk[p, at_keys, :] += dot(grad_scores, split_lanes(query))
                dqt[lanes, pl.ds(at, TILE)] = halves_of(dot(kt[lanes, at_keys], grad_scores))

            ahead = head(0)
            for p in range(pairs):
                now = ahead
                if p + 1 < pairs:
                    ahead = head(p + 1)
                finish(p, *now)

        each_width(count, branch)
        return carry

    lax.fori_loop(0, TILES, step, 0)
    copies = []
    for g in range(groups):
        for p in (g, g + groups):
            lanes = slice(p * PAIR, (p + 1) * PAIR)
            out_ref[:, place(p, 0)] = (dqt[lanes, :] * HD**-0.5).astype(jnp.bfloat16).T
            out_ref[:, place(p, 1)] = dk[p].astype(jnp.bfloat16)
            out_ref[:, place(p, 2)] = dv[p].astype(jnp.bfloat16)
            cols = pl.ds(place(p, 0).start, 3 * PAIR)
            copies.append(
                pltpu.make_async_copy(out_ref.at[:, cols], out_hbm.at[:, cols], left.at[p])
            )
            copies[-1].start()
    for copy in copies:
        copy.wait()


def attend_back(qkv, gheads, heads, key_marks, query_marks, lse, core, seq, edges):
    rows, width = heads.shape
    seqs, pairs = rows // LEN, width // PAIR
    where = jnp.concatenate([jnp.full((1,), seq, jnp.int32), core * seqs + seq])
    by_seq = lambda i, _, where: (where[0], 0)
    block = pltpu.VMEM((LEN, width), jnp.bfloat16)
    return call(
        attend_back_kernel, "attend_back", (1,),
        [
            (qkv, None, None),
            (gheads, None, None),
            (heads, None, None),
            (key_marks, (LEN, TILE), by_seq),
            (query_marks, (MARKS, LEN), lambda i, _, where: (0, where[0])),
            (lse, (1, pairs, TILES, 2 * TILE), lambda i, _, where: (where[0], 0, 0, 0)),
        ],
        [((LEN, 3 * width), jnp.bfloat16, None, None)],
        scratch=[
            *[block] * 5,
            pltpu.VMEM((LEN, 3 * width), jnp.bfloat16),
            pltpu.VMEM((pairs, LEN, PAIR + TILE), jnp.bfloat16),
            pltpu.VMEM((pairs, LEN, PAIR + TILE), jnp.bfloat16),
            pltpu.VMEM((width, LEN), jnp.bfloat16),
            pltpu.VMEM((pairs, TILES, PAIR + TILE, 2 * TILE), jnp.bfloat16),
            pltpu.VMEM((pairs, TILES, PAIR + TILE, 2 * TILE), jnp.bfloat16),
            pltpu.VMEM((pairs, LEN, PAIR), jnp.float32),
            pltpu.VMEM((pairs, LEN, PAIR), jnp.float32),
            pltpu.VMEM((width, LEN), jnp.float32),
            pltpu.SemaphoreType.DMA((5,)),
            pltpu.SemaphoreType.DMA((pairs,)),
        ],
        scalars=(edges, where),
        flops=10 * LEN * width * LEN,
        vmem=VM_BACK,
    )[0]


def project_back_kernel(seqs, x_ref, *refs):
    grads = refs[:seqs]
    out_a, out_b, sums, own_ref, other_ref, x_t = refs[seqs:]
    step = pl.program_id(0)

    @pl.when(step == 0)
    def _():
        x_t[...] = x_ref[...].T

        start = grads[0].shape[1] * pl.num_programs(0) // 2
        both = jnp.concatenate([sums[...], jnp.zeros_like(sums)], axis=0)
        end = start + out_a.shape[0]
        for buf, out_grad in ((own_ref, out_a), (other_ref, out_b)):
            buf[start:end, :] = out_grad[...]
            buf[end : end + MARKS, :] = both.astype(jnp.bfloat16)
            if end + MARKS < buf.shape[0]:
                rest = (buf.shape[0] - end - MARKS, buf.shape[1])
                buf[end + MARKS :, :] = jnp.zeros(rest, jnp.bfloat16)

    part = dot(x_t[:, :LEN], grads[0][...])
    for s in range(1, seqs):
        part = part + dot(x_t[:, s * LEN : (s + 1) * LEN], grads[s][...])
    depth = part.shape[0]
    for n, buf in enumerate((own_ref, other_ref)):

        @pl.when(step % 2 == n)
        def _():
            for m in range(3):
                rows = pl.ds(pl.multiple_of((step // 2 * 3 + m) * PAIR, PAIR), PAIR)
                for r in range(depth // PAIR):
                    buf[rows, r * PAIR : (r + 1) * PAIR] = part[
                        r * PAIR : (r + 1) * PAIR, m * PAIR : (m + 1) * PAIR
                    ].astype(jnp.bfloat16)


def project_back(x, grads, extra, height):
    rows, depth = x.shape
    wide = grads[0].shape[1]
    size = 3 * PAIR
    buf = ((height, depth), jnp.bfloat16, (height, depth), lambda i: (0, 0))
    return call(
        partial(project_back_kernel, len(grads)), "project_back", (wide // size,),
        [x, *((grad, (LEN, size), lambda i: (0, i)) for grad in grads), *extra],
        [buf, buf],
        scratch=[pltpu.VMEM((depth, rows), jnp.bfloat16)],
        flops=2 * rows * depth * wide,
        vmem=VM_PROJ,
    )


def stream_kernel(gfirst, grad, *refs):
    weights, out, table = refs[:6], refs[-2], refs[-1]

    @pl.when(pl.program_id(0) == 0)
    def _():
        count = len(weights)
        for n, weight in enumerate(weights):
            for g in range(weight.shape[1] // PAIR):
                at = (g * count + n) * PAIR
                table[:, at : at + PAIR] = weight[:, g * PAIR : (g + 1) * PAIR]

    out[...] = gfirst[...] + dot_nt(grad[...], table[...])


def stream(gfirst, grad, own, other, seq, before=None):
    rows, depth = gfirst.shape
    wide = grad.shape[1]
    per = LEN // BLOCK
    of_seq = lambda i: (seq * per + i, 0)
    ins = [(gfirst, (BLOCK, depth), of_seq), (grad, (BLOCK, wide), rows_of), *own, *other]
    aliases = {}
    if before is not None:
        aliases[len(ins)] = 0
        ins.append((before, None, None))
    return call(
        stream_kernel, "stream", (per,), ins,
        [((rows, depth), jnp.float32, (BLOCK, depth), of_seq)],
        scratch=[pltpu.VMEM((depth, wide), jnp.bfloat16)],
        aliases=aliases,
        flops=2 * LEN * depth * wide,
        vmem=VM_STREAM,
    )[0]


def swap_cores(block):
    return lax.ppermute(block, "mp", [(0, 1), (1, 0)])


def stages_of(chips, radices):
    me, core = lax.axis_index("dp"), lax.axis_index("mp")

    def pairs(masks):
        return [(2 * c + i, 2 * (c ^ masks[i]) + i) for c in range(chips) for i in range(2)]

    stages = []
    bit = 0
    if radices[:2] == (2, 2):
        low, high = me & 1, (me >> 1) & 1
        stages = [
            (jnp.where(core == 0, low, high), 2, [pairs((1, 2))]),
            (jnp.where(core == 0, high, low), 2, [pairs((2, 1))]),
        ]
        bit = 2
        radices = radices[2:]
    while 1 << bit < chips:
        radix = min(radices[0], chips >> bit)
        radices = radices[1:] or radices
        ways = [pairs((j << bit, j << bit)) for j in range(1, radix)]
        stages.append(((me >> bit) & (radix - 1), radix, ways))
        bit += radix // 2
    return stages


def send(block, pairs):
    return lax.ppermute(block, ("dp", "mp"), pairs)


def part(block, which, rows):
    return lax.dynamic_slice_in_dim(block, which * rows, rows)


def added(blocks):
    total = blocks[0].astype(jnp.float32)
    for block in blocks[1:]:
        total = total + block.astype(jnp.float32)
    return total.astype(jnp.bfloat16)


def unpack_kernel(size, shapes, places, *refs):
    pieces, outs, table = refs[: -len(shapes) - 1], refs[-len(shapes) - 1 : -1], refs[-1]
    at = 0
    for piece in pieces:
        block = piece[...].astype(jnp.float32)
        for n in range(block.shape[0] // size):
            table[pl.ds(pl.multiple_of(places[at] * size, size), size), :] = block[
                n * size : (n + 1) * size
            ]
            at += 1
    row = 0
    depth = table.shape[1]
    for out, (kind, height, width) in zip(outs, shapes):
        if kind == "rows":
            out[...] = table[row : row + height, :]
            row += height
        elif kind == "wide":
            for n in range(width // depth):
                out[:, n * depth : (n + 1) * depth] = table[row : row + height, :]
                row += height
        else:
            base, count = kind
            for g in range(width // PAIR):
                at = (g * count + base) * PAIR
                for n in range(height // PAIR):
                    out[n * PAIR : (n + 1) * PAIR, g * PAIR : (g + 1) * PAIR] = table[
                        at : at + PAIR, n * PAIR : (n + 1) * PAIR
                    ]
                row += PAIR


def unpack(pieces, places, shapes, rows, chips):
    depth = pieces[0].shape[1]
    size = rows // chips
    return call(
        partial(unpack_kernel, size, shapes), "unpack", (1,), pieces,
        [((h, w), jnp.float32, (h, w), lambda i, _: (0, 0)) for _, h, w in shapes],
        scratch=[pltpu.VMEM((rows, depth), jnp.float32)],
        scalars=(places,),
        vmem=VM_UNPACK,
    )


def sum_everywhere(own, other, shapes, chips, radices):
    rows = own.shape[0]
    stages = stages_of(chips, radices)
    cores = [(2 * c + i, 2 * c + 1 - i) for c in range(chips) for i in range(2)]
    addends = [own, *(yield [(other, cores)])]
    height = rows
    for digit, radix, ways in stages:
        height //= radix
        got = yield [
            (added([part(a, digit ^ (j + 1), height) for a in addends]), pairs)
            for j, pairs in enumerate(ways)
        ]
        addends = [part(a, digit, height) for a in addends] + got
    pieces = [added(addends)]
    places = [jnp.int32(0)]
    for n, (digit, radix, ways) in enumerate(reversed(stages)):
        weight = chips
        for _, earlier, _ in stages[: len(stages) - n]:
            weight //= earlier
        held = pieces[0] if len(pieces) == 1 else jnp.concatenate(pieces)
        pieces = [held] + (yield [(held, pairs) for pairs in ways])
        places = [p + (digit ^ j) * weight for j in range(radix) for p in places]
    return unpack(pieces, jnp.stack(places).astype(jnp.int32), shapes, rows, chips)


class Chain:
    def __init__(self, steps):
        self.steps, self.result = steps, None
        self.wishes = next(steps)

    def take(self, got):
        try:
            self.wishes = self.steps.send(got)
        except StopIteration as end:
            self.wishes, self.result = [], end.value


def advance(chains, work=None, token=None, beside=()):
    blocks = [block for chain in chains for block, _ in chain.wishes]
    if work is not None:
        *blocks, token = lax.optimization_barrier((*blocks, token))
    else:
        blocks = lax.optimization_barrier(blocks)
    ways = [pairs for chain in chains for _, pairs in chain.wishes]
    got = [send(block, pairs) for block, pairs in zip(blocks, ways)]
    out = None
    if work is not None:
        out = work(token)
        count = len(got)
        *got, last = lax.optimization_barrier((*got, out[-1], *beside))[: count + 1]
        out = (*out[:-1], last)
    for chain in chains:
        if chain.wishes:
            count = len(chain.wishes)
            chain.take(got[:count])
            got = got[count:]
    return out


def on_device(
    normed_in,
    dual_in,
    query_weight,
    key_weight,
    value_weight,
    output_weight,
    first_gain,
    first_bias,
    up_weight,
    down_weight,
    second_gain,
    second_bias,
    segments,
    grad_normed_out,
    grad_dual_out,
    chips,
):
    rows, depth = normed_in.shape
    core = lax.axis_index("mp")
    half, ff = query_weight.shape[1], up_weight.shape[1]
    own = (query_weight, key_weight, value_weight)
    other = tuple(swap_cores(w) for w in own)
    outs = (output_weight, swap_cores(output_weight))
    ups = (up_weight, swap_cores(up_weight))
    downs = (down_weight, swap_cores(down_weight))
    edges = tile_edges(segments)
    core = core.astype(jnp.int32).reshape(1)
    qkv, heads_out, log_totals, key_marks, query_marks = attend(
        edges, core, normed_in, own, other, segments
    )
    grain = 8 * chips

    def padded(count):
        return -(-count // grain) * grain

    row = lambda v: v.reshape(1, depth)
    normed_out, dual_out, grad_first, grad_heads, ffn_own, ffn_other, *extra = layer(
        heads_out, normed_in, dual_in, grad_normed_out, grad_dual_out, key_marks, outs, ups, downs,
        row(first_gain), row(first_bias), row(second_gain), row(second_bias),
    )
    back = partial(
        attend_back, qkv, grad_heads, heads_out, key_marks, query_marks, log_totals, core
    )
    fed = Chain(
        sum_everywhere(
            ffn_own, ffn_other,
            [("rows", ff, depth), ("wide", depth, ff)], chips, (2, 2, 4)
        )
    )
    grad_qkv = []
    for seq in range(rows // LEN):
        grad_qkv += advance([fed], lambda token: (back(seq, token),), edges)
    height = padded(3 * half + half + MARKS)
    own_grads, other_grads = advance(
        [fed], lambda x: project_back(x, grad_qkv, extra, height), normed_in
    )
    rest = Chain(
        sum_everywhere(
            own_grads, other_grads,
            [((n, 3), depth, half) for n in range(3)]
            + [("rows", half, depth)] + [("rows", 1, depth)] * 4,
            chips, (4,),
        )
    )
    advance([fed, rest])
    chains, grad_stream = [fed, rest], None
    for seq, grad in enumerate(grad_qkv):
        last = seq == len(grad_qkv) - 1
        while last and fed.wishes:
            advance(chains)
        (grad_stream,) = advance(
            chains,
            lambda token: (stream(token, grad, own, other, seq, grad_stream),),
            grad_first,
            fed.result[:1] if last else (),
        )
    down_total, up_total = fed.result
    query_total, key_total, value_total, output_total, *small = rest.result
    small = [total.reshape(depth) for total in small]
    return (
        normed_out,
        dual_out,
        grad_stream,
        query_total,
        key_total,
        value_total,
        output_total,
        small[0],
        small[1],
        up_total,
        down_total,
        small[2],
        small[3],
    )


def solution(mesh):
    rows = P(("dp", "mp"), None)
    columns = P(None, "mp")
    return jax.shard_map(
        partial(on_device, chips=mesh.shape["dp"]),
        mesh=mesh,
        in_specs=(
            rows, rows, columns, columns, columns, P("mp", None), P(), P(),
            columns, P("mp", None), P(), P(), P("dp"), rows, rows,
        ),
        out_specs=(
            rows, rows, rows, columns, columns, columns, P("mp", None), P(), P(),
            columns, P("mp", None), P(), P(),
        ),
        check_vma=False,
    )
```

```python
import math
from functools import partial

import jax
import jax.numpy as jnp
from jax import lax
from jax.experimental import pallas as pl
from jax.experimental.pallas import tpu as pltpu
from jax.sharding import PartitionSpec as P

norm_eps = 1e-05
BLOCK = 512
GATE = 0.7978845608028654
CUBE = 0.044715
SAFE = 3600.0
LAYER_BLOCK, SLOPE_TYPE = 256, jnp.float32
VM_ATT, VM_LAYER, VM_BACK, VM_PROJ, VM_STREAM, VM_UNPACK = 56, 56, 56, 56, 56, 56
HD = 64
LEN = 1024
TILE = 128
TILES = LEN // TILE
PAIR = 2 * HD
FAR = -1e30
MARKS = 16
LSE_ROW = 8
LIVE_LANE = 12
MIB = 2**20


def dot(left, right):
    return jnp.dot(left, right, preferred_element_type=jnp.float32)


def three_parts(row):
    high = row.astype(jnp.bfloat16)
    rest = row - high.astype(jnp.float32)
    mid = rest.astype(jnp.bfloat16)
    low = (rest - mid.astype(jnp.float32)).astype(jnp.bfloat16)
    return high, mid, low


def label_marks(labels):
    row = lax.broadcasted_iota(jnp.int32, (TILE, labels.shape[1]), 0)
    same = labels == row
    ones = (row < LSE_ROW + 3) | ((row == LIVE_LANE) & (labels != 0))
    keys = jnp.where(row < LSE_ROW, jnp.where(same, 0.0, FAR), jnp.where(ones, 1.0, 0.0))
    queries = jnp.where(same & (row < LSE_ROW), 1.0, 0.0)[:MARKS]
    return keys.astype(jnp.bfloat16).T, queries.astype(jnp.bfloat16)


def key_range(labels, base, i):
    def head(j):
        return labels[(base + j) * TILE]

    def tail(j):
        return labels[(base + j) * TILE + TILE - 1]

    low, high = head(i), tail(i)
    first, last = i, i
    for j in reversed(range(TILES)):
        first = jnp.where((j < i) & (tail(j) == low), j, first)
    for j in range(TILES):
        last = jnp.where((j > i) & (head(j) == high), j, last)
    return first, last - first + 1


def halves_of(block):
    return jnp.concatenate([block[:HD, :TILE], block[HD:, TILE:]], axis=0)


def split_lanes(tile):
    lane = lax.broadcasted_iota(jnp.int32, tile.shape, 1)
    zero = jnp.zeros_like(tile)
    return jnp.concatenate(
        [jnp.where(lane < HD, tile, zero), jnp.where(lane < HD, zero, tile)], axis=0
    )


def each_width(count, branch):
    for width in range(1, TILES + 1):
        pl.when(count == width)(partial(branch, width))


def dot_nt(left, right):
    return lax.dot_general(
        left, right, (((1,), (1,)), ((), ())), preferred_element_type=jnp.float32
    )


def dot_tn(left, right):
    return lax.dot_general(
        left, right, (((0,), (0,)), ((), ())), preferred_element_type=jnp.float32
    )


def full(ref):
    shape = ref.shape
    return pl.BlockSpec(shape, lambda *_: (0,) * len(shape), pipeline_mode=pl.Buffered(1))


def call(kernel, name, grid, ins, outs, scratch=(), scalars=(), flops=0, aliases=None, vmem=56):
    specs, arrays = [], []
    for item in ins:
        if isinstance(item, tuple):
            arrays.append(item[0])
            if item[1] is None:
                specs.append(pl.BlockSpec(memory_space=pl.ANY))
            else:
                specs.append(pl.BlockSpec(item[1], item[2]))
        else:
            arrays.append(item)
            specs.append(full(item))
    size = sum(a.size * a.dtype.itemsize for a in arrays)
    size += sum(jnp.dtype(d).itemsize * math.prod(s) for s, d, _, _ in outs)
    return pl.pallas_call(
        kernel,
        grid_spec=pltpu.PrefetchScalarGridSpec(
            num_scalar_prefetch=len(scalars),
            grid=grid,
            in_specs=specs,
            out_specs=[
                pl.BlockSpec(b, m) if b else pl.BlockSpec(memory_space=pl.ANY)
                for _, _, b, m in outs
            ],
            scratch_shapes=scratch,
        ),
        out_shape=[jax.ShapeDtypeStruct(s, d) for s, d, _, _ in outs],
        compiler_params=pltpu.CompilerParams(vmem_limit_bytes=vmem * MIB),
        cost_estimate=pl.CostEstimate(flops=flops, bytes_accessed=size, transcendentals=0),
        input_output_aliases=aliases or {},
        name=name,
    )(*scalars, *arrays)


def rows_of(i, *_):
    return (i, 0)


def stats(z):
    mean = jnp.mean(z, axis=-1, keepdims=True)
    centred = z - mean
    spread = jnp.mean(centred * centred, axis=-1, keepdims=True)
    scale = lax.rsqrt(spread + norm_eps)
    return centred * scale, scale


def norm_back(upstream, unit, scale, gain):
    t = upstream * gain
    inner = jnp.mean(t * unit, axis=-1, keepdims=True)
    return (t - jnp.mean(t, axis=-1, keepdims=True) - unit * inner) * scale


def layer_kernel(
    heads, x, dual, gn, gd, marks, out_a, out_b, up_a, up_b, down_a, down_b, g1, b1, g2, b2,
    normed_out, dual_out, gfirst_ref, gheads, ffn_grad_a, ffn_grad_b,
    out_grad_a, out_grad_b, sums,
    hid, slope, acc_up, acc_down, acc_out,
):
    i = pl.program_id(0)
    half = out_a.shape[0]
    ff = up_a.shape[1]
    chunk = 512

    @pl.when(i == 0)
    def _():
        sums[...] = jnp.zeros_like(sums)
        acc_up[...] = jnp.zeros_like(acc_up)
        acc_down[...] = jnp.zeros_like(acc_down)
        acc_out[...] = jnp.zeros_like(acc_out)

    attn = dot(heads[:, :half], out_a[...]) + dot(heads[:, half:], out_b[...])
    z1 = x[...].astype(jnp.float32) + attn
    unit, scale = stats(z1)
    normed = unit * g1[...] + b1[...]
    low = normed.astype(jnp.bfloat16)
    ffn = None
    for n, (up, down) in enumerate(((up_a, down_a), (up_b, down_b))):
        for c in range(ff // chunk):
            cols = slice(c * chunk, (c + 1) * chunk)
            at = slice(n * ff + c * chunk, n * ff + (c + 1) * chunk)
            v = dot(low, up[:, cols])
            square = v * v
            t = jnp.tanh(v * (GATE + (GATE * CUBE) * square))
            open_part = 0.5 + 0.5 * t
            hidden = (v * open_part).astype(jnp.bfloat16)
            hid[:, at] = hidden
            slope[:, at] = open_part + (v * (0.5 - 0.5 * t * t)) * (
                GATE + (3 * GATE * CUBE) * square
            )
            part = dot(hidden, down[cols, :])
            ffn = part if ffn is None else ffn + part
    unit2, scale2 = stats(normed + ffn)
    normed_out[...] = (unit2 * g2[...] + b2[...]).astype(jnp.bfloat16)
    dual_out[...] = (dual[...].astype(jnp.float32) + attn + ffn).astype(jnp.bfloat16)
    upstream = gn[...].astype(jnp.float32)
    gmid = norm_back(upstream, unit2, scale2, g2[...])
    gdual = gd[...].astype(jnp.float32)
    gffn = (gmid + gdual).astype(jnp.bfloat16)
    gffn_t = gffn.T
    low_t = low.T
    gnormed = gmid
    for n, (up, down) in enumerate(((up_a, down_a), (up_b, down_b))):
        for c in range(ff // chunk):
            cols = slice(c * chunk, (c + 1) * chunk)
            at = slice(n * ff + c * chunk, n * ff + (c + 1) * chunk)
            gpre = (dot_nt(gffn, down[cols, :]) * slope[:, at]).astype(jnp.bfloat16)
            acc_down[:, at] += dot(gffn_t, hid[:, at])
            acc_up[:, at] += dot(low_t, gpre)
            gnormed = gnormed + dot_nt(gpre, up[:, cols])
    gfirst = norm_back(gnormed, unit, scale, g1[...])
    gfirst_ref[...] = gfirst
    gattn = (gfirst + gdual).astype(jnp.bfloat16)
    sums[0:1, :] += jnp.sum(gnormed * unit, axis=0, keepdims=True)
    sums[1:2, :] += jnp.sum(gnormed, axis=0, keepdims=True)
    sums[2:3, :] += jnp.sum(upstream * unit2, axis=0, keepdims=True)
    sums[3:4, :] += jnp.sum(upstream, axis=0, keepdims=True)
    acc_out[...] += dot_tn(heads[...], gattn)
    live = marks[:, LIVE_LANE : LIVE_LANE + 1].astype(jnp.float32)
    gheads[:, :half] = (dot_nt(gattn, out_a[...]) * live).astype(jnp.bfloat16)
    gheads[:, half:] = (dot_nt(gattn, out_b[...]) * live).astype(jnp.bfloat16)

    @pl.when(i == pl.num_programs(0) - 1)
    def _():
        depth = acc_up.shape[0]
        for n, (ffn_grad, out_grad) in enumerate(
            ((ffn_grad_a, out_grad_a), (ffn_grad_b, out_grad_b))
        ):
            ffn_grad[:ff, :] = acc_down[:, n * ff : (n + 1) * ff].T.astype(jnp.bfloat16)
            for c in range(ff // depth):
                at = n * ff + c * depth
                ffn_grad[ff + c * depth : ff + (c + 1) * depth, :] = acc_up[
                    :, at : at + depth
                ].astype(jnp.bfloat16)
            out_grad[...] = acc_out[n * half : (n + 1) * half, :].astype(jnp.bfloat16)


def layer(heads, x, dual, gn, gd, marks, outs, ups, downs, g1, b1, g2, b2, block=BLOCK):
    rows, depth = x.shape
    ff, half = ups[0].shape[1], outs[0].shape[0]
    tall = ((rows, depth), jnp.bfloat16, (block, depth), rows_of)
    tall32 = ((rows, depth), jnp.float32, (block, depth), rows_of)

    def once(*shape, dtype=jnp.bfloat16):
        return (shape, dtype, shape, lambda i: (0, 0))

    return call(
        layer_kernel, "layer", (rows // block,),
        [(a, (block, a.shape[1]), rows_of) for a in (heads, x, dual, gn, gd, marks)]
        + [*outs, *ups, *downs, g1, b1, g2, b2],
        [tall, tall, tall32, tall, once(2 * ff, depth), once(2 * ff, depth),
         once(half, depth), once(half, depth), once(8, depth, dtype=jnp.float32)],
        scratch=[
            pltpu.VMEM((block, 2 * ff), jnp.bfloat16),
            pltpu.VMEM((block, 2 * ff), jnp.float32),
            pltpu.VMEM((depth, 2 * ff), jnp.float32),
            pltpu.VMEM((depth, 2 * ff), jnp.float32),
            pltpu.VMEM((2 * half, depth), jnp.float32),
        ],
        flops=2 * rows * depth * (3 * depth + 12 * ff),
        vmem=VM_LAYER,
    )


def fill_block(table, p, i, tile_t):
    table[p, i, :HD, :TILE] = tile_t[:HD]
    table[p, i, HD:PAIR, TILE:] = tile_t[HD:]


def score_bound(qkv, width):
    row = lax.broadcasted_iota(jnp.int32, (width, TILE), 0)
    head = lax.broadcasted_iota(jnp.int32, (width, TILE), 1)
    heads = (row // HD == head).astype(jnp.bfloat16)
    largest = []
    for at in (0, width):
        block = qkv[:, at : at + width].astype(jnp.float32)
        norms = dot((block * block).astype(jnp.bfloat16), heads)
        largest.append(jnp.max(norms, axis=0, keepdims=True))
    return jnp.max(largest[0] * largest[1]) * (1.02 / HD)


def attend_kernel(
    edges, core, x_ref, qa, ka, va, qb, kb, vb, labels,
    qkv_hbm, out_ref, lse_ref, key_marks, query_marks, qkv_ref, kcat, vt, qt, mixed_t, left,
):
    seq = pl.program_id(0)
    base = (core[0] * pl.num_programs(0) + seq) * TILES
    key_marks[...], query_marks[...] = label_marks(labels[...])
    half = qa.shape[1]
    width = 2 * half
    pairs = width // PAIR
    x = x_ref[...]

    @pl.when(seq == 0)
    def _():
        qt[...] = jnp.zeros_like(qt)

    for n, w in enumerate((qa, qb, ka, kb, va, vb)):
        qkv_ref[:, n * half : (n + 1) * half] = dot(x, w[...]).astype(jnp.bfloat16)
    rows = pl.ds(pl.multiple_of(seq * LEN, LEN), LEN)
    leaving = pltpu.make_async_copy(qkv_ref, qkv_hbm.at[rows, :], left)
    leaving.start()
    small_scores = score_bound(qkv_ref, width) < SAFE
    for p in range(pairs):
        lanes = slice(p * PAIR, (p + 1) * PAIR)
        kcat[p, :, :PAIR] = qkv_ref[:, width + p * PAIR : width + (p + 1) * PAIR]
        kcat[p, :, PAIR:] = key_marks[...]
        vt[lanes, :] = qkv_ref[:, 2 * width + p * PAIR : 2 * width + (p + 1) * PAIR].T
        for i in range(TILES):
            cols = slice(i * TILE, (i + 1) * TILE)
            fill_block(qt, p, i, (qkv_ref[cols, lanes] * jnp.bfloat16(HD**-0.5)).T)
            qt[p, i, PAIR : PAIR + MARKS, :TILE] = query_marks[:, cols]
            qt[p, i, PAIR : PAIR + MARKS, TILE:] = query_marks[:, cols]

    def step(i, carry):
        at = pl.multiple_of(i * TILE, TILE)
        first, count = key_range(edges, base, i)
        first = jnp.where(small_scores, first, 0)
        start = pl.multiple_of(first * TILE, TILE)

        def branch(width, small=True):
            at_keys = pl.ds(start, width * TILE)

            def scores_of(p):
                return dot(kcat[p, at_keys, :], qt[p, i])

            def finish(p, scores):
                top = None
                if not small:
                    top = jnp.max(scores, axis=0, keepdims=True)
                    scores = scores - top
                probs = jnp.exp(scores)
                total = jnp.sum(probs, axis=0, keepdims=True)
                mixed = dot(vt[p * PAIR : (p + 1) * PAIR, at_keys], probs.astype(jnp.bfloat16))
                mixed_t[p * PAIR : (p + 1) * PAIR, pl.ds(at, TILE)] = halves_of(mixed / total)
                log_total = jnp.log(total)
                lse_ref[0, p, pl.ds(i, 1), :] = log_total if small else top + log_total

            ahead = scores_of(0)
            for p in range(pairs):
                scores = ahead
                if p + 1 < pairs:
                    ahead = scores_of(p + 1)
                finish(p, scores)

        each_width(jnp.where(small_scores, count, 0), branch)
        pl.when(jnp.logical_not(small_scores))(partial(branch, TILES, False))
        return carry

    lax.fori_loop(0, TILES, step, 0)
    live = 1.0 - query_marks[:1, :].astype(jnp.float32)
    for p in range(pairs):
        lanes = slice(p * PAIR, (p + 1) * PAIR)
        out_ref[:, lanes] = (mixed_t[lanes, :] * live).astype(jnp.bfloat16).T
    leaving.wait()


def attend(edges, core, x, own, other, segments):
    rows, depth = x.shape
    half = own[0].shape[1]
    width = 2 * half
    seqs, pairs = rows // LEN, width // PAIR
    return call(
        attend_kernel, "attend", (seqs,),
        [
            (x, (LEN, depth), lambda s, *_: (s, 0)),
            *own,
            *other,
            (segments.reshape(1, -1), (1, LEN), lambda s, _, core: (0, core[0] * seqs + s)),
        ],
        [
            ((rows, 3 * width), jnp.bfloat16, None, None),
            ((rows, width), jnp.bfloat16, (LEN, width), lambda s, *_: (s, 0)),
            (
                (seqs, pairs, TILES, 2 * TILE), jnp.float32, (1, pairs, TILES, 2 * TILE),
                lambda s, *_: (s, 0, 0, 0),
            ),
            ((rows, TILE), jnp.bfloat16, (LEN, TILE), lambda s, *_: (s, 0)),
            ((MARKS, rows), jnp.bfloat16, (MARKS, LEN), lambda s, *_: (0, s)),
        ],
        scratch=[
            pltpu.VMEM((LEN, 3 * width), jnp.bfloat16),
            pltpu.VMEM((pairs, LEN, PAIR + TILE), jnp.bfloat16),
            pltpu.VMEM((width, LEN), jnp.bfloat16),
            pltpu.VMEM((pairs, TILES, PAIR + TILE, 2 * TILE), jnp.bfloat16),
            pltpu.VMEM((width, LEN), jnp.float32),
            pltpu.SemaphoreType.DMA,
        ],
        scalars=(edges, core),
        flops=2 * rows * (3 * width * depth + 2 * width * LEN),
        vmem=VM_ATT,
    )


def attend_back_kernel(
    edges, core, seq, qkv_hbm, g_hbm, o_hbm, key_marks, query_marks, lse_ref, out_hbm,
    q_ref, k_ref, v_ref, g_ref, o_ref, out_ref, kcat, vcat, kt, qt, gt, dk, dv, dqt, arrived, left,
):
    base = (core[0] * (qkv_hbm.shape[0] // LEN) + seq[0]) * TILES
    width = q_ref.shape[1]
    pairs = width // PAIR
    groups = pairs // 2
    rows = pl.ds(pl.multiple_of(seq[0] * LEN, LEN), LEN)
    k_copy, v_copy, q_copy, g_copy, o_copy = (
        pltpu.make_async_copy(source, target, arrived.at[n])
        for n, (source, target) in enumerate(
            (
                (qkv_hbm.at[rows, pl.ds(width, width)], k_ref),
                (qkv_hbm.at[rows, pl.ds(2 * width, width)], v_ref),
                (qkv_hbm.at[rows, pl.ds(0, width)], q_ref),
                (g_hbm.at[rows, :], g_ref),
                (o_hbm.at[rows, :], o_ref),
            )
        )
    )
    for copy in (k_copy, v_copy, q_copy, g_copy, o_copy):
        copy.start()

    def place(p, what):
        at = (((p % groups) * 2 + p // groups) * 3 + what) * PAIR
        return slice(at, at + PAIR)

    def negated(row):
        return [part.astype(jnp.float32) for part in three_parts(-row)]

    qt[...] = jnp.zeros_like(qt)
    gt[...] = jnp.zeros_like(gt)
    dk[...] = jnp.zeros_like(dk)
    dv[...] = jnp.zeros_like(dv)
    for p in range(pairs):
        kcat[p, :, PAIR:] = key_marks[...]
        vcat[p, :, PAIR:] = key_marks[...]
    k_copy.wait()
    for p in range(pairs):
        lanes = slice(p * PAIR, (p + 1) * PAIR)
        kcat[p, :, :PAIR] = k_ref[:, lanes]
        kt[lanes, :] = k_ref[:, lanes].T
    v_copy.wait()
    for p in range(pairs):
        vcat[p, :, :PAIR] = v_ref[:, p * PAIR : (p + 1) * PAIR]
    q_copy.wait()
    g_copy.wait()
    o_copy.wait()
    pad = jnp.zeros((MARKS - LSE_ROW - 3, 2 * TILE), jnp.float32)
    none = jnp.zeros((LSE_ROW, 2 * TILE), jnp.float32)
    for p in range(pairs):
        lanes = slice(p * PAIR, (p + 1) * PAIR)
        for i in range(TILES):
            cols = slice(i * TILE, (i + 1) * TILE)
            fill_block(qt, p, i, (q_ref[cols, lanes] * jnp.bfloat16(HD**-0.5)).T)
            grad_t = g_ref[cols, lanes].T
            fill_block(gt, p, i, grad_t)
            agree = grad_t.astype(jnp.float32) * o_ref[cols, lanes].T.astype(jnp.float32)
            delta = jnp.concatenate(
                [
                    jnp.sum(agree[:HD], axis=0, keepdims=True),
                    jnp.sum(agree[HD:], axis=0, keepdims=True),
                ],
                axis=1,
            )
            marks = query_marks[:LSE_ROW, cols].astype(jnp.float32)
            marks = jnp.concatenate([marks, marks], axis=1)
            lse = lse_ref[0, p, i : i + 1, :]
            qt[p, i, PAIR : PAIR + MARKS, :] = jnp.concatenate(
                [marks, *negated(lse), pad], axis=0
            ).astype(jnp.bfloat16)
            gt[p, i, PAIR : PAIR + MARKS, :] = jnp.concatenate(
                [none, *negated(delta), pad], axis=0
            ).astype(jnp.bfloat16)

    def step(i, carry):
        at = pl.multiple_of(i * TILE, TILE)
        first, count = key_range(edges, base, i)
        start = pl.multiple_of(first * TILE, TILE)

        def branch(width):
            at_keys = pl.ds(start, width * TILE)

            def head(p):
                scores = dot(kcat[p, at_keys, :], qt[p, i])
                grad_probs = dot(vcat[p, at_keys, :], gt[p, i])
                return scores, grad_probs

            def finish(p, scores, grad_probs):
                lanes = slice(p * PAIR, (p + 1) * PAIR)
                query = q_ref[pl.ds(at, TILE), lanes] * jnp.bfloat16(HD**-0.5)
                grad = g_ref[pl.ds(at, TILE), lanes]
                probs = jnp.exp(scores)
                grad_scores = (probs * grad_probs).astype(jnp.bfloat16)
                dv[p, at_keys, :] += dot(probs.astype(jnp.bfloat16), split_lanes(grad))
                dk[p, at_keys, :] += dot(grad_scores, split_lanes(query))
                dqt[lanes, pl.ds(at, TILE)] = halves_of(dot(kt[lanes, at_keys], grad_scores))

            ahead = head(0)
            for p in range(pairs):
                now = ahead
                if p + 1 < pairs:
                    ahead = head(p + 1)
                finish(p, *now)

        each_width(count, branch)
        return carry

    lax.fori_loop(0, TILES, step, 0)
    copies = []
    for g in range(groups):
        for p in (g, g + groups):
            lanes = slice(p * PAIR, (p + 1) * PAIR)
            out_ref[:, place(p, 0)] = (dqt[lanes, :] * HD**-0.5).astype(jnp.bfloat16).T
            out_ref[:, place(p, 1)] = dk[p].astype(jnp.bfloat16)
            out_ref[:, place(p, 2)] = dv[p].astype(jnp.bfloat16)
            cols = pl.ds(place(p, 0).start, 3 * PAIR)
            copies.append(
                pltpu.make_async_copy(out_ref.at[:, cols], out_hbm.at[:, cols], left.at[p])
            )
            copies[-1].start()
    for copy in copies:
        copy.wait()


def attend_back(qkv, gheads, heads, key_marks, query_marks, lse, core, seq, edges):
    rows, width = heads.shape
    seqs, pairs = rows // LEN, width // PAIR
    by_seq = lambda i, edges, core, seq: (seq[0], 0)
    block = pltpu.VMEM((LEN, width), jnp.bfloat16)
    return call(
        attend_back_kernel, "attend_back", (1,),
        [
            (qkv, None, None),
            (gheads, None, None),
            (heads, None, None),
            (key_marks, (LEN, TILE), by_seq),
            (query_marks, (MARKS, LEN), lambda i, edges, core, seq: (0, seq[0])),
            (lse, (1, pairs, TILES, 2 * TILE), lambda i, edges, core, seq: (seq[0], 0, 0, 0)),
        ],
        [((LEN, 3 * width), jnp.bfloat16, None, None)],
        scratch=[
            *[block] * 5,
            pltpu.VMEM((LEN, 3 * width), jnp.bfloat16),
            pltpu.VMEM((pairs, LEN, PAIR + TILE), jnp.bfloat16),
            pltpu.VMEM((pairs, LEN, PAIR + TILE), jnp.bfloat16),
            pltpu.VMEM((width, LEN), jnp.bfloat16),
            pltpu.VMEM((pairs, TILES, PAIR + TILE, 2 * TILE), jnp.bfloat16),
            pltpu.VMEM((pairs, TILES, PAIR + TILE, 2 * TILE), jnp.bfloat16),
            pltpu.VMEM((pairs, LEN, PAIR), jnp.float32),
            pltpu.VMEM((pairs, LEN, PAIR), jnp.float32),
            pltpu.VMEM((width, LEN), jnp.float32),
            pltpu.SemaphoreType.DMA((5,)),
            pltpu.SemaphoreType.DMA((pairs,)),
        ],
        scalars=(edges, core, jnp.full((1,), seq, jnp.int32)),
        flops=10 * LEN * width * LEN,
        vmem=VM_BACK,
    )[0]


def project_back_kernel(seqs, x_hbm, *refs):
    grads = refs[:seqs]
    out_a, out_b, sums, own_ref, other_ref, x_ref, x_t, g_ref, arrived = refs[seqs:]
    size = 6 * PAIR
    chunks = g_ref.shape[1] // size
    x_copies, g_copies = [], []
    for s in range(seqs):
        rows = slice(s * LEN, (s + 1) * LEN)
        x_copies.append(
            pltpu.make_async_copy(x_hbm.at[rows, :], x_ref.at[rows, :], arrived.at[s])
        )
    for c in range(chunks):
        cols = pl.ds(c * size, size)
        g_copies.append(
            [
                pltpu.make_async_copy(
                    grads[s].at[:, cols],
                    g_ref.at[s * LEN : (s + 1) * LEN, cols],
                    arrived.at[seqs * (c + 1) + s],
                )
                for s in range(seqs)
            ]
        )
    for copy in (*x_copies, *(copy for pair in g_copies for copy in pair)):
        copy.start()
    start = size // 2 * chunks
    end = start + out_a.shape[0]
    both = jnp.concatenate([sums[...], jnp.zeros_like(sums)], axis=0)
    for buf, out_grad in ((own_ref, out_a), (other_ref, out_b)):
        buf[start:end, :] = out_grad[...]
        buf[end : end + MARKS, :] = both.astype(jnp.bfloat16)
        if end + MARKS < buf.shape[0]:
            rest = (buf.shape[0] - end - MARKS, buf.shape[1])
            buf[end + MARKS :, :] = jnp.zeros(rest, jnp.bfloat16)
    for s, copy in enumerate(x_copies):
        copy.wait()
        rows = slice(s * LEN, (s + 1) * LEN)
        x_t[:, rows] = x_ref[rows, :].T
    for c, pair in enumerate(g_copies):
        for copy in pair:
            copy.wait()
        part = dot(x_t[...], g_ref[:, c * size : (c + 1) * size])
        for m in range(6):
            buf = (own_ref, other_ref)[m // 3]
            rows = slice((c * 3 + m % 3) * PAIR, (c * 3 + m % 3 + 1) * PAIR)
            for r in range(part.shape[0] // PAIR):
                buf[rows, r * PAIR : (r + 1) * PAIR] = part[
                    r * PAIR : (r + 1) * PAIR, m * PAIR : (m + 1) * PAIR
                ].astype(jnp.bfloat16)


def project_back(x, grads, extra, height):
    rows, depth = x.shape
    wide = grads[0].shape[1]
    seqs = len(grads)
    buf = ((height, depth), jnp.bfloat16, (height, depth), lambda i: (0, 0))
    return call(
        partial(project_back_kernel, seqs), "project_back", (1,),
        [(x, None, None), *((grad, None, None) for grad in grads), *extra],
        [buf, buf],
        scratch=[
            pltpu.VMEM((rows, depth), jnp.bfloat16),
            pltpu.VMEM((depth, rows), jnp.bfloat16),
            pltpu.VMEM((rows, wide), jnp.bfloat16),
            pltpu.SemaphoreType.DMA((seqs * (wide // (6 * PAIR) + 1),)),
        ],
        flops=2 * rows * depth * wide,
        vmem=VM_PROJ,
    )


def stream_kernel(gfirst, grad, *refs):
    weights, out, table = refs[:6], refs[-2], refs[-1]

    @pl.when(pl.program_id(0) == 0)
    def _():
        count = len(weights)
        for n, weight in enumerate(weights):
            for g in range(weight.shape[1] // PAIR):
                at = (g * count + n) * PAIR
                table[:, at : at + PAIR] = weight[:, g * PAIR : (g + 1) * PAIR]

    out[...] = gfirst[...] + dot_nt(grad[...], table[...])


def stream(gfirst, grad, own, other, seq, before=None):
    rows, depth = gfirst.shape
    wide = grad.shape[1]
    per = LEN // BLOCK
    of_seq = lambda i: (seq * per + i, 0)
    ins = [(gfirst, (BLOCK, depth), of_seq), (grad, (BLOCK, wide), rows_of), *own, *other]
    aliases = {}
    if before is not None:
        aliases[len(ins)] = 0
        ins.append((before, None, None))
    return call(
        stream_kernel, "stream", (per,), ins,
        [((rows, depth), jnp.float32, (BLOCK, depth), of_seq)],
        scratch=[pltpu.VMEM((depth, wide), jnp.bfloat16)],
        aliases=aliases,
        flops=2 * LEN * depth * wide,
        vmem=VM_STREAM,
    )[0]


def swap_cores(block):
    return lax.ppermute(block, "mp", [(0, 1), (1, 0)])


def stages_of(chips, radices):
    me, core = lax.axis_index("dp"), lax.axis_index("mp")

    def pairs(masks):
        return [(2 * c + i, 2 * (c ^ masks[i]) + i) for c in range(chips) for i in range(2)]

    stages = []
    bit = 0
    if radices[:2] == (2, 2):
        low, high = me & 1, (me >> 1) & 1
        stages = [
            (jnp.where(core == 0, low, high), 2, [pairs((1, 2))]),
            (jnp.where(core == 0, high, low), 2, [pairs((2, 1))]),
        ]
        bit = 2
        radices = radices[2:]
    while 1 << bit < chips:
        radix = min(radices[0], chips >> bit)
        radices = radices[1:] or radices
        ways = [pairs((j << bit, j << bit)) for j in range(1, radix)]
        stages.append(((me >> bit) & (radix - 1), radix, ways))
        bit += radix // 2
    return stages


def send(block, pairs):
    return lax.ppermute(block, ("dp", "mp"), pairs)


def part(block, which, rows):
    return lax.dynamic_slice_in_dim(block, which * rows, rows)


def added(blocks):
    total = blocks[0].astype(jnp.float32)
    for block in blocks[1:]:
        total = total + block.astype(jnp.float32)
    return total.astype(jnp.bfloat16)


def unpack_kernel(size, shapes, places, *refs):
    pieces, outs, table = refs[: -len(shapes) - 1], refs[-len(shapes) - 1 : -1], refs[-1]
    at = 0
    for piece in pieces:
        block = piece[...].astype(jnp.float32)
        for n in range(block.shape[0] // size):
            table[pl.ds(pl.multiple_of(places[at] * size, size), size), :] = block[
                n * size : (n + 1) * size
            ]
            at += 1
    row = 0
    depth = table.shape[1]
    for out, (kind, height, width) in zip(outs, shapes):
        if kind == "rows":
            out[...] = table[row : row + height, :]
            row += height
        elif kind == "wide":
            for n in range(width // depth):
                out[:, n * depth : (n + 1) * depth] = table[row : row + height, :]
                row += height
        else:
            base, count = kind
            for g in range(width // PAIR):
                at = (g * count + base) * PAIR
                for n in range(height // PAIR):
                    out[n * PAIR : (n + 1) * PAIR, g * PAIR : (g + 1) * PAIR] = table[
                        at : at + PAIR, n * PAIR : (n + 1) * PAIR
                    ]
                row += PAIR


def unpack(pieces, places, shapes, rows, chips):
    depth = pieces[0].shape[1]
    size = rows // chips
    return call(
        partial(unpack_kernel, size, shapes), "unpack", (1,), pieces,
        [((h, w), jnp.float32, (h, w), lambda i, _: (0, 0)) for _, h, w in shapes],
        scratch=[pltpu.VMEM((rows, depth), jnp.float32)],
        scalars=(places,),
        vmem=VM_UNPACK,
    )


def sum_everywhere(own, other, shapes, chips, radices):
    rows = own.shape[0]
    stages = stages_of(chips, radices)
    cores = [(2 * c + i, 2 * c + 1 - i) for c in range(chips) for i in range(2)]
    addends = [own, *(yield [(other, cores)])]
    height = rows
    for digit, radix, ways in stages:
        height //= radix
        got = yield [
            (added([part(a, digit ^ (j + 1), height) for a in addends]), pairs)
            for j, pairs in enumerate(ways)
        ]
        addends = [part(a, digit, height) for a in addends] + got
    pieces = [added(addends)]
    places = [jnp.int32(0)]
    for n, (digit, radix, ways) in enumerate(reversed(stages)):
        weight = chips
        for _, earlier, _ in stages[: len(stages) - n]:
            weight //= earlier
        held = pieces[0] if len(pieces) == 1 else jnp.concatenate(pieces)
        pieces = [held] + (yield [(held, pairs) for pairs in ways])
        places = [p + (digit ^ j) * weight for j in range(radix) for p in places]
    return unpack(pieces, jnp.stack(places).astype(jnp.int32), shapes, rows, chips)


class Chain:
    def __init__(self, steps):
        self.steps, self.result = steps, None
        self.wishes = next(steps)

    def take(self, got):
        try:
            self.wishes = self.steps.send(got)
        except StopIteration as end:
            self.wishes, self.result = [], end.value


def advance(chains, work=None, token=None, beside=()):
    blocks = [block for chain in chains for block, _ in chain.wishes]
    if work is not None:
        *blocks, token = lax.optimization_barrier((*blocks, token))
    else:
        blocks = lax.optimization_barrier(blocks)
    ways = [pairs for chain in chains for _, pairs in chain.wishes]
    got = [send(block, pairs) for block, pairs in zip(blocks, ways)]
    out = None
    if work is not None:
        out = work(token)
        count = len(got)
        *got, last = lax.optimization_barrier((*got, out[-1], *beside))[: count + 1]
        out = (*out[:-1], last)
    for chain in chains:
        if chain.wishes:
            count = len(chain.wishes)
            chain.take(got[:count])
            got = got[count:]
    return out


def on_device(
    normed_in,
    dual_in,
    query_weight,
    key_weight,
    value_weight,
    output_weight,
    first_gain,
    first_bias,
    up_weight,
    down_weight,
    second_gain,
    second_bias,
    segments,
    grad_normed_out,
    grad_dual_out,
    chips,
):
    rows, depth = normed_in.shape
    core = lax.axis_index("mp")
    half, ff = query_weight.shape[1], up_weight.shape[1]
    own = (query_weight, key_weight, value_weight)
    other = tuple(swap_cores(w) for w in own)
    *_, late_out, late_up, late_down = lax.optimization_barrier(
        (*other, output_weight, up_weight, down_weight)
    )
    outs = (output_weight, swap_cores(late_out))
    ups = (up_weight, swap_cores(late_up))
    downs = (down_weight, swap_cores(late_down))
    edges = segments
    core = core.astype(jnp.int32).reshape(1)
    qkv, heads_out, log_totals, key_marks, query_marks = attend(
        edges, core, normed_in, own, other, segments
    )
    grain = 8 * chips

    def padded(count):
        return -(-count // grain) * grain

    row = lambda v: v.reshape(1, depth)
    normed_out, dual_out, grad_first, grad_heads, ffn_own, ffn_other, *extra = layer(
        heads_out, normed_in, dual_in, grad_normed_out, grad_dual_out, key_marks, outs, ups, downs,
        row(first_gain), row(first_bias), row(second_gain), row(second_bias),
    )
    back = partial(
        attend_back, qkv, grad_heads, heads_out, key_marks, query_marks, log_totals, core
    )
    fed = Chain(
        sum_everywhere(
            ffn_own, ffn_other,
            [("rows", ff, depth), ("wide", depth, ff)], chips, (2, 2, 4)
        )
    )
    grad_qkv = []
    for seq in range(rows // LEN):
        grad_qkv += advance([fed], lambda token: (back(seq, token),), edges)
    height = padded(3 * half + half + MARKS)
    own_grads, other_grads = advance(
        [fed], lambda x: project_back(x, grad_qkv, extra, height), normed_in
    )
    rest = Chain(
        sum_everywhere(
            own_grads, other_grads,
            [((n, 3), depth, half) for n in range(3)]
            + [("rows", half, depth)] + [("rows", 1, depth)] * 4,
            chips, (4,),
        )
    )
    advance([fed, rest])
    chains, grad_stream = [fed, rest], None
    for seq, grad in enumerate(grad_qkv):
        last = seq == len(grad_qkv) - 1
        while last and fed.wishes:
            advance(chains)
        (grad_stream,) = advance(
            chains,
            lambda token: (stream(token, grad, own, other, seq, grad_stream),),
            grad_first,
            fed.result[:1] if last else (),
        )
    down_total, up_total = fed.result
    query_total, key_total, value_total, output_total, *small = rest.result
    small = [total.reshape(depth) for total in small]
    return (
        normed_out,
        dual_out,
        grad_stream,
        query_total,
        key_total,
        value_total,
        output_total,
        small[0],
        small[1],
        up_total,
        down_total,
        small[2],
        small[3],
    )


def solution(mesh):
    rows = P(("dp", "mp"), None)
    columns = P(None, "mp")
    return jax.shard_map(
        partial(on_device, chips=mesh.shape["dp"]),
        mesh=mesh,
        in_specs=(
            rows, rows, columns, columns, columns, P("mp", None), P(), P(),
            columns, P("mp", None), P(), P(), P("dp"), rows, rows,
        ),
        out_specs=(
            rows, rows, rows, columns, columns, columns, P("mp", None), P(), P(),
            columns, P("mp", None), P(), P(),
        ),
        check_vma=False,
    )
```

```python
import math
from functools import partial

import jax
import jax.numpy as jnp
from jax import lax
from jax.experimental import pallas as pl
from jax.experimental.pallas import tpu as pltpu
from jax.sharding import PartitionSpec as P

norm_eps = 1e-05
BLOCK = 512
GATE = 0.7978845608028654
CUBE = 0.044715
SAFE = 3600.0
LAYER_BLOCK, SLOPE_TYPE = 256, jnp.float32
VM_ATT, VM_LAYER, VM_BACK, VM_PROJ, VM_STREAM, VM_UNPACK = 56, 56, 56, 56, 56, 56
HD = 64
LEN = 1024
TILE = 128
TILES = LEN // TILE
PAIR = 2 * HD
FAR = -1e30
MARKS = 16
LSE_ROW = 8
LIVE_LANE = 12
MIB = 2**20


def dot(left, right):
    return jnp.dot(left, right, preferred_element_type=jnp.float32)


def three_parts(row):
    high = row.astype(jnp.bfloat16)
    rest = row - high.astype(jnp.float32)
    mid = rest.astype(jnp.bfloat16)
    low = (rest - mid.astype(jnp.float32)).astype(jnp.bfloat16)
    return high, mid, low


def label_marks(labels):
    row = lax.broadcasted_iota(jnp.int32, (TILE, labels.shape[1]), 0)
    same = labels == row
    ones = (row < LSE_ROW + 3) | ((row == LIVE_LANE) & (labels != 0))
    keys = jnp.where(row < LSE_ROW, jnp.where(same, 0.0, FAR), jnp.where(ones, 1.0, 0.0))
    queries = jnp.where(same & (row < LSE_ROW), 1.0, 0.0)[:MARKS]
    return keys.astype(jnp.bfloat16).T, queries.astype(jnp.bfloat16)


def key_range(labels, base, i):
    def head(j):
        return labels[(base + j) * TILE]

    def tail(j):
        return labels[(base + j) * TILE + TILE - 1]

    low, high = head(i), tail(i)
    first, last = i, i
    for j in reversed(range(TILES)):
        first = jnp.where((j < i) & (tail(j) == low), j, first)
    for j in range(TILES):
        last = jnp.where((j > i) & (head(j) == high), j, last)
    return first, last - first + 1


def halves_of(block):
    return jnp.concatenate([block[:HD, :TILE], block[HD:, TILE:]], axis=0)


def split_lanes(tile):
    lane = lax.broadcasted_iota(jnp.int32, tile.shape, 1)
    zero = jnp.zeros_like(tile)
    return jnp.concatenate(
        [jnp.where(lane < HD, tile, zero), jnp.where(lane < HD, zero, tile)], axis=0
    )


def each_width(count, branch):
    for width in range(1, TILES + 1):
        pl.when(count == width)(partial(branch, width))


def dot_nt(left, right):
    return lax.dot_general(
        left, right, (((1,), (1,)), ((), ())), preferred_element_type=jnp.float32
    )


def dot_tn(left, right):
    return lax.dot_general(
        left, right, (((0,), (0,)), ((), ())), preferred_element_type=jnp.float32
    )


def full(ref):
    shape = ref.shape
    return pl.BlockSpec(shape, lambda *_: (0,) * len(shape), pipeline_mode=pl.Buffered(1))


def call(kernel, name, grid, ins, outs, scratch=(), scalars=(), flops=0, aliases=None, vmem=56):
    specs, arrays = [], []
    for item in ins:
        if isinstance(item, tuple):
            arrays.append(item[0])
            if item[1] is None:
                specs.append(pl.BlockSpec(memory_space=pl.ANY))
            else:
                specs.append(pl.BlockSpec(item[1], item[2]))
        else:
            arrays.append(item)
            specs.append(full(item))
    size = sum(a.size * a.dtype.itemsize for a in arrays)
    size += sum(jnp.dtype(d).itemsize * math.prod(s) for s, d, _, _ in outs)
    return pl.pallas_call(
        kernel,
        grid_spec=pltpu.PrefetchScalarGridSpec(
            num_scalar_prefetch=len(scalars),
            grid=grid,
            in_specs=specs,
            out_specs=[
                pl.BlockSpec(b, m) if b else pl.BlockSpec(memory_space=pl.ANY)
                for _, _, b, m in outs
            ],
            scratch_shapes=scratch,
        ),
        out_shape=[jax.ShapeDtypeStruct(s, d) for s, d, _, _ in outs],
        compiler_params=pltpu.CompilerParams(vmem_limit_bytes=vmem * MIB),
        cost_estimate=pl.CostEstimate(flops=flops, bytes_accessed=size, transcendentals=0),
        input_output_aliases=aliases or {},
        name=name,
    )(*scalars, *arrays)


def rows_of(i, *_):
    return (i, 0)


def stats(z):
    mean = jnp.mean(z, axis=-1, keepdims=True)
    centred = z - mean
    spread = jnp.mean(centred * centred, axis=-1, keepdims=True)
    scale = lax.rsqrt(spread + norm_eps)
    return centred * scale, scale


def norm_back(upstream, unit, scale, gain):
    t = upstream * gain
    inner = jnp.mean(t * unit, axis=-1, keepdims=True)
    return (t - jnp.mean(t, axis=-1, keepdims=True) - unit * inner) * scale


def layer_kernel(
    heads, x, dual, gn, gd, marks, out_a, out_b, up_a, up_b, down_a, down_b, g1, b1, g2, b2,
    normed_out, dual_out, gfirst_ref, gheads, ffn_grad_a, ffn_grad_b,
    out_grad_a, out_grad_b, sums,
    hid, slope, acc_up, acc_down, acc_out,
):
    i = pl.program_id(0)
    half = out_a.shape[0]
    ff = up_a.shape[1]
    chunk = 1024

    @pl.when(i == 0)
    def _():
        sums[...] = jnp.zeros_like(sums)
        acc_up[...] = jnp.zeros_like(acc_up)
        acc_down[...] = jnp.zeros_like(acc_down)
        acc_out[...] = jnp.zeros_like(acc_out)

    attn = dot(heads[:, :half], out_a[...]) + dot(heads[:, half:], out_b[...])
    z1 = x[...].astype(jnp.float32) + attn
    unit, scale = stats(z1)
    normed = unit * g1[...] + b1[...]
    low = normed.astype(jnp.bfloat16)
    ffn = None
    for n, (up, down) in enumerate(((up_a, down_a), (up_b, down_b))):
        for c in range(ff // chunk):
            cols = slice(c * chunk, (c + 1) * chunk)
            at = slice(n * ff + c * chunk, n * ff + (c + 1) * chunk)
            v = dot(low, up[:, cols])
            square = v * v
            t = jnp.tanh(v * (GATE + (GATE * CUBE) * square))
            open_part = 0.5 + 0.5 * t
            hidden = (v * open_part).astype(jnp.bfloat16)
            hid[:, at] = hidden
            slope[:, at] = open_part + (v * (0.5 - 0.5 * t * t)) * (
                GATE + (3 * GATE * CUBE) * square
            )
            part = dot(hidden, down[cols, :])
            ffn = part if ffn is None else ffn + part
    unit2, scale2 = stats(normed + ffn)
    normed_out[...] = (unit2 * g2[...] + b2[...]).astype(jnp.bfloat16)
    dual_out[...] = (dual[...].astype(jnp.float32) + attn + ffn).astype(jnp.bfloat16)
    upstream = gn[...].astype(jnp.float32)
    gmid = norm_back(upstream, unit2, scale2, g2[...])
    gdual = gd[...].astype(jnp.float32)
    gffn = (gmid + gdual).astype(jnp.bfloat16)
    gffn_t = gffn.T
    low_t = low.T
    gnormed = gmid
    for n, (up, down) in enumerate(((up_a, down_a), (up_b, down_b))):
        for c in range(ff // chunk):
            cols = slice(c * chunk, (c + 1) * chunk)
            at = slice(n * ff + c * chunk, n * ff + (c + 1) * chunk)
            gpre = (dot_nt(gffn, down[cols, :]) * slope[:, at]).astype(jnp.bfloat16)
            acc_down[:, at] += dot(gffn_t, hid[:, at])
            acc_up[:, at] += dot(low_t, gpre)
            gnormed = gnormed + dot_nt(gpre, up[:, cols])
    gfirst = norm_back(gnormed, unit, scale, g1[...])
    gfirst_ref[...] = gfirst
    gattn = (gfirst + gdual).astype(jnp.bfloat16)
    sums[0:1, :] += jnp.sum(gnormed * unit, axis=0, keepdims=True)
    sums[1:2, :] += jnp.sum(gnormed, axis=0, keepdims=True)
    sums[2:3, :] += jnp.sum(upstream * unit2, axis=0, keepdims=True)
    sums[3:4, :] += jnp.sum(upstream, axis=0, keepdims=True)
    acc_out[...] += dot_tn(heads[...], gattn)
    live = marks[:, LIVE_LANE : LIVE_LANE + 1].astype(jnp.float32)
    gheads[:, :half] = (dot_nt(gattn, out_a[...]) * live).astype(jnp.bfloat16)
    gheads[:, half:] = (dot_nt(gattn, out_b[...]) * live).astype(jnp.bfloat16)

    @pl.when(i == pl.num_programs(0) - 1)
    def _():
        depth = acc_up.shape[0]
        for n, (ffn_grad, out_grad) in enumerate(
            ((ffn_grad_a, out_grad_a), (ffn_grad_b, out_grad_b))
        ):
            ffn_grad[:ff, :] = acc_down[:, n * ff : (n + 1) * ff].T.astype(jnp.bfloat16)
            for c in range(ff // depth):
                at = n * ff + c * depth
                ffn_grad[ff + c * depth : ff + (c + 1) * depth, :] = acc_up[
                    :, at : at + depth
                ].astype(jnp.bfloat16)
            out_grad[...] = acc_out[n * half : (n + 1) * half, :].astype(jnp.bfloat16)


def layer(heads, x, dual, gn, gd, marks, outs, ups, downs, g1, b1, g2, b2, block=BLOCK):
    rows, depth = x.shape
    ff, half = ups[0].shape[1], outs[0].shape[0]
    tall = ((rows, depth), jnp.bfloat16, (block, depth), rows_of)
    tall32 = ((rows, depth), jnp.float32, (block, depth), rows_of)

    def once(*shape, dtype=jnp.bfloat16):
        return (shape, dtype, shape, lambda i: (0, 0))

    return call(
        layer_kernel, "layer", (rows // block,),
        [(a, (block, a.shape[1]), rows_of) for a in (heads, x, dual, gn, gd, marks)]
        + [*outs, *ups, *downs, g1, b1, g2, b2],
        [tall, tall, tall32, tall, once(2 * ff, depth), once(2 * ff, depth),
         once(half, depth), once(half, depth), once(8, depth, dtype=jnp.float32)],
        scratch=[
            pltpu.VMEM((block, 2 * ff), jnp.bfloat16),
            pltpu.VMEM((block, 2 * ff), jnp.float32),
            pltpu.VMEM((depth, 2 * ff), jnp.float32),
            pltpu.VMEM((depth, 2 * ff), jnp.float32),
            pltpu.VMEM((2 * half, depth), jnp.float32),
        ],
        flops=2 * rows * depth * (3 * depth + 12 * ff),
        vmem=VM_LAYER,
    )


def fill_block(table, p, i, tile_t):
    table[p, i, :HD, :TILE] = tile_t[:HD]
    table[p, i, HD:PAIR, TILE:] = tile_t[HD:]


def score_bound(qkv, width):
    row = lax.broadcasted_iota(jnp.int32, (width, TILE), 0)
    head = lax.broadcasted_iota(jnp.int32, (width, TILE), 1)
    heads = (row // HD == head).astype(jnp.bfloat16)
    largest = []
    for at in (0, width):
        block = qkv[:, at : at + width].astype(jnp.float32)
        norms = dot((block * block).astype(jnp.bfloat16), heads)
        largest.append(jnp.max(norms, axis=0, keepdims=True))
    return jnp.max(largest[0] * largest[1]) * (1.02 / HD)


def attend_kernel(
    edges, core, x_ref, qa, ka, va, qb, kb, vb, labels,
    qkv_hbm, out_ref, lse_ref, key_marks, query_marks, qkv_ref, kcat, vt, qt, mixed_t, left,
):
    seq = pl.program_id(0)
    base = (core[0] * pl.num_programs(0) + seq) * TILES
    key_marks[...], query_marks[...] = label_marks(labels[...])
    half = qa.shape[1]
    width = 2 * half
    pairs = width // PAIR
    x = x_ref[...]

    @pl.when(seq == 0)
    def _():
        qt[...] = jnp.zeros_like(qt)

    for n, w in enumerate((qa, qb, ka, kb, va, vb)):
        qkv_ref[:, n * half : (n + 1) * half] = dot(x, w[...]).astype(jnp.bfloat16)
    rows = pl.ds(pl.multiple_of(seq * LEN, LEN), LEN)
    leaving = pltpu.make_async_copy(qkv_ref, qkv_hbm.at[rows, :], left)
    leaving.start()
    small_scores = score_bound(qkv_ref, width) < SAFE
    for p in range(pairs):
        lanes = slice(p * PAIR, (p + 1) * PAIR)
        kcat[p, :, :PAIR] = qkv_ref[:, width + p * PAIR : width + (p + 1) * PAIR]
        kcat[p, :, PAIR:] = key_marks[...]
        vt[lanes, :] = qkv_ref[:, 2 * width + p * PAIR : 2 * width + (p + 1) * PAIR].T
        for i in range(TILES):
            cols = slice(i * TILE, (i + 1) * TILE)
            fill_block(qt, p, i, (qkv_ref[cols, lanes] * jnp.bfloat16(HD**-0.5)).T)
            qt[p, i, PAIR : PAIR + MARKS, :TILE] = query_marks[:, cols]
            qt[p, i, PAIR : PAIR + MARKS, TILE:] = query_marks[:, cols]

    def step(i, carry):
        at = pl.multiple_of(i * TILE, TILE)
        first, count = key_range(edges, base, i)
        first = jnp.where(small_scores, first, 0)
        start = pl.multiple_of(first * TILE, TILE)

        def branch(width, small=True):
            at_keys = pl.ds(start, width * TILE)

            def scores_of(p):
                return dot(kcat[p, at_keys, :], qt[p, i])

            def finish(p, scores):
                top = None
                if not small:
                    top = jnp.max(scores, axis=0, keepdims=True)
                    scores = scores - top
                probs = jnp.exp(scores)
                total = jnp.sum(probs, axis=0, keepdims=True)
                mixed = dot(vt[p * PAIR : (p + 1) * PAIR, at_keys], probs.astype(jnp.bfloat16))
                mixed_t[p * PAIR : (p + 1) * PAIR, pl.ds(at, TILE)] = halves_of(mixed / total)
                log_total = jnp.log(total)
                lse_ref[0, p, pl.ds(i, 1), :] = log_total if small else top + log_total

            ahead = scores_of(0)
            for p in range(pairs):
                scores = ahead
                if p + 1 < pairs:
                    ahead = scores_of(p + 1)
                finish(p, scores)

        each_width(jnp.where(small_scores, count, 0), branch)
        pl.when(jnp.logical_not(small_scores))(partial(branch, TILES, False))
        return carry

    lax.fori_loop(0, TILES, step, 0)
    live = 1.0 - query_marks[:1, :].astype(jnp.float32)
    for p in range(pairs):
        lanes = slice(p * PAIR, (p + 1) * PAIR)
        out_ref[:, lanes] = (mixed_t[lanes, :] * live).astype(jnp.bfloat16).T
    leaving.wait()


def attend(edges, core, x, own, other, segments):
    rows, depth = x.shape
    half = own[0].shape[1]
    width = 2 * half
    seqs, pairs = rows // LEN, width // PAIR
    return call(
        attend_kernel, "attend", (seqs,),
        [
            (x, (LEN, depth), lambda s, *_: (s, 0)),
            *own,
            *other,
            (segments.reshape(1, -1), (1, LEN), lambda s, _, core: (0, core[0] * seqs + s)),
        ],
        [
            ((rows, 3 * width), jnp.bfloat16, None, None),
            ((rows, width), jnp.bfloat16, (LEN, width), lambda s, *_: (s, 0)),
            (
                (seqs, pairs, TILES, 2 * TILE), jnp.float32, (1, pairs, TILES, 2 * TILE),
                lambda s, *_: (s, 0, 0, 0),
            ),
            ((rows, TILE), jnp.bfloat16, (LEN, TILE), lambda s, *_: (s, 0)),
            ((MARKS, rows), jnp.bfloat16, (MARKS, LEN), lambda s, *_: (0, s)),
        ],
        scratch=[
            pltpu.VMEM((LEN, 3 * width), jnp.bfloat16),
            pltpu.VMEM((pairs, LEN, PAIR + TILE), jnp.bfloat16),
            pltpu.VMEM((width, LEN), jnp.bfloat16),
            pltpu.VMEM((pairs, TILES, PAIR + TILE, 2 * TILE), jnp.bfloat16),
            pltpu.VMEM((width, LEN), jnp.float32),
            pltpu.SemaphoreType.DMA,
        ],
        scalars=(edges, core),
        flops=2 * rows * (3 * width * depth + 2 * width * LEN),
        vmem=VM_ATT,
    )


def attend_back_kernel(
    edges, core, seq, qkv_hbm, g_hbm, o_hbm, key_marks, query_marks, lse_ref, out_hbm,
    q_ref, k_ref, v_ref, g_ref, o_ref, out_ref, kcat, vcat, kt, qt, gt, dk, dv, dqt, arrived, left,
):
    base = (core[0] * (qkv_hbm.shape[0] // LEN) + seq[0]) * TILES
    width = q_ref.shape[1]
    pairs = width // PAIR
    groups = pairs // 2
    rows = pl.ds(pl.multiple_of(seq[0] * LEN, LEN), LEN)
    k_copy, v_copy, q_copy, g_copy, o_copy = (
        pltpu.make_async_copy(source, target, arrived.at[n])
        for n, (source, target) in enumerate(
            (
                (qkv_hbm.at[rows, pl.ds(width, width)], k_ref),
                (qkv_hbm.at[rows, pl.ds(2 * width, width)], v_ref),
                (qkv_hbm.at[rows, pl.ds(0, width)], q_ref),
                (g_hbm.at[rows, :], g_ref),
                (o_hbm.at[rows, :], o_ref),
            )
        )
    )
    for copy in (k_copy, v_copy, q_copy, g_copy, o_copy):
        copy.start()

    def place(p, what):
        at = (((p % groups) * 2 + p // groups) * 3 + what) * PAIR
        return slice(at, at + PAIR)

    def negated(row):
        return [part.astype(jnp.float32) for part in three_parts(-row)]

    qt[...] = jnp.zeros_like(qt)
    gt[...] = jnp.zeros_like(gt)
    dk[...] = jnp.zeros_like(dk)
    dv[...] = jnp.zeros_like(dv)
    for p in range(pairs):
        kcat[p, :, PAIR:] = key_marks[...]
        vcat[p, :, PAIR:] = key_marks[...]
    k_copy.wait()
    for p in range(pairs):
        lanes = slice(p * PAIR, (p + 1) * PAIR)
        kcat[p, :, :PAIR] = k_ref[:, lanes]
        kt[lanes, :] = k_ref[:, lanes].T
    v_copy.wait()
    for p in range(pairs):
        vcat[p, :, :PAIR] = v_ref[:, p * PAIR : (p + 1) * PAIR]
    q_copy.wait()
    g_copy.wait()
    o_copy.wait()
    pad = jnp.zeros((MARKS - LSE_ROW - 3, 2 * TILE), jnp.float32)
    none = jnp.zeros((LSE_ROW, 2 * TILE), jnp.float32)
    for p in range(pairs):
        lanes = slice(p * PAIR, (p + 1) * PAIR)
        for i in range(TILES):
            cols = slice(i * TILE, (i + 1) * TILE)
            fill_block(qt, p, i, (q_ref[cols, lanes] * jnp.bfloat16(HD**-0.5)).T)
            grad_t = g_ref[cols, lanes].T
            fill_block(gt, p, i, grad_t)
            agree = grad_t.astype(jnp.float32) * o_ref[cols, lanes].T.astype(jnp.float32)
            delta = jnp.concatenate(
                [
                    jnp.sum(agree[:HD], axis=0, keepdims=True),
                    jnp.sum(agree[HD:], axis=0, keepdims=True),
                ],
                axis=1,
            )
            marks = query_marks[:LSE_ROW, cols].astype(jnp.float32)
            marks = jnp.concatenate([marks, marks], axis=1)
            lse = lse_ref[0, p, i : i + 1, :]
            qt[p, i, PAIR : PAIR + MARKS, :] = jnp.concatenate(
                [marks, *negated(lse), pad], axis=0
            ).astype(jnp.bfloat16)
            gt[p, i, PAIR : PAIR + MARKS, :] = jnp.concatenate(
                [none, *negated(delta), pad], axis=0
            ).astype(jnp.bfloat16)

    def step(i, carry):
        at = pl.multiple_of(i * TILE, TILE)
        first, count = key_range(edges, base, i)
        start = pl.multiple_of(first * TILE, TILE)

        def branch(width):
            at_keys = pl.ds(start, width * TILE)

            def head(p):
                scores = dot(kcat[p, at_keys, :], qt[p, i])
                grad_probs = dot(vcat[p, at_keys, :], gt[p, i])
                return scores, grad_probs

            def finish(p, scores, grad_probs):
                lanes = slice(p * PAIR, (p + 1) * PAIR)
                query = q_ref[pl.ds(at, TILE), lanes] * jnp.bfloat16(HD**-0.5)
                grad = g_ref[pl.ds(at, TILE), lanes]
                probs = jnp.exp(scores)
                grad_scores = (probs * grad_probs).astype(jnp.bfloat16)
                dv[p, at_keys, :] += dot(probs.astype(jnp.bfloat16), split_lanes(grad))
                dk[p, at_keys, :] += dot(grad_scores, split_lanes(query))
                dqt[lanes, pl.ds(at, TILE)] = halves_of(dot(kt[lanes, at_keys], grad_scores))

            ahead = head(0)
            for p in range(pairs):
                now = ahead
                if p + 1 < pairs:
                    ahead = head(p + 1)
                finish(p, *now)

        each_width(count, branch)
        return carry

    lax.fori_loop(0, TILES, step, 0)
    copies = []
    for g in range(groups):
        for p in (g, g + groups):
            lanes = slice(p * PAIR, (p + 1) * PAIR)
            out_ref[:, place(p, 0)] = (dqt[lanes, :] * HD**-0.5).astype(jnp.bfloat16).T
            out_ref[:, place(p, 1)] = dk[p].astype(jnp.bfloat16)
            out_ref[:, place(p, 2)] = dv[p].astype(jnp.bfloat16)
            cols = pl.ds(place(p, 0).start, 3 * PAIR)
            copies.append(
                pltpu.make_async_copy(out_ref.at[:, cols], out_hbm.at[:, cols], left.at[p])
            )
            copies[-1].start()
    for copy in copies:
        copy.wait()


def attend_back(qkv, gheads, heads, key_marks, query_marks, lse, core, seq, edges):
    rows, width = heads.shape
    seqs, pairs = rows // LEN, width // PAIR
    by_seq = lambda i, edges, core, seq: (seq[0], 0)
    block = pltpu.VMEM((LEN, width), jnp.bfloat16)
    return call(
        attend_back_kernel, "attend_back", (1,),
        [
            (qkv, None, None),
            (gheads, None, None),
            (heads, None, None),
            (key_marks, (LEN, TILE), by_seq),
            (query_marks, (MARKS, LEN), lambda i, edges, core, seq: (0, seq[0])),
            (lse, (1, pairs, TILES, 2 * TILE), lambda i, edges, core, seq: (seq[0], 0, 0, 0)),
        ],
        [((LEN, 3 * width), jnp.bfloat16, None, None)],
        scratch=[
            *[block] * 5,
            pltpu.VMEM((LEN, 3 * width), jnp.bfloat16),
            pltpu.VMEM((pairs, LEN, PAIR + TILE), jnp.bfloat16),
            pltpu.VMEM((pairs, LEN, PAIR + TILE), jnp.bfloat16),
            pltpu.VMEM((width, LEN), jnp.bfloat16),
            pltpu.VMEM((pairs, TILES, PAIR + TILE, 2 * TILE), jnp.bfloat16),
            pltpu.VMEM((pairs, TILES, PAIR + TILE, 2 * TILE), jnp.bfloat16),
            pltpu.VMEM((pairs, LEN, PAIR), jnp.float32),
            pltpu.VMEM((pairs, LEN, PAIR), jnp.float32),
            pltpu.VMEM((width, LEN), jnp.float32),
            pltpu.SemaphoreType.DMA((5,)),
            pltpu.SemaphoreType.DMA((pairs,)),
        ],
        scalars=(edges, core, jnp.full((1,), seq, jnp.int32)),
        flops=10 * LEN * width * LEN,
        vmem=VM_BACK,
    )[0]


def project_back_kernel(seqs, x_hbm, *refs):
    grads = refs[:seqs]
    out_a, out_b, sums, own_ref, other_ref, x_ref, x_t, g_ref, arrived = refs[seqs:]
    size = 6 * PAIR
    chunks = g_ref.shape[1] // size
    x_copies, g_copies = [], []
    for s in range(seqs):
        rows = slice(s * LEN, (s + 1) * LEN)
        x_copies.append(
            pltpu.make_async_copy(x_hbm.at[rows, :], x_ref.at[rows, :], arrived.at[s])
        )
    for c in range(chunks):
        cols = pl.ds(c * size, size)
        g_copies.append(
            [
                pltpu.make_async_copy(
                    grads[s].at[:, cols],
                    g_ref.at[s * LEN : (s + 1) * LEN, cols],
                    arrived.at[seqs * (c + 1) + s],
                )
                for s in range(seqs)
            ]
        )
    for copy in (*x_copies, *(copy for pair in g_copies for copy in pair)):
        copy.start()
    start = size // 2 * chunks
    end = start + out_a.shape[0]
    both = jnp.concatenate([sums[...], jnp.zeros_like(sums)], axis=0)
    for buf, out_grad in ((own_ref, out_a), (other_ref, out_b)):
        buf[start:end, :] = out_grad[...]
        buf[end : end + MARKS, :] = both.astype(jnp.bfloat16)
        if end + MARKS < buf.shape[0]:
            rest = (buf.shape[0] - end - MARKS, buf.shape[1])
            buf[end + MARKS :, :] = jnp.zeros(rest, jnp.bfloat16)
    for s, copy in enumerate(x_copies):
        copy.wait()
        rows = slice(s * LEN, (s + 1) * LEN)
        x_t[:, rows] = x_ref[rows, :].T
    for c, pair in enumerate(g_copies):
        for copy in pair:
            copy.wait()
        for r in range(x_t.shape[0] // PAIR):
            at = slice(r * PAIR, (r + 1) * PAIR)
            part = dot(x_t[at, :], g_ref[:, c * size : (c + 1) * size]).astype(jnp.bfloat16)
            for m in range(6):
                rows = slice((c * 3 + m % 3) * PAIR, (c * 3 + m % 3 + 1) * PAIR)
                (own_ref, other_ref)[m // 3][rows, at] = part[:, m * PAIR : (m + 1) * PAIR]


def project_back(x, grads, extra, height):
    rows, depth = x.shape
    wide = grads[0].shape[1]
    seqs = len(grads)
    buf = ((height, depth), jnp.bfloat16, (height, depth), lambda i: (0, 0))
    return call(
        partial(project_back_kernel, seqs), "project_back", (1,),
        [(x, None, None), *((grad, None, None) for grad in grads), *extra],
        [buf, buf],
        scratch=[
            pltpu.VMEM((rows, depth), jnp.bfloat16),
            pltpu.VMEM((depth, rows), jnp.bfloat16),
            pltpu.VMEM((rows, wide), jnp.bfloat16),
            pltpu.SemaphoreType.DMA((seqs * (wide // (6 * PAIR) + 1),)),
        ],
        flops=2 * rows * depth * wide,
        vmem=VM_PROJ,
    )


def stream_kernel(gfirst, grad, *refs):
    weights, out, table = refs[:6], refs[-2], refs[-1]

    @pl.when(pl.program_id(0) == 0)
    def _():
        count = len(weights)
        for n, weight in enumerate(weights):
            for g in range(weight.shape[1] // PAIR):
                at = (g * count + n) * PAIR
                table[:, at : at + PAIR] = weight[:, g * PAIR : (g + 1) * PAIR]

    out[...] = gfirst[...] + dot_nt(grad[...], table[...])


def stream(gfirst, grad, own, other, seq, before=None):
    rows, depth = gfirst.shape
    wide = grad.shape[1]
    per = LEN // BLOCK
    of_seq = lambda i: (seq * per + i, 0)
    ins = [(gfirst, (BLOCK, depth), of_seq), (grad, (BLOCK, wide), rows_of), *own, *other]
    aliases = {}
    if before is not None:
        aliases[len(ins)] = 0
        ins.append((before, None, None))
    return call(
        stream_kernel, "stream", (per,), ins,
        [((rows, depth), jnp.float32, (BLOCK, depth), of_seq)],
        scratch=[pltpu.VMEM((depth, wide), jnp.bfloat16)],
        aliases=aliases,
        flops=2 * LEN * depth * wide,
        vmem=VM_STREAM,
    )[0]


def swap_cores(block):
    return lax.ppermute(block, "mp", [(0, 1), (1, 0)])


def stages_of(chips, radices):
    me, core = lax.axis_index("dp"), lax.axis_index("mp")

    def pairs(masks):
        return [(2 * c + i, 2 * (c ^ masks[i]) + i) for c in range(chips) for i in range(2)]

    stages = []
    bit = 0
    if radices[:2] == (2, 2):
        low, high = me & 1, (me >> 1) & 1
        stages = [
            (jnp.where(core == 0, low, high), 2, [pairs((1, 2))]),
            (jnp.where(core == 0, high, low), 2, [pairs((2, 1))]),
        ]
        bit = 2
        radices = radices[2:]
    while 1 << bit < chips:
        radix = min(radices[0], chips >> bit)
        radices = radices[1:] or radices
        ways = [pairs((j << bit, j << bit)) for j in range(1, radix)]
        stages.append(((me >> bit) & (radix - 1), radix, ways))
        bit += radix // 2
    return stages


def send(block, pairs):
    return lax.ppermute(block, ("dp", "mp"), pairs)


def part(block, which, rows):
    return lax.dynamic_slice_in_dim(block, which * rows, rows)


def added(blocks):
    total = blocks[0].astype(jnp.float32)
    for block in blocks[1:]:
        total = total + block.astype(jnp.float32)
    return total.astype(jnp.bfloat16)


def unpack_kernel(size, shapes, places, *refs):
    pieces, outs, table = refs[: -len(shapes) - 1], refs[-len(shapes) - 1 : -1], refs[-1]
    at = 0
    for piece in pieces:
        block = piece[...].astype(jnp.float32)
        for n in range(block.shape[0] // size):
            table[pl.ds(pl.multiple_of(places[at] * size, size), size), :] = block[
                n * size : (n + 1) * size
            ]
            at += 1
    row = 0
    depth = table.shape[1]
    for out, (kind, height, width) in zip(outs, shapes):
        if kind == "rows":
            out[...] = table[row : row + height, :]
            row += height
        elif kind == "wide":
            for n in range(width // depth):
                out[:, n * depth : (n + 1) * depth] = table[row : row + height, :]
                row += height
        else:
            base, count = kind
            for g in range(width // PAIR):
                at = (g * count + base) * PAIR
                for n in range(height // PAIR):
                    out[n * PAIR : (n + 1) * PAIR, g * PAIR : (g + 1) * PAIR] = table[
                        at : at + PAIR, n * PAIR : (n + 1) * PAIR
                    ]
                row += PAIR


def unpack(pieces, places, shapes, rows, chips):
    depth = pieces[0].shape[1]
    size = rows // chips
    return call(
        partial(unpack_kernel, size, shapes), "unpack", (1,), pieces,
        [((h, w), jnp.float32, (h, w), lambda i, _: (0, 0)) for _, h, w in shapes],
        scratch=[pltpu.VMEM((rows, depth), jnp.float32)],
        scalars=(places,),
        vmem=VM_UNPACK,
    )


def sum_everywhere(own, other, shapes, chips, radices):
    rows = own.shape[0]
    stages = stages_of(chips, radices)
    cores = [(2 * c + i, 2 * c + 1 - i) for c in range(chips) for i in range(2)]
    addends = [own, *(yield [(other, cores)])]
    height = rows
    for digit, radix, ways in stages:
        height //= radix
        got = yield [
            (added([part(a, digit ^ (j + 1), height) for a in addends]), pairs)
            for j, pairs in enumerate(ways)
        ]
        addends = [part(a, digit, height) for a in addends] + got
    pieces = [added(addends)]
    places = [jnp.int32(0)]
    for n, (digit, radix, ways) in enumerate(reversed(stages)):
        weight = chips
        for _, earlier, _ in stages[: len(stages) - n]:
            weight //= earlier
        held = pieces[0] if len(pieces) == 1 else jnp.concatenate(pieces)
        pieces = [held] + (yield [(held, pairs) for pairs in ways])
        places = [p + (digit ^ j) * weight for j in range(radix) for p in places]
    return unpack(pieces, jnp.stack(places).astype(jnp.int32), shapes, rows, chips)


class Chain:
    def __init__(self, steps):
        self.steps, self.result = steps, None
        self.wishes = next(steps)

    def take(self, got):
        try:
            self.wishes = self.steps.send(got)
        except StopIteration as end:
            self.wishes, self.result = [], end.value


def advance(chains, work=None, token=None, beside=()):
    blocks = [block for chain in chains for block, _ in chain.wishes]
    if work is not None:
        *blocks, token = lax.optimization_barrier((*blocks, token))
    else:
        blocks = lax.optimization_barrier(blocks)
    ways = [pairs for chain in chains for _, pairs in chain.wishes]
    got = [send(block, pairs) for block, pairs in zip(blocks, ways)]
    out = None
    if work is not None:
        out = work(token)
        count = len(got)
        *got, last = lax.optimization_barrier((*got, out[-1], *beside))[: count + 1]
        out = (*out[:-1], last)
    for chain in chains:
        if chain.wishes:
            count = len(chain.wishes)
            chain.take(got[:count])
            got = got[count:]
    return out


def on_device(
    normed_in,
    dual_in,
    query_weight,
    key_weight,
    value_weight,
    output_weight,
    first_gain,
    first_bias,
    up_weight,
    down_weight,
    second_gain,
    second_bias,
    segments,
    grad_normed_out,
    grad_dual_out,
    chips,
):
    rows, depth = normed_in.shape
    core = lax.axis_index("mp")
    half, ff = query_weight.shape[1], up_weight.shape[1]
    own = (query_weight, key_weight, value_weight)
    other = tuple(swap_cores(w) for w in own)
    *_, late_out, late_up, late_down = lax.optimization_barrier(
        (*other, output_weight, up_weight, down_weight)
    )
    outs = (output_weight, swap_cores(late_out))
    ups = (up_weight, swap_cores(late_up))
    downs = (down_weight, swap_cores(late_down))
    edges = segments
    core = core.astype(jnp.int32).reshape(1)
    qkv, heads_out, log_totals, key_marks, query_marks = attend(
        edges, core, normed_in, own, other, segments
    )
    grain = 8 * chips

    def padded(count):
        return -(-count // grain) * grain

    row = lambda v: v.reshape(1, depth)
    normed_out, dual_out, grad_first, grad_heads, ffn_own, ffn_other, *extra = layer(
        heads_out, normed_in, dual_in, grad_normed_out, grad_dual_out, key_marks, outs, ups, downs,
        row(first_gain), row(first_bias), row(second_gain), row(second_bias),
    )
    back = partial(
        attend_back, qkv, grad_heads, heads_out, key_marks, query_marks, log_totals, core
    )
    fed = Chain(
        sum_everywhere(
            ffn_own, ffn_other,
            [("rows", ff, depth), ("wide", depth, ff)], chips, (2, 2, 4)
        )
    )
    grad_qkv = []
    for seq in range(rows // LEN):
        grad_qkv += advance([fed], lambda token: (back(seq, token),), edges)
    height = padded(3 * half + half + MARKS)
    own_grads, other_grads = advance(
        [fed], lambda x: project_back(x, grad_qkv, extra, height), normed_in
    )
    rest = Chain(
        sum_everywhere(
            own_grads, other_grads,
            [((n, 3), depth, half) for n in range(3)]
            + [("rows", half, depth)] + [("rows", 1, depth)] * 4,
            chips, (4,),
        )
    )
    advance([fed, rest])
    chains, grad_stream = [fed, rest], None
    for seq, grad in enumerate(grad_qkv):
        last = seq == len(grad_qkv) - 1
        while last and fed.wishes:
            advance(chains)
        (grad_stream,) = advance(
            chains,
            lambda token: (stream(token, grad, own, other, seq, grad_stream),),
            grad_first,
            fed.result[:1] if last else (),
        )
    down_total, up_total = fed.result
    query_total, key_total, value_total, output_total, *small = rest.result
    small = [total.reshape(depth) for total in small]
    return (
        normed_out,
        dual_out,
        grad_stream,
        query_total,
        key_total,
        value_total,
        output_total,
        small[0],
        small[1],
        up_total,
        down_total,
        small[2],
        small[3],
    )


def solution(mesh):
    rows = P(("dp", "mp"), None)
    columns = P(None, "mp")
    return jax.shard_map(
        partial(on_device, chips=mesh.shape["dp"]),
        mesh=mesh,
        in_specs=(
            rows, rows, columns, columns, columns, P("mp", None), P(), P(),
            columns, P("mp", None), P(), P(), P("dp"), rows, rows,
        ),
        out_specs=(
            rows, rows, rows, columns, columns, columns, P("mp", None), P(), P(),
            columns, P("mp", None), P(), P(),
        ),
        check_vma=False,
    )
```

```python
import math
from functools import partial

import jax
import jax.numpy as jnp
from jax import lax
from jax.experimental import pallas as pl
from jax.experimental.pallas import tpu as pltpu
from jax.sharding import PartitionSpec as P

norm_eps = 1e-05
BLOCK = 512
GATE = 0.7978845608028654
CUBE = 0.044715
SAFE = 3600.0
LAYER_BLOCK, SLOPE_TYPE = 256, jnp.float32
VM_ATT, VM_LAYER, VM_BACK, VM_PROJ, VM_STREAM, VM_UNPACK = 56, 56, 56, 56, 56, 56
HD = 64
LEN = 1024
TILE = 128
TILES = LEN // TILE
PAIR = 2 * HD
FAR = -1e30
MARKS = 16
LSE_ROW = 8
LIVE_LANE = 12
MIB = 2**20


def dot(left, right):
    return jnp.dot(left, right, preferred_element_type=jnp.float32)


def three_parts(row):
    high = row.astype(jnp.bfloat16)
    rest = row - high.astype(jnp.float32)
    mid = rest.astype(jnp.bfloat16)
    low = (rest - mid.astype(jnp.float32)).astype(jnp.bfloat16)
    return high, mid, low


def label_marks(labels):
    row = lax.broadcasted_iota(jnp.int32, (TILE, labels.shape[1]), 0)
    same = labels == row
    ones = (row < LSE_ROW + 3) | ((row == LIVE_LANE) & (labels != 0))
    keys = jnp.where(row < LSE_ROW, jnp.where(same, 0.0, FAR), jnp.where(ones, 1.0, 0.0))
    queries = jnp.where(same & (row < LSE_ROW), 1.0, 0.0)[:MARKS]
    return keys.astype(jnp.bfloat16).T, queries.astype(jnp.bfloat16)


def key_range(labels, base, i):
    def head(j):
        return labels[(base + j) * TILE]

    def tail(j):
        return labels[(base + j) * TILE + TILE - 1]

    low, high = head(i), tail(i)
    first, last = i, i
    for j in reversed(range(TILES)):
        first = jnp.where((j < i) & (tail(j) == low), j, first)
    for j in range(TILES):
        last = jnp.where((j > i) & (head(j) == high), j, last)
    return first, last - first + 1


def halves_of(block):
    return jnp.concatenate([block[:HD, :TILE], block[HD:, TILE:]], axis=0)


def split_lanes(tile):
    lane = lax.broadcasted_iota(jnp.int32, tile.shape, 1)
    zero = jnp.zeros_like(tile)
    return jnp.concatenate(
        [jnp.where(lane < HD, tile, zero), jnp.where(lane < HD, zero, tile)], axis=0
    )


def each_width(count, branch):
    for width in range(1, TILES + 1):
        pl.when(count == width)(partial(branch, width))


def dot_nt(left, right):
    return lax.dot_general(
        left, right, (((1,), (1,)), ((), ())), preferred_element_type=jnp.float32
    )


def dot_tn(left, right):
    return lax.dot_general(
        left, right, (((0,), (0,)), ((), ())), preferred_element_type=jnp.float32
    )


def full(ref):
    shape = ref.shape
    return pl.BlockSpec(shape, lambda *_: (0,) * len(shape), pipeline_mode=pl.Buffered(1))


def call(kernel, name, grid, ins, outs, scratch=(), scalars=(), flops=0, aliases=None, vmem=56):
    specs, arrays = [], []
    for item in ins:
        if isinstance(item, tuple):
            arrays.append(item[0])
            if item[1] is None:
                specs.append(pl.BlockSpec(memory_space=pl.ANY))
            else:
                specs.append(pl.BlockSpec(item[1], item[2]))
        else:
            arrays.append(item)
            specs.append(full(item))
    size = sum(a.size * a.dtype.itemsize for a in arrays)
    size += sum(jnp.dtype(d).itemsize * math.prod(s) for s, d, _, _ in outs)
    return pl.pallas_call(
        kernel,
        grid_spec=pltpu.PrefetchScalarGridSpec(
            num_scalar_prefetch=len(scalars),
            grid=grid,
            in_specs=specs,
            out_specs=[
                pl.BlockSpec(b, m) if b else pl.BlockSpec(memory_space=pl.ANY)
                for _, _, b, m in outs
            ],
            scratch_shapes=scratch,
        ),
        out_shape=[jax.ShapeDtypeStruct(s, d) for s, d, _, _ in outs],
        compiler_params=pltpu.CompilerParams(vmem_limit_bytes=vmem * MIB),
        cost_estimate=pl.CostEstimate(flops=flops, bytes_accessed=size, transcendentals=0),
        input_output_aliases=aliases or {},
        name=name,
    )(*scalars, *arrays)


def rows_of(i, *_):
    return (i, 0)


def stats(z):
    mean = jnp.mean(z, axis=-1, keepdims=True)
    centred = z - mean
    spread = jnp.mean(centred * centred, axis=-1, keepdims=True)
    scale = lax.rsqrt(spread + norm_eps)
    return centred * scale, scale


def norm_back(upstream, unit, scale, gain):
    t = upstream * gain
    inner = jnp.mean(t * unit, axis=-1, keepdims=True)
    return (t - jnp.mean(t, axis=-1, keepdims=True) - unit * inner) * scale


def layer_kernel(
    heads, x, dual, gn, gd, marks, out_a, out_b, up_a, up_b, down_a, down_b, g1, b1, g2, b2,
    normed_out, dual_out, gfirst_ref, gheads, ffn_grad_a, ffn_grad_b,
    out_grad_a, out_grad_b, sums,
    hid, slope, acc_up, acc_down, acc_out,
):
    i = pl.program_id(0)
    half = out_a.shape[0]
    ff = up_a.shape[1]
    chunk = 1024

    @pl.when(i == 0)
    def _():
        sums[...] = jnp.zeros_like(sums)
        acc_up[...] = jnp.zeros_like(acc_up)
        acc_down[...] = jnp.zeros_like(acc_down)
        acc_out[...] = jnp.zeros_like(acc_out)

    attn = dot(heads[:, :half], out_a[...]) + dot(heads[:, half:], out_b[...])
    z1 = x[...].astype(jnp.float32) + attn
    unit, scale = stats(z1)
    normed = unit * g1[...] + b1[...]
    low = normed.astype(jnp.bfloat16)
    ffn = None
    for n, (up, down) in enumerate(((up_a, down_a), (up_b, down_b))):
        for c in range(ff // chunk):
            cols = slice(c * chunk, (c + 1) * chunk)
            at = slice(n * ff + c * chunk, n * ff + (c + 1) * chunk)
            v = dot(low, up[:, cols])
            square = v * v
            t = jnp.tanh(v * (GATE + (GATE * CUBE) * square))
            open_part = 0.5 + 0.5 * t
            hidden = (v * open_part).astype(jnp.bfloat16)
            hid[:, at] = hidden
            slope[:, at] = open_part + (v * (0.5 - 0.5 * t * t)) * (
                GATE + (3 * GATE * CUBE) * square
            )
            part = dot(hidden, down[cols, :])
            ffn = part if ffn is None else ffn + part
    unit2, scale2 = stats(normed + ffn)
    normed_out[...] = (unit2 * g2[...] + b2[...]).astype(jnp.bfloat16)
    dual_out[...] = (dual[...].astype(jnp.float32) + attn + ffn).astype(jnp.bfloat16)
    upstream = gn[...].astype(jnp.float32)
    gmid = norm_back(upstream, unit2, scale2, g2[...])
    gdual = gd[...].astype(jnp.float32)
    gffn = (gmid + gdual).astype(jnp.bfloat16)
    gffn_t = gffn.T
    low_t = low.T
    gnormed = gmid
    for n, (up, down) in enumerate(((up_a, down_a), (up_b, down_b))):
        for c in range(ff // chunk):
            cols = slice(c * chunk, (c + 1) * chunk)
            at = slice(n * ff + c * chunk, n * ff + (c + 1) * chunk)
            gpre = (dot_nt(gffn, down[cols, :]) * slope[:, at]).astype(jnp.bfloat16)
            acc_down[:, at] += dot(gffn_t, hid[:, at])
            acc_up[:, at] += dot(low_t, gpre)
            gnormed = gnormed + dot_nt(gpre, up[:, cols])
    gfirst = norm_back(gnormed, unit, scale, g1[...])
    gfirst_ref[...] = gfirst.astype(jnp.bfloat16)
    gattn = (gfirst + gdual).astype(jnp.bfloat16)
    sums[0:1, :] += jnp.sum(gnormed * unit, axis=0, keepdims=True)
    sums[1:2, :] += jnp.sum(gnormed, axis=0, keepdims=True)
    sums[2:3, :] += jnp.sum(upstream * unit2, axis=0, keepdims=True)
    sums[3:4, :] += jnp.sum(upstream, axis=0, keepdims=True)
    acc_out[...] += dot_tn(heads[...], gattn)
    live = marks[:, LIVE_LANE : LIVE_LANE + 1].astype(jnp.float32)
    gheads[:, :half] = (dot_nt(gattn, out_a[...]) * live).astype(jnp.bfloat16)
    gheads[:, half:] = (dot_nt(gattn, out_b[...]) * live).astype(jnp.bfloat16)

    @pl.when(i == pl.num_programs(0) - 1)
    def _():
        depth = acc_up.shape[0]
        for n, (ffn_grad, out_grad) in enumerate(
            ((ffn_grad_a, out_grad_a), (ffn_grad_b, out_grad_b))
        ):
            ffn_grad[:ff, :] = acc_down[:, n * ff : (n + 1) * ff].astype(jnp.bfloat16).T
            for c in range(ff // depth):
                at = n * ff + c * depth
                ffn_grad[ff + c * depth : ff + (c + 1) * depth, :] = acc_up[
                    :, at : at + depth
                ].astype(jnp.bfloat16)
            out_grad[...] = acc_out[n * half : (n + 1) * half, :].astype(jnp.bfloat16)


def layer(heads, x, dual, gn, gd, marks, outs, ups, downs, g1, b1, g2, b2, block=BLOCK):
    rows, depth = x.shape
    ff, half = ups[0].shape[1], outs[0].shape[0]
    tall = ((rows, depth), jnp.bfloat16, (block, depth), rows_of)

    def once(*shape, dtype=jnp.bfloat16):
        return (shape, dtype, shape, lambda i: (0, 0))

    return call(
        layer_kernel, "layer", (rows // block,),
        [(a, (block, a.shape[1]), rows_of) for a in (heads, x, dual, gn, gd, marks)]
        + [*outs, *ups, *downs, g1, b1, g2, b2],
        [tall, tall, tall, tall, once(2 * ff, depth), once(2 * ff, depth),
         once(half, depth), once(half, depth), once(8, depth, dtype=jnp.float32)],
        scratch=[
            pltpu.VMEM((block, 2 * ff), jnp.bfloat16),
            pltpu.VMEM((block, 2 * ff), jnp.float32),
            pltpu.VMEM((depth, 2 * ff), jnp.float32),
            pltpu.VMEM((depth, 2 * ff), jnp.float32),
            pltpu.VMEM((2 * half, depth), jnp.float32),
        ],
        flops=2 * rows * depth * (3 * depth + 12 * ff),
        vmem=VM_LAYER,
    )


def fill_block(table, p, i, tile_t):
    table[p, i, :HD, :TILE] = tile_t[:HD]
    table[p, i, HD:PAIR, TILE:] = tile_t[HD:]


def score_bound(qkv, width):
    row = lax.broadcasted_iota(jnp.int32, (width, TILE), 0)
    head = lax.broadcasted_iota(jnp.int32, (width, TILE), 1)
    heads = (row // HD == head).astype(jnp.bfloat16)
    largest = []
    for at in (0, width):
        block = qkv[:, at : at + width].astype(jnp.float32)
        norms = dot((block * block).astype(jnp.bfloat16), heads)
        largest.append(jnp.max(norms, axis=0, keepdims=True))
    return jnp.max(largest[0] * largest[1]) * (1.02 / HD)


def attend_kernel(
    edges, core, x_ref, qa, ka, va, qb, kb, vb, labels,
    qkv_hbm, out_ref, lse_ref, key_marks, query_marks, qkv_ref, kcat, vt, qt, mixed_t, left,
):
    seq = pl.program_id(0)
    base = (core[0] * pl.num_programs(0) + seq) * TILES
    key_marks[...], query_marks[...] = label_marks(labels[...])
    half = qa.shape[1]
    width = 2 * half
    pairs = width // PAIR
    x = x_ref[...]

    @pl.when(seq == 0)
    def _():
        qt[...] = jnp.zeros_like(qt)

    for n, w in enumerate((qa, qb, ka, kb, va, vb)):
        qkv_ref[:, n * half : (n + 1) * half] = dot(x, w[...]).astype(jnp.bfloat16)
    rows = pl.ds(pl.multiple_of(seq * LEN, LEN), LEN)
    leaving = pltpu.make_async_copy(qkv_ref, qkv_hbm.at[rows, :], left)
    leaving.start()
    small_scores = score_bound(qkv_ref, width) < SAFE
    for p in range(pairs):
        lanes = slice(p * PAIR, (p + 1) * PAIR)
        kcat[p, :, :PAIR] = qkv_ref[:, width + p * PAIR : width + (p + 1) * PAIR]
        kcat[p, :, PAIR:] = key_marks[...]
        vt[lanes, :] = qkv_ref[:, 2 * width + p * PAIR : 2 * width + (p + 1) * PAIR].T
        for i in range(TILES):
            cols = slice(i * TILE, (i + 1) * TILE)
            fill_block(qt, p, i, (qkv_ref[cols, lanes] * jnp.bfloat16(HD**-0.5)).T)
            qt[p, i, PAIR : PAIR + MARKS, :TILE] = query_marks[:, cols]
            qt[p, i, PAIR : PAIR + MARKS, TILE:] = query_marks[:, cols]

    def step(i, carry):
        at = pl.multiple_of(i * TILE, TILE)
        first, count = key_range(edges, base, i)
        first = jnp.where(small_scores, first, 0)
        start = pl.multiple_of(first * TILE, TILE)

        def branch(width, small=True):
            at_keys = pl.ds(start, width * TILE)

            def scores_of(p):
                return dot(kcat[p, at_keys, :], qt[p, i])

            def finish(p, scores):
                top = None
                if not small:
                    top = jnp.max(scores, axis=0, keepdims=True)
                    scores = scores - top
                probs = jnp.exp(scores)
                total = jnp.sum(probs, axis=0, keepdims=True)
                mixed = dot(vt[p * PAIR : (p + 1) * PAIR, at_keys], probs.astype(jnp.bfloat16))
                mixed_t[p * PAIR : (p + 1) * PAIR, pl.ds(at, TILE)] = halves_of(mixed / total)
                log_total = jnp.log(total)
                lse_ref[0, p, pl.ds(i, 1), :] = log_total if small else top + log_total

            ahead = scores_of(0)
            for p in range(pairs):
                scores = ahead
                if p + 1 < pairs:
                    ahead = scores_of(p + 1)
                finish(p, scores)

        each_width(jnp.where(small_scores, count, 0), branch)
        pl.when(jnp.logical_not(small_scores))(partial(branch, TILES, False))
        return carry

    lax.fori_loop(0, TILES, step, 0)
    live = 1.0 - query_marks[:1, :].astype(jnp.float32)
    for p in range(pairs):
        lanes = slice(p * PAIR, (p + 1) * PAIR)
        out_ref[:, lanes] = (mixed_t[lanes, :] * live).astype(jnp.bfloat16).T
    leaving.wait()


def attend(edges, core, x, own, other, segments):
    rows, depth = x.shape
    half = own[0].shape[1]
    width = 2 * half
    seqs, pairs = rows // LEN, width // PAIR
    return call(
        attend_kernel, "attend", (seqs,),
        [
            (x, (LEN, depth), lambda s, *_: (s, 0)),
            *own,
            *other,
            (segments.reshape(1, -1), (1, LEN), lambda s, _, core: (0, core[0] * seqs + s)),
        ],
        [
            ((rows, 3 * width), jnp.bfloat16, None, None),
            ((rows, width), jnp.bfloat16, (LEN, width), lambda s, *_: (s, 0)),
            (
                (seqs, pairs, TILES, 2 * TILE), jnp.float32, (1, pairs, TILES, 2 * TILE),
                lambda s, *_: (s, 0, 0, 0),
            ),
            ((rows, TILE), jnp.bfloat16, (LEN, TILE), lambda s, *_: (s, 0)),
            ((MARKS, rows), jnp.bfloat16, (MARKS, LEN), lambda s, *_: (0, s)),
        ],
        scratch=[
            pltpu.VMEM((LEN, 3 * width), jnp.bfloat16),
            pltpu.VMEM((pairs, LEN, PAIR + TILE), jnp.bfloat16),
            pltpu.VMEM((width, LEN), jnp.bfloat16),
            pltpu.VMEM((pairs, TILES, PAIR + TILE, 2 * TILE), jnp.bfloat16),
            pltpu.VMEM((width, LEN), jnp.float32),
            pltpu.SemaphoreType.DMA,
        ],
        scalars=(edges, core),
        flops=2 * rows * (3 * width * depth + 2 * width * LEN),
        vmem=VM_ATT,
    )


def attend_back_kernel(
    edges, core, seq, qkv_hbm, g_hbm, o_hbm, key_marks, query_marks, lse_ref, out_hbm,
    q_ref, k_ref, v_ref, g_ref, o_ref, out_ref, kcat, vcat, kt, qt, gt, dk, dv, dqt, arrived, left,
):
    base = (core[0] * (qkv_hbm.shape[0] // LEN) + seq[0]) * TILES
    width = q_ref.shape[1]
    pairs = width // PAIR
    groups = pairs // 2
    rows = pl.ds(pl.multiple_of(seq[0] * LEN, LEN), LEN)
    k_copy, v_copy, q_copy, g_copy, o_copy = (
        pltpu.make_async_copy(source, target, arrived.at[n])
        for n, (source, target) in enumerate(
            (
                (qkv_hbm.at[rows, pl.ds(width, width)], k_ref),
                (qkv_hbm.at[rows, pl.ds(2 * width, width)], v_ref),
                (qkv_hbm.at[rows, pl.ds(0, width)], q_ref),
                (g_hbm.at[rows, :], g_ref),
                (o_hbm.at[rows, :], o_ref),
            )
        )
    )
    for copy in (k_copy, v_copy, q_copy, g_copy, o_copy):
        copy.start()

    def place(p, what):
        at = (((p % groups) * 2 + p // groups) * 3 + what) * PAIR
        return slice(at, at + PAIR)

    def negated(row):
        return [part.astype(jnp.float32) for part in three_parts(-row)]

    qt[...] = jnp.zeros_like(qt)
    gt[...] = jnp.zeros_like(gt)
    dk[...] = jnp.zeros_like(dk)
    dv[...] = jnp.zeros_like(dv)
    for p in range(pairs):
        kcat[p, :, PAIR:] = key_marks[...]
        vcat[p, :, PAIR:] = key_marks[...]
    k_copy.wait()
    for p in range(pairs):
        lanes = slice(p * PAIR, (p + 1) * PAIR)
        kcat[p, :, :PAIR] = k_ref[:, lanes]
        kt[lanes, :] = k_ref[:, lanes].T
    v_copy.wait()
    for p in range(pairs):
        vcat[p, :, :PAIR] = v_ref[:, p * PAIR : (p + 1) * PAIR]
    q_copy.wait()
    g_copy.wait()
    o_copy.wait()
    pad = jnp.zeros((MARKS - LSE_ROW - 3, 2 * TILE), jnp.float32)
    none = jnp.zeros((LSE_ROW, 2 * TILE), jnp.float32)
    for p in range(pairs):
        lanes = slice(p * PAIR, (p + 1) * PAIR)
        for i in range(TILES):
            cols = slice(i * TILE, (i + 1) * TILE)
            fill_block(qt, p, i, (q_ref[cols, lanes] * jnp.bfloat16(HD**-0.5)).T)
            grad_t = g_ref[cols, lanes].T
            fill_block(gt, p, i, grad_t)
            agree = grad_t.astype(jnp.float32) * o_ref[cols, lanes].T.astype(jnp.float32)
            delta = jnp.concatenate(
                [
                    jnp.sum(agree[:HD], axis=0, keepdims=True),
                    jnp.sum(agree[HD:], axis=0, keepdims=True),
                ],
                axis=1,
            )
            marks = query_marks[:LSE_ROW, cols].astype(jnp.float32)
            marks = jnp.concatenate([marks, marks], axis=1)
            lse = lse_ref[0, p, i : i + 1, :]
            qt[p, i, PAIR : PAIR + MARKS, :] = jnp.concatenate(
                [marks, *negated(lse), pad], axis=0
            ).astype(jnp.bfloat16)
            gt[p, i, PAIR : PAIR + MARKS, :] = jnp.concatenate(
                [none, *negated(delta), pad], axis=0
            ).astype(jnp.bfloat16)

    def step(i, carry):
        at = pl.multiple_of(i * TILE, TILE)
        first, count = key_range(edges, base, i)
        start = pl.multiple_of(first * TILE, TILE)

        def branch(width):
            at_keys = pl.ds(start, width * TILE)

            def head(p):
                scores = dot(kcat[p, at_keys, :], qt[p, i])
                grad_probs = dot(vcat[p, at_keys, :], gt[p, i])
                return scores, grad_probs

            def finish(p, scores, grad_probs):
                lanes = slice(p * PAIR, (p + 1) * PAIR)
                query = q_ref[pl.ds(at, TILE), lanes] * jnp.bfloat16(HD**-0.5)
                grad = g_ref[pl.ds(at, TILE), lanes]
                probs = jnp.exp(scores)
                grad_scores = (probs * grad_probs).astype(jnp.bfloat16)
                dv[p, at_keys, :] += dot(probs.astype(jnp.bfloat16), split_lanes(grad))
                dk[p, at_keys, :] += dot(grad_scores, split_lanes(query))
                dqt[lanes, pl.ds(at, TILE)] = halves_of(dot(kt[lanes, at_keys], grad_scores))

            ahead = head(0)
            for p in range(pairs):
                now = ahead
                if p + 1 < pairs:
                    ahead = head(p + 1)
                finish(p, *now)

        each_width(count, branch)
        return carry

    lax.fori_loop(0, TILES, step, 0)
    copies = []
    for g in range(groups):
        for p in (g, g + groups):
            lanes = slice(p * PAIR, (p + 1) * PAIR)
            out_ref[:, place(p, 0)] = (dqt[lanes, :] * HD**-0.5).astype(jnp.bfloat16).T
            out_ref[:, place(p, 1)] = dk[p].astype(jnp.bfloat16)
            out_ref[:, place(p, 2)] = dv[p].astype(jnp.bfloat16)
            cols = pl.ds(place(p, 0).start, 3 * PAIR)
            copies.append(
                pltpu.make_async_copy(out_ref.at[:, cols], out_hbm.at[:, cols], left.at[p])
            )
            copies[-1].start()
    for copy in copies:
        copy.wait()


def attend_back(qkv, gheads, heads, key_marks, query_marks, lse, core, seq, edges):
    rows, width = heads.shape
    seqs, pairs = rows // LEN, width // PAIR
    by_seq = lambda i, edges, core, seq: (seq[0], 0)
    block = pltpu.VMEM((LEN, width), jnp.bfloat16)
    return call(
        attend_back_kernel, "attend_back", (1,),
        [
            (qkv, None, None),
            (gheads, None, None),
            (heads, None, None),
            (key_marks, (LEN, TILE), by_seq),
            (query_marks, (MARKS, LEN), lambda i, edges, core, seq: (0, seq[0])),
            (lse, (1, pairs, TILES, 2 * TILE), lambda i, edges, core, seq: (seq[0], 0, 0, 0)),
        ],
        [((LEN, 3 * width), jnp.bfloat16, None, None)],
        scratch=[
            *[block] * 5,
            pltpu.VMEM((LEN, 3 * width), jnp.bfloat16),
            pltpu.VMEM((pairs, LEN, PAIR + TILE), jnp.bfloat16),
            pltpu.VMEM((pairs, LEN, PAIR + TILE), jnp.bfloat16),
            pltpu.VMEM((width, LEN), jnp.bfloat16),
            pltpu.VMEM((pairs, TILES, PAIR + TILE, 2 * TILE), jnp.bfloat16),
            pltpu.VMEM((pairs, TILES, PAIR + TILE, 2 * TILE), jnp.bfloat16),
            pltpu.VMEM((pairs, LEN, PAIR), jnp.float32),
            pltpu.VMEM((pairs, LEN, PAIR), jnp.float32),
            pltpu.VMEM((width, LEN), jnp.float32),
            pltpu.SemaphoreType.DMA((5,)),
            pltpu.SemaphoreType.DMA((pairs,)),
        ],
        scalars=(edges, core, jnp.full((1,), seq, jnp.int32)),
        flops=10 * LEN * width * LEN,
        vmem=VM_BACK,
    )[0]


def project_back_kernel(seqs, x_hbm, *refs):
    grads = refs[:seqs]
    out_a, out_b, sums, own_ref, other_ref, x_ref, x_t, g_ref, arrived = refs[seqs:]
    size = 6 * PAIR
    chunks = g_ref.shape[1] // size
    x_copies, g_copies = [], []
    for s in range(seqs):
        rows = slice(s * LEN, (s + 1) * LEN)
        x_copies.append(
            pltpu.make_async_copy(x_hbm.at[rows, :], x_ref.at[rows, :], arrived.at[s])
        )
    for c in range(chunks):
        cols = pl.ds(c * size, size)
        g_copies.append(
            [
                pltpu.make_async_copy(
                    grads[s].at[:, cols],
                    g_ref.at[s * LEN : (s + 1) * LEN, cols],
                    arrived.at[seqs * (c + 1) + s],
                )
                for s in range(seqs)
            ]
        )
    for copy in (*x_copies, *(copy for pair in g_copies for copy in pair)):
        copy.start()
    start = size // 2 * chunks
    end = start + out_a.shape[0]
    both = jnp.concatenate([sums[...], jnp.zeros_like(sums)], axis=0)
    for buf, out_grad in ((own_ref, out_a), (other_ref, out_b)):
        buf[start:end, :] = out_grad[...]
        buf[end : end + MARKS, :] = both.astype(jnp.bfloat16)
        if end + MARKS < buf.shape[0]:
            rest = (buf.shape[0] - end - MARKS, buf.shape[1])
            buf[end + MARKS :, :] = jnp.zeros(rest, jnp.bfloat16)
    for s, copy in enumerate(x_copies):
        copy.wait()
        rows = slice(s * LEN, (s + 1) * LEN)
        x_t[:, rows] = x_ref[rows, :].T
    for c, pair in enumerate(g_copies):
        for copy in pair:
            copy.wait()
        for r in range(x_t.shape[0] // PAIR):
            at = slice(r * PAIR, (r + 1) * PAIR)
            part = dot(x_t[at, :], g_ref[:, c * size : (c + 1) * size]).astype(jnp.bfloat16)
            for m in range(6):
                rows = slice((c * 3 + m % 3) * PAIR, (c * 3 + m % 3 + 1) * PAIR)
                (own_ref, other_ref)[m // 3][rows, at] = part[:, m * PAIR : (m + 1) * PAIR]


def project_back(x, grads, extra, height):
    rows, depth = x.shape
    wide = grads[0].shape[1]
    seqs = len(grads)
    buf = ((height, depth), jnp.bfloat16, (height, depth), lambda i: (0, 0))
    return call(
        partial(project_back_kernel, seqs), "project_back", (1,),
        [(x, None, None), *((grad, None, None) for grad in grads), *extra],
        [buf, buf],
        scratch=[
            pltpu.VMEM((rows, depth), jnp.bfloat16),
            pltpu.VMEM((depth, rows), jnp.bfloat16),
            pltpu.VMEM((rows, wide), jnp.bfloat16),
            pltpu.SemaphoreType.DMA((seqs * (wide // (6 * PAIR) + 1),)),
        ],
        flops=2 * rows * depth * wide,
        vmem=VM_PROJ,
    )


def stream_kernel(gfirst, grad, *refs):
    weights, out, table = refs[:6], refs[-2], refs[-1]

    @pl.when(pl.program_id(0) == 0)
    def _():
        count = len(weights)
        for n, weight in enumerate(weights):
            for g in range(weight.shape[1] // PAIR):
                at = (g * count + n) * PAIR
                table[:, at : at + PAIR] = weight[:, g * PAIR : (g + 1) * PAIR]

    out[...] = gfirst[...].astype(jnp.float32) + dot_nt(grad[...], table[...])


def stream(gfirst, grad, own, other, seq, before=None):
    rows, depth = gfirst.shape
    wide = grad.shape[1]
    per = LEN // BLOCK
    of_seq = lambda i: (seq * per + i, 0)
    ins = [(gfirst, (BLOCK, depth), of_seq), (grad, (BLOCK, wide), rows_of), *own, *other]
    aliases = {}
    if before is not None:
        aliases[len(ins)] = 0
        ins.append((before, None, None))
    return call(
        stream_kernel, "stream", (per,), ins,
        [((rows, depth), jnp.float32, (BLOCK, depth), of_seq)],
        scratch=[pltpu.VMEM((depth, wide), jnp.bfloat16)],
        aliases=aliases,
        flops=2 * LEN * depth * wide,
        vmem=VM_STREAM,
    )[0]


def swap_cores(block):
    return lax.ppermute(block, "mp", [(0, 1), (1, 0)])


def stages_of(chips, radices):
    me, core = lax.axis_index("dp"), lax.axis_index("mp")

    def pairs(masks):
        return [(2 * c + i, 2 * (c ^ masks[i]) + i) for c in range(chips) for i in range(2)]

    stages = []
    bit = 0
    if radices[:2] == (2, 2):
        low, high = me & 1, (me >> 1) & 1
        stages = [
            (jnp.where(core == 0, low, high), 2, [pairs((1, 2))]),
            (jnp.where(core == 0, high, low), 2, [pairs((2, 1))]),
        ]
        bit = 2
        radices = radices[2:]
    while 1 << bit < chips:
        radix = min(radices[0], chips >> bit)
        radices = radices[1:] or radices
        ways = [pairs((j << bit, j << bit)) for j in range(1, radix)]
        stages.append(((me >> bit) & (radix - 1), radix, ways))
        bit += radix // 2
    return stages


def send(block, pairs):
    return lax.ppermute(block, ("dp", "mp"), pairs)


def part(block, which, rows):
    return lax.dynamic_slice_in_dim(block, which * rows, rows)


def added(blocks):
    total = blocks[0].astype(jnp.float32)
    for block in blocks[1:]:
        total = total + block.astype(jnp.float32)
    return total.astype(jnp.bfloat16)


def unpack_kernel(size, shapes, places, *refs):
    pieces, outs, table = refs[: -len(shapes) - 1], refs[-len(shapes) - 1 : -1], refs[-1]
    at = 0
    for piece in pieces:
        block = piece[...].astype(jnp.float32)
        for n in range(block.shape[0] // size):
            table[pl.ds(pl.multiple_of(places[at] * size, size), size), :] = block[
                n * size : (n + 1) * size
            ]
            at += 1
    row = 0
    depth = table.shape[1]
    for out, (kind, height, width) in zip(outs, shapes):
        if kind == "rows":
            out[...] = table[row : row + height, :]
            row += height
        elif kind == "wide":
            for n in range(width // depth):
                out[:, n * depth : (n + 1) * depth] = table[row : row + height, :]
                row += height
        else:
            base, count = kind
            for g in range(width // PAIR):
                at = (g * count + base) * PAIR
                for n in range(height // PAIR):
                    out[n * PAIR : (n + 1) * PAIR, g * PAIR : (g + 1) * PAIR] = table[
                        at : at + PAIR, n * PAIR : (n + 1) * PAIR
                    ]
                row += PAIR


def unpack(pieces, places, shapes, rows, chips):
    depth = pieces[0].shape[1]
    size = rows // chips
    return call(
        partial(unpack_kernel, size, shapes), "unpack", (1,), pieces,
        [((h, w), jnp.float32, (h, w), lambda i, _: (0, 0)) for _, h, w in shapes],
        scratch=[pltpu.VMEM((rows, depth), jnp.float32)],
        scalars=(places,),
        vmem=VM_UNPACK,
    )


def sum_everywhere(own, other, shapes, chips, radices):
    rows = own.shape[0]
    stages = stages_of(chips, radices)
    cores = [(2 * c + i, 2 * c + 1 - i) for c in range(chips) for i in range(2)]
    addends = [own, *(yield [(other, cores)])]
    height = rows
    for digit, radix, ways in stages:
        height //= radix
        got = yield [
            (added([part(a, digit ^ (j + 1), height) for a in addends]), pairs)
            for j, pairs in enumerate(ways)
        ]
        addends = [part(a, digit, height) for a in addends] + got
    pieces = [added(addends)]
    places = [jnp.int32(0)]
    for n, (digit, radix, ways) in enumerate(reversed(stages)):
        weight = chips
        for _, earlier, _ in stages[: len(stages) - n]:
            weight //= earlier
        held = pieces[0] if len(pieces) == 1 else jnp.concatenate(pieces)
        pieces = [held] + (yield [(held, pairs) for pairs in ways])
        places = [p + (digit ^ j) * weight for j in range(radix) for p in places]
    return unpack(pieces, jnp.stack(places).astype(jnp.int32), shapes, rows, chips)


class Chain:
    def __init__(self, steps):
        self.steps, self.result = steps, None
        self.wishes = next(steps)

    def take(self, got):
        try:
            self.wishes = self.steps.send(got)
        except StopIteration as end:
            self.wishes, self.result = [], end.value


def advance(chains, work=None, token=None, beside=()):
    blocks = [block for chain in chains for block, _ in chain.wishes]
    if work is not None:
        *blocks, token = lax.optimization_barrier((*blocks, token))
    else:
        blocks = lax.optimization_barrier(blocks)
    ways = [pairs for chain in chains for _, pairs in chain.wishes]
    got = [send(block, pairs) for block, pairs in zip(blocks, ways)]
    out = None
    if work is not None:
        out = work(token)
        count = len(got)
        *got, last = lax.optimization_barrier((*got, out[-1], *beside))[: count + 1]
        out = (*out[:-1], last)
    for chain in chains:
        if chain.wishes:
            count = len(chain.wishes)
            chain.take(got[:count])
            got = got[count:]
    return out


def on_device(
    normed_in,
    dual_in,
    query_weight,
    key_weight,
    value_weight,
    output_weight,
    first_gain,
    first_bias,
    up_weight,
    down_weight,
    second_gain,
    second_bias,
    segments,
    grad_normed_out,
    grad_dual_out,
    chips,
):
    rows, depth = normed_in.shape
    core = lax.axis_index("mp")
    half, ff = query_weight.shape[1], up_weight.shape[1]
    own = (query_weight, key_weight, value_weight)
    other = tuple(swap_cores(w) for w in own)
    *_, late_out, late_up, late_down = lax.optimization_barrier(
        (*other, output_weight, up_weight, down_weight)
    )
    outs = (output_weight, swap_cores(late_out))
    ups = (up_weight, swap_cores(late_up))
    downs = (down_weight, swap_cores(late_down))
    edges = segments
    core = core.astype(jnp.int32).reshape(1)
    qkv, heads_out, log_totals, key_marks, query_marks = attend(
        edges, core, normed_in, own, other, segments
    )
    grain = 8 * chips

    def padded(count):
        return -(-count // grain) * grain

    row = lambda v: v.reshape(1, depth)
    normed_out, dual_out, grad_first, grad_heads, ffn_own, ffn_other, *extra = layer(
        heads_out, normed_in, dual_in, grad_normed_out, grad_dual_out, key_marks, outs, ups, downs,
        row(first_gain), row(first_bias), row(second_gain), row(second_bias),
    )
    back = partial(
        attend_back, qkv, grad_heads, heads_out, key_marks, query_marks, log_totals, core
    )
    fed = Chain(
        sum_everywhere(
            ffn_own, ffn_other,
            [("rows", ff, depth), ("wide", depth, ff)], chips, (2, 2, 4)
        )
    )
    grad_qkv = []
    for seq in range(rows // LEN):
        grad_qkv += advance([fed], lambda token: (back(seq, token),), edges)
    height = padded(3 * half + half + MARKS)
    own_grads, other_grads = advance(
        [fed], lambda x: project_back(x, grad_qkv, extra, height), normed_in
    )
    rest = Chain(
        sum_everywhere(
            own_grads, other_grads,
            [((n, 3), depth, half) for n in range(3)]
            + [("rows", half, depth)] + [("rows", 1, depth)] * 4,
            chips, (4,),
        )
    )
    advance([fed, rest])
    chains, grad_stream = [fed, rest], None
    for seq, grad in enumerate(grad_qkv):
        last = seq == len(grad_qkv) - 1
        while last and fed.wishes:
            advance(chains)
        (grad_stream,) = advance(
            chains,
            lambda token: (stream(token, grad, own, other, seq, grad_stream),),
            grad_first,
            fed.result[:1] if last else (),
        )
    down_total, up_total = fed.result
    query_total, key_total, value_total, output_total, *small = rest.result
    small = [total.reshape(depth) for total in small]
    return (
        normed_out,
        dual_out,
        grad_stream,
        query_total,
        key_total,
        value_total,
        output_total,
        small[0],
        small[1],
        up_total,
        down_total,
        small[2],
        small[3],
    )


def solution(mesh):
    rows = P(("dp", "mp"), None)
    columns = P(None, "mp")
    return jax.shard_map(
        partial(on_device, chips=mesh.shape["dp"]),
        mesh=mesh,
        in_specs=(
            rows, rows, columns, columns, columns, P("mp", None), P(), P(),
            columns, P("mp", None), P(), P(), P("dp"), rows, rows,
        ),
        out_specs=(
            rows, rows, rows, columns, columns, columns, P("mp", None), P(), P(),
            columns, P("mp", None), P(), P(),
        ),
        check_vma=False,
    )
```
